32 devices in a mesh: wide: 4 (over y, x), narrow: 8 (over z, core).
Axes of the slice: x: 2, y: 2, z: 4, core: 2. Of those that a mesh axis runs over, the one named last changes fastest.
Arguments:
- right_side: float32 [128, 320, 128], P(('wide', 'narrow')), may hold values from -6 to 6
- fine_blocks: float32 [128, 320, 320], P(('wide', 'narrow'))
- fine_inverses: float32 [128, 320, 320], P(('wide', 'narrow')), as said below
- fine_lifts: float32 [6, 320, 80], replicated, may hold values from -0.625 to 0.625
- fine_coefs: float32 [128, 6, 80], P(('wide', 'narrow')), may hold values from 0.1 to 0.4
- coarse_blocks: float32 [128, 40, 40], P(('wide', 'narrow'))
- coarse_inverses: float32 [128, 40, 40], P(('wide', 'narrow')), as said below
- coarse_lifts: float32 [6, 40, 20], replicated, may hold values from -1.25 to 1.25
- coarse_coefs: float32 [128, 6, 20], P(('wide', 'narrow')), may hold values from 0.15 to 0.6
- neighbours: int32 [128, 6], P(('wide', 'narrow')), may hold values from -1 to 127, as said below
- counts: int32 [32], P(('wide', 'narrow')), may hold values from 2 to 4, as said below
Outputs:
- solution: float32 [128, 320, 128], P(('wide', 'narrow'))
The draws below stay inside these ranges and needn't reach their ends.
Inputs may be any that keep to these rules, and one draw needn't show every extreme that they name: Slots 0 to counts - 1 of a device are its live elements, the rest are empty. Some device has all 4 slots live and some has only 2. Each entry is -1 or the index of a live element; empty slots hold -1 on all faces. If neighbours[e, f] = g then neighbours[g, f xor 1] = e. Across faces 0 and 1 the neighbour lies on the same device or on the device one wide index lower (face 0) or higher (face 1) with the same narrow index; across faces 2 and 3 likewise along narrow; across faces 4 and 5 on the same device. For every pair of devices next to each other along either axis exactly 1 face crosses between them. `fine_inverses`: an approximate inverse of the element's fine block, as incomplete factors give it. `coarse_inverses`: an approximate inverse of the element's coarse block, as incomplete factors give it.
All inputs are finite; a program needn't handle non-finite values.
Results may differ from the reference program's by a relative error of at most 0.00022.
Values sent between devices are 32-bit elements; how exact they have to be, the bound alone decides.
No kernel may reach another device: no remote copies, remote signals or barrier semaphores. Data moves between devices by JAX's collectives and lax.ppermute only.
A program may use at most 64 MiB of HBM per device.

```python
import math
import jax
import jax.numpy as jnp
import numpy as np
from jax import lax

NVAR = 5
NODE1 = 4
NF = 320
NFACE = 80
NC = 40
NCF = 20
E_DEV = 4
RHS = 128
PRE_SWEEPS = 2
POST_SWEEPS = 2
COARSE_SWEEPS = 4
NE = 128
N_WIDE = 4
N_NARROW = 8


def block_pair(base_key, elements, order):
    diag_key = jax.random.fold_in(base_key, 301)
    coupling_key = jax.random.fold_in(base_key, 302)
    noise_key = jax.random.fold_in(base_key, 303)
    diagonal = jnp.exp(jax.random.uniform(diag_key, (elements, order), jnp.float32, 0.0, 0.6931))
    coupling = jax.random.normal(coupling_key, (elements, order, order), jnp.float32) * (0.3 / np.sqrt(order))
    identity = jnp.eye(order, dtype=jnp.float32)
    blocks = diagonal[:, :, None] * identity + coupling
    reciprocal = 1.0 / diagonal
    approximate = reciprocal[:, :, None] * identity - reciprocal[:, :, None] * coupling * reciprocal[:, None, :]
    noise = jax.random.normal(noise_key, (elements, order, order), jnp.float32) * (0.02 / np.sqrt(order))
    return (blocks, approximate + noise)


def bounded_perm(base_key, length):
    shuffled = jax.random.permutation(base_key, E_DEV)
    places = jnp.arange(E_DEV)
    ordering = jnp.argsort(jnp.where(shuffled < length, places, E_DEV + places))
    result = shuffled[ordering]
    return (result, jnp.argsort(result))


def axis_faces(device_ids, places, counts, forward, backward, local_perm, local_inv, step_size, position, extent, devices):
    crossing = E_DEV // 4
    rows_back = backward[jnp.clip(device_ids[:, 0] - step_size, 0, devices - 1)]
    plus_cross = places < crossing
    plus_cross_slot = crossing + jnp.take_along_axis(forward, jnp.clip(places + 0 * device_ids, 0, crossing - 1), axis=1)
    plus_local_k = jnp.take_along_axis(local_perm, jnp.clip(places - crossing + 0 * device_ids, 0, E_DEV - 1), axis=1)
    plus_local_slot = jnp.where(plus_local_k < crossing, plus_local_k, plus_local_k + crossing)
    plus_dev = jnp.where(plus_cross, device_ids + step_size, device_ids)
    plus_slot = jnp.where(plus_cross, plus_cross_slot, plus_local_slot)
    plus_ok = jnp.where(plus_cross, position < extent - 1, places < counts[:, None])
    minus_cross = jnp.logical_and(places >= crossing, places < 2 * crossing)
    minus_cross_slot = jnp.take_along_axis(rows_back, jnp.clip(places - crossing + 0 * device_ids, 0, crossing - 1), axis=1)
    minus_local_k = jnp.where(places < crossing, places, places - crossing) + 0 * device_ids
    minus_local_slot = crossing + jnp.take_along_axis(local_inv, jnp.clip(minus_local_k, 0, E_DEV - 1), axis=1)
    minus_dev = jnp.where(minus_cross, device_ids - step_size, device_ids)
    minus_slot = jnp.where(minus_cross, minus_cross_slot, minus_local_slot)
    minus_ok = jnp.where(minus_cross, position > 0, places < counts[:, None])
    return ((minus_dev, minus_slot, minus_ok), (plus_dev, plus_slot, plus_ok))


def mesh_links(base_key):
    devices = N_WIDE * N_NARROW
    crossing = E_DEV // 4
    lowest = E_DEV // 2
    key_list = jax.random.split(jax.random.fold_in(base_key, 7), 9)
    counts = jax.random.randint(key_list[0], (devices,), lowest, E_DEV + 1)
    full_at = devices - 1
    least_at = (full_at + 1 + jax.random.randint(key_list[2], (), 0, devices - 1)) % devices
    counts = counts.at[least_at].set(lowest).at[full_at].set(E_DEV)

    def cross_perm(one_key):
        return jax.random.permutation(one_key, crossing)
    perm_wide = jax.vmap(cross_perm)(jax.random.split(key_list[3], devices))
    perm_narrow = jax.vmap(cross_perm)(jax.random.split(key_list[4], devices))
    inv_wide = jnp.argsort(perm_wide, axis=1)
    inv_narrow = jnp.argsort(perm_narrow, axis=1)
    free_length = counts - crossing
    local_wide, local_wide_inv = jax.vmap(bounded_perm)(jax.random.split(key_list[5], devices), free_length)
    local_narrow, local_narrow_inv = jax.vmap(bounded_perm)(jax.random.split(key_list[6], devices), free_length)
    local_depth, local_depth_inv = jax.vmap(bounded_perm)(jax.random.split(key_list[7], devices), counts)
    labels, labels_inv = jax.vmap(bounded_perm)(jax.random.split(key_list[8], devices), counts)
    device_ids = jnp.arange(devices)[:, None]
    places = jnp.arange(E_DEV)[None, :]
    wide_position = device_ids // N_NARROW
    narrow_position = device_ids % N_NARROW
    faces_wide = axis_faces(device_ids, places, counts, perm_wide, inv_wide, local_wide, local_wide_inv, N_NARROW, wide_position, N_WIDE, devices)
    faces_narrow = axis_faces(device_ids, places, counts, perm_narrow, inv_narrow, local_narrow, local_narrow_inv, 1, narrow_position, N_NARROW, devices)
    alive = places < counts[:, None]
    same_device = device_ids + 0 * places
    depth_minus = (same_device, local_depth_inv, alive)
    depth_plus = (same_device, local_depth, alive)
    pattern = [faces_wide[0], faces_wide[1], faces_narrow[0], faces_narrow[1], depth_minus, depth_plus]
    columns = []
    for face_side in range(6):
        face_dev, face_slot, face_ok = pattern[face_side]
        clip_dev = jnp.clip(face_dev, 0, devices - 1)
        clip_slot = jnp.clip(face_slot, 0, E_DEV - 1)
        global_ids = clip_dev * E_DEV + labels[clip_dev, clip_slot]
        global_ids = jnp.where(jnp.logical_and(face_ok, alive), global_ids, -1)
        moved = jnp.take_along_axis(global_ids, labels_inv, axis=1)
        moved = jnp.where(alive, moved, -1)
        columns.append(moved)
    table_all = jnp.stack(columns, axis=2).reshape(devices * E_DEV, 6).astype(jnp.int32)
    return (counts.astype(jnp.int32), table_all)


def draw_fine_blocks(key, part):
    return block_pair(jax.random.fold_in(key, 11), NE, NF)[0]


def draw_fine_inverses(key, part):
    return block_pair(jax.random.fold_in(key, 11), NE, NF)[1]


def draw_coarse_blocks(key, part):
    return block_pair(jax.random.fold_in(key, 12), NE, NC)[0]


def draw_coarse_inverses(key, part):
    return block_pair(jax.random.fold_in(key, 12), NE, NC)[1]


def draw_neighbours(key, part):
    return mesh_links(key)[1]


def draw_counts(key, part):
    return mesh_links(key)[0]


def block_levels(key, dims, cuts, low, largest):
    def one(dim, blocks):
        steps = jax.random.uniform(jax.random.fold_in(jax.random.fold_in(key, 6), dim), (blocks,), jnp.float32, low / len(cuts), largest / len(cuts))
        return jnp.repeat(jnp.exp(steps), dims[dim] // blocks).reshape((-1,) + (1,) * (len(dims) - dim - 1))

    loudness = one(*cuts[0])
    for cut in cuts[1:]:
        loudness = loudness * one(*cut)
    return loudness


def normal_values(key, shape, width, limit, shards=(), kind=jnp.bfloat16):
    gain = block_levels(key, shape, shards, -0.22, 0.18) if shards else 1.0
    entries = jax.random.normal(key, shape, jnp.float32) * width * gain
    return jnp.minimum(jnp.maximum(entries, -limit), limit).astype(kind)


def setup_inputs(seed: int = 0) -> dict:
    key_of = jax.random.split(jax.random.key(seed), 12)
    right_side = normal_values(key_of[0], (NE, NF, RHS), 1.0, 6.0, ((0, 32),), jnp.float32)
    fine_blocks = draw_fine_blocks(jax.random.fold_in(key_of[11], 71), 0)
    fine_inverses = draw_fine_inverses(jax.random.fold_in(key_of[11], 71), 0)
    fine_lifts = normal_values(key_of[3], (6, NF, NFACE), NFACE ** -0.5, 0.625, (), jnp.float32)
    fine_coefs = jnp.clip(jnp.exp(math.log(0.4) - 1.3862944 * jax.random.uniform(key_of[4], (NE, 6, NFACE), jnp.float32) ** block_levels(key_of[4], (NE, 6, NFACE), ((0, 32),), -0.2, 0.2)), 0.1, 0.4)
    coarse_blocks = draw_coarse_blocks(jax.random.fold_in(key_of[11], 71), 0)
    coarse_inverses = draw_coarse_inverses(jax.random.fold_in(key_of[11], 71), 0)
    coarse_lifts = normal_values(key_of[7], (6, NC, NCF), NCF ** -0.5, 1.25, (), jnp.float32)
    coarse_coefs = jnp.clip(jnp.exp(math.log(0.6) - 1.3862944 * jax.random.uniform(key_of[8], (NE, 6, NCF), jnp.float32) ** block_levels(key_of[8], (NE, 6, NCF), ((0, 32),), -0.2, 0.2)), 0.15, 0.6)
    neighbours = draw_neighbours(jax.random.fold_in(key_of[11], 71), 0)
    counts = draw_counts(jax.random.fold_in(key_of[11], 71), 0)
    return {"right_side": right_side, "fine_blocks": fine_blocks, "fine_inverses": fine_inverses, "fine_lifts": fine_lifts, "fine_coefs": fine_coefs, "coarse_blocks": coarse_blocks, "coarse_inverses": coarse_inverses, "coarse_lifts": coarse_lifts, "coarse_coefs": coarse_coefs, "neighbours": neighbours, "counts": counts}


damping = 0.8
highest = lax.Precision.HIGHEST

def face_rows(node_count, variables):
    cube_size = node_count * node_count * node_count
    lattice = np.arange(cube_size).reshape(node_count, node_count, node_count)
    table_list = []
    for face_side in range(6):
        layer_index = 0 if face_side % 2 == 0 else node_count - 1
        direction = face_side // 2
        if direction == 0:
            layer = lattice[layer_index, :, :]
        elif direction == 1:
            layer = lattice[:, layer_index, :]
        else:
            layer = lattice[:, :, layer_index]
        nodes_on = layer.reshape(-1)
        table_list.append(np.concatenate([nodes_on + variable * cube_size for variable in range(variables)]))
    return np.stack(table_list).astype(np.int32)

def prolong_table(node_count, variables):
    if node_count == 4:
        points = np.array([-1.0, -1.0 / np.sqrt(5.0), 1.0 / np.sqrt(5.0), 1.0])
    else:
        points = np.linspace(-1.0, 1.0, node_count)
    linear = np.stack([(1.0 - points) / 2.0, (1.0 + points) / 2.0], axis=1)
    tensor_hat = linear[:, None, None, :, None, None] * linear[None, :, None, None, :, None] * linear[None, None, :, None, None, :]
    tensor_hat = tensor_hat.reshape(node_count * node_count * node_count, 8)
    return np.kron(np.eye(variables), tensor_hat).astype(np.float32)

def block_apply(blocks, vectors):
    return jnp.einsum('epq,eqr->epr', blocks, vectors, precision=highest)

def couple(state_field, neighbours, face_coefs, face_lifts, face_table):
    present = neighbours >= 0
    clipped = jnp.where(present, neighbours, 0)
    summed = jnp.zeros(state_field.shape, state_field.dtype)
    for face_side in range(6):
        traces = state_field[:, face_table[face_side ^ 1], :]
        nearby = jnp.where(present[:, face_side, None, None], traces[clipped[:, face_side]], 0.0)
        scaled = face_coefs[:, face_side, :, None] * nearby
        summed = summed + jnp.einsum('pq,eqr->epr', face_lifts[face_side], scaled, precision=highest)
    return summed

def sweep(solution, rhs_live, blocks, inverses, couple_fn):
    residual = rhs_live - block_apply(blocks, solution) - couple_fn(solution)
    return solution + damping * block_apply(inverses, residual)

def reference(right_side, fine_blocks, fine_inverses, fine_lifts, fine_coefs, coarse_blocks, coarse_inverses, coarse_lifts, coarse_coefs, neighbours, counts):
    elements = right_side.shape[0]
    places = jnp.arange(elements)
    live_mask = (places % E_DEV < counts[places // E_DEV]).astype(right_side.dtype)
    rhs_live = right_side * live_mask[:, None, None]
    fine_table = face_rows(NODE1, NVAR)
    coarse_table = face_rows(2, NVAR)
    prolong = jnp.asarray(prolong_table(NODE1, NVAR), right_side.dtype)

    def fine_couple(state_field):
        return couple(state_field, neighbours, fine_coefs, fine_lifts, fine_table)

    def coarse_couple(state_field):
        return couple(state_field, neighbours, coarse_coefs, coarse_lifts, coarse_table)
    solution = jnp.zeros(right_side.shape, right_side.dtype)
    for sweep_index in range(PRE_SWEEPS):
        solution = sweep(solution, rhs_live, fine_blocks, fine_inverses, fine_couple)
    residual = rhs_live - block_apply(fine_blocks, solution) - fine_couple(solution)
    coarse_rhs = 0.25 * jnp.einsum('pq,epr->eqr', prolong, residual, precision=highest)
    coarse_solution = jnp.zeros(coarse_rhs.shape, coarse_rhs.dtype)
    for sweep_index in range(COARSE_SWEEPS):
        coarse_solution = sweep(coarse_solution, coarse_rhs, coarse_blocks, coarse_inverses, coarse_couple)
    solution = solution + jnp.einsum('pq,eqr->epr', prolong, coarse_solution, precision=highest)
    for sweep_index in range(POST_SWEEPS):
        solution = sweep(solution, rhs_live, fine_blocks, fine_inverses, fine_couple)
    return solution
```

```python
import jax
import jax.numpy as jnp
import numpy as np
from jax import lax
from jax.sharding import PartitionSpec as P

NVAR = 5
NODE1 = 4
PRE_SWEEPS = 2
POST_SWEEPS = 2
COARSE_SWEEPS = 4
AXES = ("wide", "narrow")

damping = 0.8
highest = lax.Precision.HIGHEST


def prolong_table(node_count, variables):
    points = np.array([-1.0, -1.0 / np.sqrt(5.0), 1.0 / np.sqrt(5.0), 1.0])
    linear = np.stack([(1.0 - points) / 2.0, (1.0 + points) / 2.0], axis=1)
    tensor_hat = (
        linear[:, None, None, :, None, None]
        * linear[None, :, None, None, :, None]
        * linear[None, None, :, None, None, :]
    )
    tensor_hat = tensor_hat.reshape(node_count * node_count * node_count, 8)
    face_hat = (linear[:, None, :, None] * linear[None, :, None, :]).reshape(node_count * node_count, 4)
    eye = np.eye(variables)
    return np.kron(eye, tensor_hat).astype(np.float32), np.kron(eye, face_hat).astype(np.float32)


def block_apply(blocks, vectors):
    return jnp.einsum("epq,eqr->epr", blocks, vectors, precision=highest)


def face_traces(state_field, node_count):
    slot_count = state_field.shape[0]
    columns = state_field.shape[2]
    shaped = state_field.reshape(slot_count, NVAR, node_count, node_count, node_count, columns)
    last = node_count - 1
    layers = [
        shaped[:, :, 0],
        shaped[:, :, last],
        shaped[:, :, :, 0],
        shaped[:, :, :, last],
        shaped[:, :, :, :, 0],
        shaped[:, :, :, :, last],
    ]
    flat = [layer.reshape(slot_count, NVAR * node_count * node_count, columns) for layer in layers]
    return jnp.stack(flat, axis=1)


def square_groups(wide_size, narrow_size, shift):
    groups = []
    for a in range(0, wide_size, 2):
        for c in range(0, narrow_size, 2):
            rows = ((a + shift) % wide_size, (a + shift + 1) % wide_size)
            cols = ((c + shift) % narrow_size, (c + shift + 1) % narrow_size)
            groups.append([w * narrow_size + n for w in rows for n in cols])
    return groups


def exchange(outgoing):
    wide_size, narrow_size = lax.axis_size("wide"), lax.axis_size("narrow")
    w, n = lax.axis_index("wide"), lax.axis_index("narrow")
    arrivals = [None] * 4
    parts = []
    for shift in range(2):
        wi, ni = (w + shift) % 2, (n + shift) % 2
        to_wide = jnp.where(wi == 0, outgoing[1], outgoing[0])
        to_narrow = jnp.where(ni == 0, outgoing[3], outgoing[2])
        chunks = jnp.stack([jnp.where(m // 2 != wi, to_wide, to_narrow) for m in range(4)])
        got = lax.all_to_all(
            chunks, AXES, 0, 0, axis_index_groups=square_groups(wide_size, narrow_size, shift), tiled=True
        )
        from_wide = lax.dynamic_index_in_dim(got, (1 - wi) * 2 + ni, 0, keepdims=False)
        from_narrow = lax.dynamic_index_in_dim(got, wi * 2 + 1 - ni, 0, keepdims=False)
        parts.append((wi, ni, from_wide, from_narrow))
    (wi, ni, aw, an), (_, _, bw, bn) = parts
    return jnp.stack(
        [
            jnp.where(wi == 0, bw, aw),
            jnp.where(wi == 0, aw, bw),
            jnp.where(ni == 0, bn, an),
            jnp.where(ni == 0, an, bn),
        ]
    )


def body(
    right_side,
    fine_blocks,
    fine_inverses,
    fine_lifts,
    fine_coefs,
    coarse_blocks,
    coarse_inverses,
    coarse_lifts,
    coarse_coefs,
    neighbours,
    counts,
):
    slots, _, columns = right_side.shape
    nc = coarse_blocks.shape[1]
    ncf = coarse_lifts.shape[2]
    narrow_size = lax.axis_size("narrow")
    devices = lax.axis_size("wide") * narrow_size
    share = columns // devices
    device_id = lax.axis_index("wide") * narrow_size + lax.axis_index("narrow")
    live_mask = (jnp.arange(slots) < counts[0]).astype(jnp.float32)
    rhs_live = right_side * live_mask[:, None, None]
    prolong_np, prolong_face_np = prolong_table(NODE1, NVAR)
    prolong, prolong_face = jnp.asarray(prolong_np), jnp.asarray(prolong_face_np)
    present = neighbours >= 0
    owner = neighbours // slots
    local = jnp.logical_and(
        jnp.logical_and(present, owner == device_id)[:, :, None],
        (neighbours % slots)[:, :, None] == jnp.arange(slots),
    ).astype(jnp.float32)
    crossing = jnp.logical_and(present, owner != device_id).astype(jnp.float32)[:, :4]

    def outgoing_of(traces):
        return jnp.einsum("ef,efqr->fqr", crossing, traces[:, :4], precision=highest)

    def couple(traces, arrived, lifts, coefs):
        nearby = []
        for f in range(6):
            got = jnp.einsum("eg,gqr->eqr", local[:, f], traces[:, f ^ 1], precision=highest)
            if f < 4:
                got = got + crossing[:, f, None, None] * arrived[f]
            nearby.append(got * coefs[:, f, :, None])
        return jnp.einsum("fpq,feqr->epr", lifts, jnp.stack(nearby), precision=highest)

    def residual_of(state, traces, arrived):
        return rhs_live - block_apply(fine_blocks, state) - couple(traces, arrived, fine_lifts, fine_coefs)

    def split_solve(coarse_rhs):
        flat = jnp.concatenate(
            [
                coarse_blocks.reshape(-1),
                coarse_inverses.reshape(-1),
                coarse_coefs.reshape(-1),
                local.reshape(-1),
                crossing.reshape(-1),
            ]
        )
        everyone = lax.all_gather(flat, AXES)
        lanes = jnp.repeat(everyone.T, share, axis=1)
        sizes = np.cumsum([coarse_blocks.size, coarse_inverses.size, coarse_coefs.size, local.size])
        cb, ci, cc, lo, cr = jnp.split(lanes, [int(s) for s in sizes], axis=0)
        wide_lanes = lanes.shape[1]
        cb = cb.reshape(slots, nc, nc, wide_lanes)
        ci = ci.reshape(slots, nc, nc, wide_lanes)
        cc = cc.reshape(slots, 6, ncf, wide_lanes)
        lo = lo.reshape(slots, 6, slots, wide_lanes)
        cr = cr.reshape(slots, 4, wide_lanes)

        shifts = [narrow_size * share, -narrow_size * share, share, -share]

        def coarse_ghosts(traces):
            out = jnp.einsum("efL,efqL->fqL", cr, traces[:, :4])
            return [jnp.roll(out[f ^ 1], shifts[f], axis=1) for f in range(4)]

        def coarse_couple(state):
            traces = face_traces(state, 2)
            ghosts = coarse_ghosts(traces)
            nearby = []
            for f in range(6):
                got = jnp.sum(lo[:, f, :, None, :] * traces[None, :, f ^ 1], axis=1)
                if f < 4:
                    got = got + cr[:, f, None, :] * ghosts[f]
                nearby.append(got * cc[:, f])
            return jnp.einsum("fpq,feqL->epL", coarse_lifts, jnp.stack(nearby), precision=highest)

        def coarse_apply(matrix, state):
            return jnp.sum(matrix * state[:, None], axis=2)

        def coarse_solve(rhs):
            state = damping * coarse_apply(ci, rhs)
            for _ in range(COARSE_SWEEPS - 1):
                res = rhs - coarse_apply(cb, state) - coarse_couple(state)
                state = state + damping * coarse_apply(ci, res)
            return state

        send = coarse_rhs.transpose(2, 0, 1).reshape(devices, share * slots * nc)
        got = lax.all_to_all(send, AXES, 0, 0, tiled=True)
        got = got.reshape(devices * share, slots * nc).T.reshape(slots, nc, devices * share)
        coarse = coarse_solve(got)
        ghosts = jnp.stack(coarse_ghosts(face_traces(coarse, 2)))
        back = jnp.concatenate([coarse.reshape(slots * nc, -1), ghosts.reshape(4 * ncf, -1)], axis=0)
        back = back.T.reshape(devices, share * (slots * nc + 4 * ncf))
        got = lax.all_to_all(back, AXES, 0, 0, tiled=True)
        got = got.reshape(columns, slots * nc + 4 * ncf).T
        coarse = got[: slots * nc].reshape(slots, nc, columns)
        ghosts = got[slots * nc :].reshape(4, ncf, columns)
        return coarse, ghosts

    def spread_solve(coarse_rhs):
        state = damping * block_apply(coarse_inverses, coarse_rhs)
        for _ in range(COARSE_SWEEPS - 1):
            traces = face_traces(state, 2)
            arrived = exchange(outgoing_of(traces))
            coupled = couple(traces, arrived, coarse_lifts, coarse_coefs)
            res = coarse_rhs - block_apply(coarse_blocks, state) - coupled
            state = state + damping * block_apply(coarse_inverses, res)
        return state, exchange(outgoing_of(face_traces(state, 2)))

    state = damping * block_apply(fine_inverses, rhs_live)
    for _ in range(PRE_SWEEPS - 1):
        traces = face_traces(state, NODE1)
        arrived = exchange(outgoing_of(traces))
        state = state + damping * block_apply(fine_inverses, residual_of(state, traces, arrived))
    traces = face_traces(state, NODE1)
    arrived = exchange(outgoing_of(traces))
    residual = residual_of(state, traces, arrived)
    coarse_rhs = 0.25 * jnp.einsum("pq,epr->eqr", prolong, residual, precision=highest)
    solver = split_solve if columns % devices == 0 else spread_solve
    coarse, ghosts = solver(coarse_rhs)
    state = state + jnp.einsum("pq,eqr->epr", prolong, coarse, precision=highest)
    arrived = arrived + jnp.einsum("pq,fqr->fpr", prolong_face, ghosts, precision=highest)
    for i in range(POST_SWEEPS):
        traces = face_traces(state, NODE1)
        if i > 0:
            arrived = exchange(outgoing_of(traces))
        state = state + damping * block_apply(fine_inverses, residual_of(state, traces, arrived))
    return state


def solution(mesh):
    placed = (
        P(AXES, None, None),
        P(AXES, None, None),
        P(AXES, None, None),
        P(),
        P(AXES, None, None),
        P(AXES, None, None),
        P(AXES, None, None),
        P(),
        P(AXES, None, None),
        P(AXES, None),
        P(AXES),
    )
    return jax.shard_map(
        body,
        mesh=mesh,
        in_specs=placed,
        out_specs=P(AXES, None, None),
        check_vma=False,
    )
```

```python
import functools

import jax
import jax.numpy as jnp
import numpy as np
from jax import lax
from jax.experimental import pallas as pl
from jax.experimental.pallas import tpu as pltpu
from jax.sharding import PartitionSpec as P

NVAR = 5
NODE1 = 4
PRE_SWEEPS = 2
POST_SWEEPS = 2
COARSE_SWEEPS = 4
AXES = ("wide", "narrow")
LANES = 128
VMEM_LIMIT = 40 * 1024 * 1024

damping = 0.8
highest = lax.Precision.HIGHEST
f32 = jnp.float32


def prolong_table(node_count, variables):
    points = np.array([-1.0, -1.0 / np.sqrt(5.0), 1.0 / np.sqrt(5.0), 1.0])
    linear = np.stack([(1.0 - points) / 2.0, (1.0 + points) / 2.0], axis=1)
    tensor_hat = (
        linear[:, None, None, :, None, None]
        * linear[None, :, None, None, :, None]
        * linear[None, None, :, None, None, :]
    )
    tensor_hat = tensor_hat.reshape(node_count * node_count * node_count, 8)
    return np.kron(np.eye(variables), tensor_hat).astype(np.float32)


def face_rows(node_count, variables):
    cube = node_count**3
    lattice = np.arange(cube).reshape(node_count, node_count, node_count)
    tables = []
    for face in range(6):
        layer = np.take(lattice, 0 if face % 2 == 0 else node_count - 1, axis=face // 2).reshape(-1)
        tables.append(np.concatenate([layer + v * cube for v in range(variables)]))
    return np.stack(tables)


def split(x):
    high = x.astype(jnp.bfloat16)
    return high, (x - high.astype(f32)).astype(jnp.bfloat16)


def dot(a, x):
    ah, al = split(a)
    xh, xl = split(x)
    n = x.shape[1]
    both = jnp.dot(ah, jnp.concatenate([xh, xl], axis=1), preferred_element_type=f32)
    return both[:, :n] + both[:, n:] + jnp.dot(al, xh, preferred_element_type=f32)


def face_of(state, e, face):
    if face == 0 or face == 1:
        start = 48 * face
        return jnp.concatenate([state[e, pl.ds(64 * v + start, 16)] for v in range(NVAR)], axis=0)
    if face >= 4:
        return state[e, pl.ds(3 * (face - 4), 80, stride=4)]
    half = 8 * (face - 2)
    first = jnp.concatenate([state[e, pl.ds(32 * m + half, 8)] for m in range(10)], axis=0)
    second = jnp.concatenate([state[e, pl.ds(32 * m + 16 + half, 8)] for m in range(10)], axis=0)
    low = lax.broadcasted_iota(jnp.int32, first.shape, 0) % 8 < 4
    if face == 2:
        return jnp.where(low, first, pltpu.roll(second, 4, 0))
    return jnp.where(low, pltpu.roll(first, 76, 0), second)


def link(ids, nbr, slots, e, face):
    g = nbr[e, face]
    owner = lax.div(g, slots)
    here = jnp.logical_and(g >= 0, owner == ids[2])
    away = jnp.logical_and(g >= 0, owner != ids[2])
    return here, away, jnp.maximum(lax.rem(g, slots), 0)


def swap_of(ids, face):
    return lax.rem(face % 2 + ids[face // 2] % 2 + 1, 2)


def local_residual(ids, nbr, rhs_of, state, blocks, lifts, coef, traces, out):
    slots = state.shape[0]
    for e in range(slots):
        for f in range(6):
            traces[f * slots + e] = face_of(state, e, f)
    for e in range(slots):
        near = []
        for f in range(6):
            here, _, s = link(ids, nbr, slots, e, f)
            t = traces[(f ^ 1) * slots + s] * coef[e, pl.ds(80 * f, 80)]
            near.append(jnp.where(here, t, 0.0))
        near = jnp.concatenate(near, axis=0)
        out[e] = rhs_of(e) - dot(blocks[e], state[e]) - dot(lifts[...], near)


def add_remote(ids, nbr, arrived, face_lifts, coef, out):
    slots = out.shape[0]
    for f in range(4):
        found, slot = False, 0
        for e in range(slots):
            _, away, _ = link(ids, nbr, slots, e, f)
            found = jnp.logical_or(found, away)
            slot = jnp.where(away, e, slot)
        t = arrived(f) * coef[slot, pl.ds(80 * f, 80)]
        out[slot] = out[slot] - dot(face_lifts[f], jnp.where(found, t, 0.0))


def fill_sends(ids, nbr, state, sends):
    slots = state.shape[0]
    leaving = []
    for f in range(4):
        t = jnp.zeros((80, state.shape[2]), f32)
        for e in range(slots):
            _, away, _ = link(ids, nbr, slots, e, f)
            t = jnp.where(away, face_of(state, e, f), t)
        leaving.append(t)
    for axis in range(2):
        low, high = leaving[2 * axis], leaving[2 * axis + 1]
        first = swap_of(ids, 2 * axis) == 0
        sends[2 * axis][...] = jnp.where(first, low, high)
        sends[2 * axis + 1][...] = jnp.where(first, high, low)


def arrivals(ids, ys):
    def arrived(f):
        a = 2 * (f // 2)
        return jnp.where(swap_of(ids, f) == 0, ys[a][...], ys[a + 1][...])

    return arrived


def first_kernel(ids, nbr, counts, rhs, inverses, v, s0, s1, s2, s3):
    for e in range(rhs.shape[0]):
        live = jnp.where(e < counts[0], rhs[e], 0.0)
        v[e] = damping * dot(inverses[e], live)
    fill_sends(ids, nbr, v, (s0, s1, s2, s3))


def local_kernel(ids, nbr, counts, rhs, state, blocks, lifts, coef, out, traces):
    def rhs_of(e):
        return jnp.where(e < counts[0], rhs[e], 0.0)

    local_residual(ids, nbr, rhs_of, state, blocks, lifts, coef, traces, out)


def sweep_kernel(send, ids, nbr, y0, y1, y2, y3, res, state, inverses, face_lifts, coef, v, *rest):
    work = rest[-1]
    work[...] = res[...]
    add_remote(ids, nbr, arrivals(ids, (y0, y1, y2, y3)), face_lifts, coef, work)
    for e in range(v.shape[0]):
        v[e] = state[e] + damping * dot(inverses[e], work[e])
    if send:
        fill_sends(ids, nbr, v, rest[:4])


def restrict_kernel(to_split, ids, nbr, y0, y1, y2, y3, res, face_lifts, coef, restrict, r, out):
    r[...] = res[...]
    add_remote(ids, nbr, arrivals(ids, (y0, y1, y2, y3)), face_lifts, coef, r)
    parts = [0.25 * dot(restrict[...], r[e]) for e in range(r.shape[0])]
    if not to_split:
        for e, part in enumerate(parts):
            out[e] = part
        return
    turned = jnp.concatenate(parts, axis=0).T
    owners, share = out.shape[:2]
    for j in range(share):
        out[:, j, :] = turned[j * owners : (j + 1) * owners]


def prolong_kernel(
    from_split, ids, nbr, coarse, r, state, blocks, inverses, lifts, face_lifts, coef, prolong, face_prolong,
    v, s0, s1, s2, s3, traces, work, correction,
):
    slots = v.shape[0]
    nc = prolong.shape[1]
    if from_split:
        share = coarse.shape[1]
        rows = jnp.concatenate([coarse[:, j, :] for j in range(share)], axis=0).T
    else:
        rows = coarse[...]
    for e in range(slots):
        correction[e] = dot(prolong[...], rows[e * nc : (e + 1) * nc])
    local_residual(ids, nbr, lambda e: r[e], correction, blocks, lifts, coef, traces, work)
    packs = [rows[(slots + a) * nc : (slots + a + 1) * nc] for a in range(2)]
    add_remote(ids, nbr, lambda f: dot(face_prolong[f ^ 1], packs[f // 2]), face_lifts, coef, work)
    for e in range(slots):
        v[e] = state[e] + correction[e] + damping * dot(inverses[e], work[e])
    fill_sends(ids, nbr, v, (s0, s1, s2, s3))


def spread_kernel(slots, gathered, out):
    rows_each = out.shape[0] // LANES + 1
    devices = gathered.shape[0] // (slots * rows_each)
    for c in range(rows_each - 1):
        parts = [
            gathered[pl.ds(e * rows_each + c, devices, stride=slots * rows_each), :] for e in range(slots)
        ]
        out[c * LANES : (c + 1) * LANES] = jnp.concatenate(parts, axis=0).T


def coarse_kernel(slots, got, table, lifts, back, rhs, w, work):
    devices, share, _ = got.shape
    nc = lifts.shape[0]
    rows = jnp.concatenate([got[:, j, :] for j in range(share)], axis=0).T
    group = lax.broadcasted_iota(jnp.int32, (nc, LANES), 1) // devices
    for j in range(share):
        total = jnp.zeros((nc, LANES), f32)
        for e in range(slots):
            x = rows[e * nc : (e + 1) * nc]
            shift = (e - j) * devices % LANES
            total = jnp.where(group == e, pltpu.roll(x, shift, 1) if shift else x, total)
        rhs[j] = total

    def apply(base, source):
        sums = [jnp.zeros((nc, LANES), f32) for _ in range(share)]
        for q in range(nc):
            m = table[base + q * nc : base + (q + 1) * nc]
            for j in range(share):
                sums[j] = sums[j] + m * source[j, pl.ds(q, 1), :]
        return sums

    inverse_at = nc * nc
    coef_at = 2 * nc * nc
    lane_at = coef_at + 6 * nc
    away_at = lane_at + 8

    def nearby(f, j):
        lane = table[lane_at + f : lane_at + f + 1].astype(jnp.int32)
        return jnp.take_along_axis(w[j], jnp.broadcast_to(lane, (nc, LANES)), axis=1, mode="promise_in_bounds")

    for j, part in enumerate(apply(inverse_at, rhs)):
        w[j] = damping * part

    def sweep(_, carry):
        near = [
            jnp.concatenate(
                [nearby(f, j) * table[coef_at + f * nc : coef_at + (f + 1) * nc] for f in range(6)], axis=0
            )
            for j in range(share)
        ]
        coupled = dot(lifts[...], jnp.concatenate(near, axis=1))
        for j, part in enumerate(apply(0, w)):
            work[j] = rhs[j] - part - coupled[:, j * LANES : (j + 1) * LANES]
        for j, part in enumerate(apply(inverse_at, work)):
            w[j] = w[j] + damping * part
        return carry

    lax.fori_loop(0, COARSE_SWEEPS - 1, sweep, 0)

    pieces = []
    for e in range(slots):
        total = jnp.zeros((nc, LANES), f32)
        for j in range(share):
            shift = (j - e) * devices % LANES
            x = w[j]
            total = jnp.where(group == j, pltpu.roll(x, shift, 1) if shift else x, total)
        pieces.append(total)
    row = lax.broadcasted_iota(jnp.int32, (nc, LANES), 0)
    for axis in range(2):
        first = row % 8 < 4 if axis == 0 else row % 4 < 2
        total = jnp.zeros((nc, LANES), f32)
        for j in range(share):
            ghosts = []
            for f in (2 * axis, 2 * axis + 1):
                g = nearby(f, j) * table[away_at + f : away_at + f + 1]
                shift = devices
                while shift < LANES:
                    g = g + pltpu.roll(g, shift, 1)
                    shift *= 2
                ghosts.append(g)
            total = jnp.where(group == j, jnp.where(first, ghosts[1], ghosts[0]), total)
        pieces.append(total)
    turned = jnp.concatenate(pieces, axis=0).T
    for j in range(share):
        back[:, j, :] = turned[j * devices : (j + 1) * devices]


def call(kernel, outs, scratch, smem, args, flops=0):
    specs = [pl.BlockSpec(memory_space=pltpu.SMEM)] * smem
    specs += [pl.BlockSpec(memory_space=pltpu.VMEM)] * (len(args) - smem)
    moved = sum(int(np.prod(a.shape)) * 4 for a in args) + sum(int(np.prod(s)) * 4 for s in outs)
    return pl.pallas_call(
        kernel,
        out_shape=[jax.ShapeDtypeStruct(s, f32) for s in outs],
        in_specs=specs,
        out_specs=[pl.BlockSpec(memory_space=pltpu.VMEM)] * len(outs),
        scratch_shapes=[pltpu.VMEM(s, f32) for s in scratch],
        compiler_params=pltpu.CompilerParams(vmem_limit_bytes=VMEM_LIMIT),
        cost_estimate=pl.CostEstimate(flops=flops, bytes_accessed=moved, transcendentals=0),
    )(*args)


def swap(parts):
    got = []
    for i, part in enumerate(parts):
        axis = AXES[i // 2]
        pairs = []
        for a in range(i % 2, lax.axis_size(axis) - 1, 2):
            pairs += [(a, a + 1), (a + 1, a)]
        got.append(lax.ppermute(part, axis, pairs))
    return got


def body(
    right_side,
    fine_blocks,
    fine_inverses,
    fine_lifts,
    fine_coefs,
    coarse_blocks,
    coarse_inverses,
    coarse_lifts,
    coarse_coefs,
    neighbours,
    counts,
):
    slots, nf, columns = right_side.shape
    nface = fine_lifts.shape[2]
    nc = coarse_blocks.shape[1]
    narrow_size = lax.axis_size("narrow")
    devices = lax.axis_size("wide") * narrow_size
    wide_here, narrow_here = lax.axis_index("wide"), lax.axis_index("narrow")
    device_id = wide_here * narrow_size + narrow_here
    ids = jnp.stack([wide_here, narrow_here, device_id]).astype(jnp.int32)
    to_split = columns % devices == 0 and slots * devices == LANES and columns == LANES
    share = columns // devices

    prolong_np = prolong_table(NODE1, NVAR)
    coarse_table = face_rows(2, NVAR)
    fine_table = face_rows(NODE1, NVAR)
    prolong = jnp.asarray(prolong_np)
    restrict = jnp.asarray(np.ascontiguousarray(prolong_np.T))
    face_prolong = jnp.asarray(np.stack([prolong_np[fine_table[f]] for f in range(4)]))
    hot = np.zeros((6, coarse_table.shape[1], nc), np.float32)
    for f in range(6):
        hot[f, np.arange(coarse_table.shape[1]), coarse_table[f ^ 1]] = 1.0
    hot = jnp.asarray(hot)

    present = neighbours >= 0
    owner = neighbours // slots
    away = jnp.logical_and(present, owner != device_id)[:, :4]
    wide_lifts = jnp.einsum("fpq,fqu->pfu", coarse_lifts, hot, precision=highest).reshape(nc, 6 * nc)

    if to_split:
        wide_coefs = jnp.einsum("efq,fqu->efu", coarse_coefs, hot, precision=highest)
        wide_coefs = wide_coefs * present[:, :, None]
        lane = jnp.where(present, (neighbours % slots) * devices + owner, 0).astype(f32)
        flat = jnp.concatenate(
            [
                coarse_blocks.transpose(0, 2, 1).reshape(slots, nc * nc),
                coarse_inverses.transpose(0, 2, 1).reshape(slots, nc * nc),
                wide_coefs.reshape(slots, 6 * nc),
                jnp.pad(lane, ((0, 0), (0, 2))),
                away.astype(f32),
            ],
            axis=1,
        )
        chunks = -(-flat.shape[1] // LANES)
        rows_each = chunks + 1
        flat = jnp.pad(flat, ((0, 0), (0, rows_each * LANES - flat.shape[1])))
        everyone = lax.all_gather(flat.reshape(slots * rows_each, LANES), AXES, tiled=True)

    coef = jnp.broadcast_to(fine_coefs.reshape(slots, 6 * nface, 1), (slots, 6 * nface, columns))
    lifts = fine_lifts.transpose(1, 0, 2).reshape(nf, 6 * nface)
    field = (slots, nf, columns)
    face = (nface, columns)
    trace_room = (6 * slots, nface, columns)
    block_flops = 3 * 2 * slots * nf * nf * columns
    lift_flops = 3 * 2 * slots * nf * 6 * nface * columns

    def local(state):
        (res,) = call(
            local_kernel, [field], [trace_room], 3,
            (ids, neighbours, counts, right_side, state, fine_blocks, lifts, coef), block_flops + lift_flops,
        )
        return res

    def sweep(send, got, res, state):
        return call(
            functools.partial(sweep_kernel, send), [field] + [face] * (4 if send else 0), [field], 2,
            (ids, neighbours, *got, res, state, fine_inverses, fine_lifts, coef), block_flops,
        )

    state, *sends = call(
        first_kernel, [field] + [face] * 4, [], 3, (ids, neighbours, counts, right_side, fine_inverses), block_flops
    )
    for _ in range(PRE_SWEEPS - 1):
        got = swap(sends)
        state, *sends = sweep(True, got, local(state), state)
    got = swap(sends)
    coarse_shape = (devices, share, slots * nc) if to_split else (slots, nc, columns)
    residual, coarse_rhs = call(
        functools.partial(restrict_kernel, to_split), [field, coarse_shape], [], 2,
        (ids, neighbours, *got, local(state), fine_lifts, coef, restrict),
    )

    if to_split:
        (table,) = call(functools.partial(spread_kernel, slots), [(chunks * LANES, LANES)], [], 0, (everyone,))
        arrived = lax.all_to_all(coarse_rhs, AXES, 0, 0, tiled=True)
        (back,) = call(
            functools.partial(coarse_kernel, slots), [(devices, share, (slots + 2) * nc)],
            [(share, nc, LANES)] * 3, 0, (arrived, table, wide_lifts),
        )
        coarse = lax.all_to_all(back, AXES, 0, 0, tiled=True)
    else:
        coarse = spread_solve(
            coarse_rhs, coarse_blocks, coarse_inverses, coarse_lifts, coarse_coefs, neighbours, device_id, ids
        )

    state, *sends = call(
        functools.partial(prolong_kernel, to_split), [field] + [face] * 4, [trace_room, field, field], 2,
        (ids, neighbours, coarse, residual, state, fine_blocks, fine_inverses, lifts, fine_lifts, coef, prolong,
         face_prolong), 2 * block_flops + lift_flops,
    )
    for i in range(POST_SWEEPS - 1):
        got = swap(sends)
        state, *sends = sweep(i < POST_SWEEPS - 2, got, local(state), state)
    return state


def spread_solve(rhs, blocks, inverses, lifts, coefs, neighbours, device_id, ids):
    slots, nc, columns = rhs.shape
    table = face_rows(2, NVAR)
    present = neighbours >= 0
    owner = neighbours // slots
    here = jnp.logical_and(present, owner == device_id)
    local = jnp.logical_and(here[:, :, None], (neighbours % slots)[:, :, None] == jnp.arange(slots)).astype(f32)
    away = jnp.logical_and(present, owner != device_id).astype(f32)[:, :4]

    def block_apply(matrix, state):
        return jnp.einsum("epq,eqr->epr", matrix, state, precision=highest)

    def traces_of(state):
        return jnp.stack([state[:, table[f]] for f in range(6)], axis=1)

    def exchange(traces):
        leaving = jnp.einsum("ef,efqr->fqr", away, traces[:, :4], precision=highest)
        sends = []
        for axis in range(2):
            first = swap_of(ids, 2 * axis) == 0
            low, high = leaving[2 * axis], leaving[2 * axis + 1]
            sends += [jnp.where(first, low, high), jnp.where(first, high, low)]
        return pick(swap(sends))

    def pick(got):
        return [
            jnp.where(swap_of(ids, f) == 0, got[2 * (f // 2)], got[2 * (f // 2) + 1]) for f in range(4)
        ]

    def couple(state):
        traces = traces_of(state)
        arrived = exchange(traces)
        near = []
        for f in range(6):
            got = jnp.einsum("eg,gqr->eqr", local[:, f], traces[:, f ^ 1], precision=highest)
            if f < 4:
                got = got + away[:, f, None, None] * arrived[f]
            near.append(got * coefs[:, f, :, None])
        return jnp.einsum("fpq,feqr->epr", lifts, jnp.stack(near), precision=highest)

    state = damping * block_apply(inverses, rhs)
    for _ in range(COARSE_SWEEPS - 1):
        state = state + damping * block_apply(inverses, rhs - block_apply(blocks, state) - couple(state))
    arrived = exchange(traces_of(state))
    packs = []
    for axis in range(2):
        pack = jnp.zeros((nc, columns), f32)
        for f in (2 * axis, 2 * axis + 1):
            pack = pack.at[table[f ^ 1]].set(arrived[f])
        packs.append(pack)
    return jnp.concatenate([state.reshape(slots * nc, columns)] + packs, axis=0)


def solution(mesh):
    placed = (
        P(AXES, None, None),
        P(AXES, None, None),
        P(AXES, None, None),
        P(),
        P(AXES, None, None),
        P(AXES, None, None),
        P(AXES, None, None),
        P(),
        P(AXES, None, None),
        P(AXES, None),
        P(AXES),
    )
    return jax.shard_map(
        body,
        mesh=mesh,
        in_specs=placed,
        out_specs=P(AXES, None, None),
        check_vma=False,
    )
```

```python
import functools

import jax
import jax.numpy as jnp
import numpy as np
from jax import lax
from jax.experimental import pallas as pl
from jax.experimental.pallas import tpu as pltpu
from jax.sharding import PartitionSpec as P

NVAR = 5
NODE1 = 4
PRE_SWEEPS = 2
POST_SWEEPS = 2
COARSE_SWEEPS = 4
AXES = ("wide", "narrow")
VMEM_LIMIT = 40 * 1024 * 1024

damping = 0.8
highest = lax.Precision.HIGHEST
f32, bf16 = jnp.float32, jnp.bfloat16


def prolong_table(node_count, variables):
    points = np.array([-1.0, -1.0 / np.sqrt(5.0), 1.0 / np.sqrt(5.0), 1.0])
    linear = np.stack([(1.0 - points) / 2.0, (1.0 + points) / 2.0], axis=1)
    tensor_hat = (
        linear[:, None, None, :, None, None]
        * linear[None, :, None, None, :, None]
        * linear[None, None, :, None, None, :]
    )
    tensor_hat = tensor_hat.reshape(node_count * node_count * node_count, 8)
    return np.kron(np.eye(variables), tensor_hat).astype(np.float32)


def face_rows(node_count, variables):
    cube = node_count**3
    lattice = np.arange(cube).reshape(node_count, node_count, node_count)
    tables = []
    for face in range(6):
        layer = np.take(lattice, 0 if face % 2 == 0 else node_count - 1, axis=face // 2).reshape(-1)
        tables.append(np.concatenate([layer + v * cube for v in range(variables)]))
    return np.stack(tables)


class Fetched:
    def __init__(self, source, room, sems, base, parts):
        self.room, self.ready = room, set()
        if parts == 1:
            self.copies = [pltpu.make_async_copy(source, room, sems.at[base])]
        else:
            self.copies = [
                pltpu.make_async_copy(source.at[i], room.at[i], sems.at[base + i]) for i in range(parts)
            ]

    def start(self):
        for copy in self.copies:
            copy.start()

    def wait(self, part):
        if part not in self.ready:
            self.ready.add(part)
            self.copies[part].wait()

    def wait_all(self):
        for part in range(len(self.copies)):
            self.wait(part)

    def __getitem__(self, index):
        first = index[0] if isinstance(index, tuple) else index
        if len(self.copies) > 1 and isinstance(first, int):
            self.wait(first)
        else:
            self.wait_all()
        return self.room[index]

    @property
    def shape(self):
        return self.room.shape


def call(kernel, outs, scratch, args, flops=0):
    specs, rooms, counts = [], [], []
    for kind, a in args:
        if kind in ("smem", "vmem"):
            specs.append(pl.BlockSpec(memory_space=pltpu.SMEM if kind == "smem" else pltpu.VMEM))
        else:
            specs.append(pl.BlockSpec(memory_space=pl.ANY))
            rooms.append(pltpu.VMEM(a.shape, a.dtype))
            counts.append(a.shape[0] if kind == "parts" else 1)
    out_rooms = [pltpu.VMEM(shape, dtype) for kind, shape, dtype in outs if kind == "hbm"]
    out_parts = sum(shape[0] for kind, shape, _ in outs if kind == "hbm")
    n_in, n_out, n_rooms = len(args), len(outs), len(rooms)

    def wrapped(*refs):
        ins, results, rest = refs[:n_in], refs[n_in : n_in + n_out], refs[n_in + n_out :]
        in_rooms, rest = rest[:n_rooms], rest[n_rooms:]
        result_rooms, rest = rest[: len(out_rooms)], rest[len(out_rooms) :]
        sems, rest = rest[0], rest[1:]
        given, base, at = [], 0, 0
        for (kind, _), ref in zip(args, ins):
            if kind in ("smem", "vmem"):
                given.append(ref)
                continue
            item = Fetched(ref, in_rooms[at], sems, base, counts[at])
            base += counts[at]
            at += 1
            given.append(item)
        for item in given:
            if isinstance(item, Fetched):
                item.start()
        leaving, produced, at = [], [], 0
        for (kind, shape, _), ref in zip(outs, results):
            if kind == "vmem":
                produced.append(ref)
                continue
            room = result_rooms[at]
            produced.append((room, [pltpu.make_async_copy(room.at[i], ref.at[i], sems.at[base + i]) for i in range(shape[0])]))
            leaving += produced[-1][1]
            base += shape[0]
            at += 1
        kernel(*given, *produced, *rest)
        for item in given:
            if isinstance(item, Fetched):
                item.wait_all()
        for copy in leaving:
            copy.wait()

    moved = sum(int(np.prod(a.shape)) * a.dtype.itemsize for _, a in args)
    moved += sum(int(np.prod(shape)) * 4 for _, shape, _ in outs)
    return pl.pallas_call(
        wrapped,
        out_shape=[jax.ShapeDtypeStruct(shape, dtype) for _, shape, dtype in outs],
        in_specs=specs,
        out_specs=[pl.BlockSpec(memory_space=pltpu.VMEM if kind == "vmem" else pl.ANY) for kind, _, _ in outs],
        scratch_shapes=rooms
        + out_rooms
        + [pltpu.SemaphoreType.DMA((max(sum(counts) + out_parts, 1),))]
        + [pltpu.VMEM(shape, dtype) for shape, dtype in scratch],
        compiler_params=pltpu.CompilerParams(vmem_limit_bytes=VMEM_LIMIT),
        cost_estimate=pl.CostEstimate(flops=flops, bytes_accessed=moved, transcendentals=0),
    )(*[a for _, a in args])


def split(x):
    high = x.astype(bf16)
    return high, (x - high.astype(f32)).astype(bf16)


def dot(a, x):
    ah, al = a if isinstance(a, tuple) else split(a)
    xh, xl = split(x)
    n = x.shape[1]
    both = jnp.dot(ah, jnp.concatenate([xh, xl], axis=1), preferred_element_type=f32)
    return both[:, :n] + both[:, n:] + jnp.dot(al, xh, preferred_element_type=f32)


def small_dot(a, x):
    return jnp.dot(a, x, precision=highest, preferred_element_type=f32)


def face_of(state, e, face):
    if face == 0 or face == 1:
        start = 48 * face
        return jnp.concatenate([state[e, pl.ds(64 * v + start, 16)] for v in range(NVAR)], axis=0)
    if face >= 4:
        return state[e, pl.ds(3 * (face - 4), 80, stride=4)]
    half = 8 * (face - 2)
    first = jnp.concatenate([state[e, pl.ds(32 * m + half, 8)] for m in range(10)], axis=0)
    second = jnp.concatenate([state[e, pl.ds(32 * m + 16 + half, 8)] for m in range(10)], axis=0)
    low = lax.broadcasted_iota(jnp.int32, first.shape, 0) % 8 < 4
    if face == 2:
        return jnp.where(low, first, pltpu.roll(second, 4, 0))
    return jnp.where(low, pltpu.roll(first, 76, 0), second)


def link(ids, nbr, slots, e, face):
    g = nbr[e, face]
    owner = lax.div(g, slots)
    here = jnp.logical_and(g >= 0, owner == ids[2])
    away = jnp.logical_and(g >= 0, owner != ids[2])
    return here, away, jnp.maximum(lax.rem(g, slots), 0)


def crossing(ids, nbr, slots, face):
    found, slot = False, 0
    for e in range(slots):
        _, away, _ = link(ids, nbr, slots, e, face)
        found = jnp.logical_or(found, away)
        slot = jnp.where(away, e, slot)
    return found, slot


def swap_of(ids, face):
    return lax.rem(face % 2 + ids[face // 2] % 2 + 1, 2)


def arrived(ids, ys, f):
    a = 2 * (f // 2)
    return jnp.where(swap_of(ids, f) == 0, ys[a][...], ys[a + 1][...])


def fill_sends(ids, nbr, slots, sends, part_of):
    leaving = []
    for f in range(4):
        t = part_of(0, f)
        for e in range(1, slots):
            _, away, _ = link(ids, nbr, slots, e, f)
            t = jnp.where(away, part_of(e, f), t)
        leaving.append(t)
    for axis in range(2):
        low, high = leaving[2 * axis], leaving[2 * axis + 1]
        first = swap_of(ids, 2 * axis) == 0
        sends[2 * axis][...] = jnp.where(first, low, high)
        sends[2 * axis + 1][...] = jnp.where(first, high, low)


def fill_traces(ids, nbr, state, sends):
    fill_sends(ids, nbr, state.shape[0], sends, lambda e, f: face_of(state, e, f))


def first_kernel(ids, nbr, counts, rhs, inverses, v, *sends):
    for e in range(rhs.shape[0]):
        live = jnp.where(e < counts[0], rhs[e], 0.0)
        v[e] = damping * dot(inverses[e], live)
    fill_traces(ids, nbr, v, sends)


def local_residual(ids, nbr, rhs_of, state, blocks, lifts, coef, out, traces):
    slots = state.shape[0]
    for e in range(slots):
        for f in range(6):
            traces[f * slots + e] = face_of(state, e, f)
    for e in range(slots):
        near = []
        for f in range(6):
            here, _, s = link(ids, nbr, slots, e, f)
            t = traces[(f ^ 1) * slots + s] * coef[e, pl.ds(80 * f, 80)]
            near.append(jnp.where(here, t, 0.0))
        near = jnp.concatenate(near, axis=0)
        out[e] = rhs_of(e) - dot(blocks[e], state[e]) - dot(lifts(), near)


def lay_out(lifts_t, coefs, lh, ll, fh, fl, coef):
    faces, nface, nf = lifts_t.shape
    slots = coef[0].shape[0]
    whole = jnp.concatenate([lifts_t[f] for f in range(faces)], axis=0).T
    for parts, value in zip((lh, ll), split(whole)):
        parts[0][0] = value
        parts[1][0].start()
    for f in range(4):
        for parts, value in zip((fh, fl), split(lifts_t[f].T)):
            parts[0][f] = value
            parts[1][f].start()
    turned = coefs[...].T
    for e in range(slots):
        for f in range(faces):
            column = turned[:, f * slots + e : f * slots + e + 1]
            coef[0][e, nface * f : nface * (f + 1)] = jnp.broadcast_to(column, (nface, coef[0].shape[2]))
        coef[1][e].start()


def first_local_kernel(
    ids, nbr, counts, state, lifts_t, coefs, blocks, rhs, out, lh, ll, fh, fl, coef, traces
):
    lay_out(lifts_t, coefs, lh, ll, fh, fl, coef)

    def rhs_of(e):
        return jnp.where(e < counts[0], rhs[e], 0.0)

    local_residual(
        ids, nbr, rhs_of, state, blocks, lambda: (lh[0][0], ll[0][0]), coef[0], out, traces
    )


def local_kernel(ids, nbr, counts, state, lh, ll, blocks, coef, rhs, out, traces):
    def rhs_of(e):
        return jnp.where(e < counts[0], rhs[e], 0.0)

    local_residual(ids, nbr, rhs_of, state, blocks, lambda: (lh[0], ll[0]), coef, out, traces)


def add_remote(ids, nbr, arrival, fh, fl, coef, out):
    slots = out.shape[0]
    for f in range(4):
        found, slot = crossing(ids, nbr, slots, f)
        t = arrival(f) * coef[slot, pl.ds(80 * f, 80)]
        out[slot] = out[slot] - dot((fh[f], fl[f]), jnp.where(found, t, 0.0))


def sweep_kernel(ids, nbr, y0, y1, y2, y3, res, state, fh, fl, coef, inverses, v, *rest):
    sends, work = rest[:-1], rest[-1]
    work[...] = res[...]
    add_remote(ids, nbr, functools.partial(arrived, ids, (y0, y1, y2, y3)), fh, fl, coef, work)
    for e in range(work.shape[0]):
        value = state[e] + damping * dot(inverses[e], work[e])
        if sends:
            v[e] = value
        else:
            v[0][e] = value
            v[1][e].start()
    if sends:
        fill_traces(ids, nbr, v, sends)


def restrict_kernel(ids, nbr, y0, y1, y2, y3, res, fh, fl, coef, restrict, inverses, r, rhs, w, *sends):
    r[...] = res[...]
    add_remote(ids, nbr, functools.partial(arrived, ids, (y0, y1, y2, y3)), fh, fl, coef, r)
    slots = r.shape[0]
    for e in range(slots):
        rhs[e] = 0.25 * dot(restrict[...], r[e])
        w[e] = damping * dot(inverses[e], rhs[e])
    fill_sends(ids, nbr, slots, sends, lambda e, f: w[e])


def prolong_kernel(ids, nbr, r, state, w, lh, ll, blocks, coef, prolong, out, corrected, traces, correction):
    slots = state.shape[0]
    for e in range(slots):
        correction[e] = dot(prolong[...], w[e])
        corrected[e] = state[e] + correction[e]
    local_residual(
        ids, nbr, lambda e: r[e], correction, blocks, lambda: (lh[0], ll[0]), coef, out, traces
    )


def post_kernel(
    ids, nbr, y0, y1, y2, y3, res, state, face_prolong, fh, fl, coef, inverses, v, *rest
):
    sends, work = rest[:-1], rest[-1]
    work[...] = res[...]
    ys = (y0, y1, y2, y3)
    add_remote(ids, nbr, lambda f: dot(face_prolong[f ^ 1], arrived(ids, ys, f)), fh, fl, coef, work)
    for e in range(work.shape[0]):
        v[e] = state[e] + damping * dot(inverses[e], work[e])
    fill_traces(ids, nbr, v, sends)


def coarse_setup_kernel(ids, nbr, lifts_t, coefs, inverses, hot_t, lifts, coef, remote):
    faces = lifts_t.shape[0]
    slots, nc, _ = inverses.shape
    turned = coefs[...].T
    wide = [small_dot(hot_t[f], lifts_t[f]) for f in range(faces)]
    lifts[...] = jnp.concatenate(wide, axis=0).T
    for f in range(faces):
        spread = small_dot(hot_t[f], turned)
        for e in range(slots):
            column = spread[:, f * slots + e : f * slots + e + 1]
            coef[e, nc * f : nc * (f + 1)] = jnp.broadcast_to(column, (nc, coef.shape[2]))
    for f in range(4):
        found, slot = crossing(ids, nbr, slots, f)
        scaled = wide[f] * coef[slot, nc * f : nc * (f + 1)][:, :nc]
        product = damping * small_dot(inverses[slot], scaled.T)
        remote[f] = jnp.where(found, product, 0.0)


def coarse_local_kernel(ids, nbr, w, rhs, blocks, inverses, lifts, coef, out):
    slots, nc, columns = w.shape
    near = []
    for e in range(slots):
        parts = []
        for f in range(6):
            here, _, s = link(ids, nbr, slots, e, f)
            parts.append(jnp.where(here, w[s] * coef[e, nc * f : nc * (f + 1)], 0.0))
        near.append(jnp.concatenate(parts, axis=0))
    coupled = dot(lifts[...], jnp.concatenate(near, axis=1))
    for e in range(slots):
        res = rhs[e] - dot(blocks[e], w[e]) - coupled[:, e * columns : (e + 1) * columns]
        out[e] = w[e] + damping * dot(inverses[e], res)


def coarse_sweep_kernel(ids, nbr, y0, y1, y2, y3, local, remote, w, *sends):
    w[...] = local[...]
    slots = w.shape[0]
    ys = (y0, y1, y2, y3)
    parts = [dot(remote[f], arrived(ids, ys, f)) for f in range(4)]
    for f in range(4):
        _, slot = crossing(ids, nbr, slots, f)
        w[slot] = w[slot] - parts[f]
    fill_sends(ids, nbr, slots, sends, lambda e, f: w[e])


def swap(parts):
    got = []
    for i, part in enumerate(parts):
        axis = AXES[i // 2]
        pairs = []
        for a in range(i % 2, lax.axis_size(axis) - 1, 2):
            pairs += [(a, a + 1), (a + 1, a)]
        got.append(lax.ppermute(part, axis, pairs))
    return got


def body(
    right_side,
    fine_blocks,
    fine_inverses,
    fine_lifts,
    fine_coefs,
    coarse_blocks,
    coarse_inverses,
    coarse_lifts,
    coarse_coefs,
    neighbours,
    counts,
):
    slots, nf, columns = right_side.shape
    nface = fine_lifts.shape[2]
    nc = coarse_blocks.shape[1]
    ncf = coarse_lifts.shape[2]
    wide_here, narrow_here = lax.axis_index("wide"), lax.axis_index("narrow")
    ids = jnp.stack([wide_here, narrow_here, wide_here * lax.axis_size("narrow") + narrow_here]).astype(jnp.int32)

    prolong_np = prolong_table(NODE1, NVAR)
    coarse_table = face_rows(2, NVAR)
    fine_table = face_rows(NODE1, NVAR)
    prolong = jnp.asarray(prolong_np)
    restrict = jnp.asarray(np.ascontiguousarray(prolong_np.T))
    face_prolong = jnp.asarray(np.stack([prolong_np[fine_table[f]] for f in range(4)]))
    hot_np = np.zeros((6, nc, ncf), np.float32)
    for f in range(6):
        hot_np[f, coarse_table[f ^ 1], np.arange(ncf)] = 1.0
    hot_t = jnp.asarray(hot_np)

    lifts_t = fine_lifts.transpose(0, 2, 1)
    coefs = fine_coefs.transpose(1, 0, 2).reshape(6 * slots, nface)
    coarse_lifts_t = coarse_lifts.transpose(0, 2, 1)
    coarse_coefs_t = coarse_coefs.transpose(1, 0, 2).reshape(6 * slots, ncf)

    field = ("vmem", (slots, nf, columns), f32)
    faces = [("vmem", (nface, columns), f32)] * 4
    coarse = ("vmem", (slots, nc, columns), f32)
    coarse_sends = [("vmem", (nc, columns), f32)] * 4
    trace_room = ((6 * slots, nface, columns), f32)
    field_room = (field[1], f32)
    block_flops = 3 * 2 * slots * nf * nf * columns
    lift_flops = 3 * 2 * slots * nf * 6 * nface * columns
    where = [("smem", ids), ("smem", neighbours)]
    live = where + [("smem", counts)]

    def vm(*arrays):
        return [("vmem", a) for a in arrays]

    def hbm(*arrays):
        return [("hbm", a) for a in arrays]

    def parts(*arrays):
        return [("parts", a) for a in arrays]

    state, *sends = call(first_kernel, [field] + faces, [], live + parts(right_side, fine_inverses), block_flops)
    got = swap(sends)
    res, lh, ll, fh, fl, coef = call(
        first_local_kernel,
        [field]
        + [("hbm", (1, nf, 6 * nface), bf16)] * 2
        + [("hbm", (4, nf, nface), bf16)] * 2
        + [("hbm", (slots, 6 * nface, columns), f32)],
        [trace_room],
        live + vm(state) + parts(lifts_t) + hbm(coefs) + parts(fine_blocks, right_side),
        block_flops + lift_flops,
    )

    def local(state):
        return call(
            local_kernel, [field], [trace_room],
            live + vm(state) + hbm(lh, ll) + parts(fine_blocks, coef, right_side), block_flops + lift_flops,
        )[0]

    def sweep(got, res, state, last):
        return call(
            sweep_kernel, [("hbm",) + field[1:]] if last else [field] + faces, [field_room],
            where + vm(*got, res, state) + parts(fh, fl, coef, fine_inverses), block_flops,
        )

    for i in range(PRE_SWEEPS - 1):
        state, *sends = sweep(got, res, state, False)
        got = swap(sends)
        res = local(state)
    coarse_wide, coarse_coef, coarse_remote = call(
        coarse_setup_kernel,
        [("vmem", (nc, 6 * nc), f32), ("vmem", (slots, 6 * nc, columns), f32), ("vmem", (4, nc, nc), f32)], [],
        where + hbm(coarse_lifts_t, coarse_coefs_t, coarse_inverses, hot_t),
    )
    residual, coarse_rhs, w, *sends = call(
        restrict_kernel, [field, coarse, coarse] + coarse_sends, [],
        where + vm(*got, res) + parts(fh, fl, coef) + hbm(restrict, coarse_inverses),
    )
    for _ in range(COARSE_SWEEPS - 1):
        got = swap(sends)
        (w_local,) = call(
            coarse_local_kernel, [coarse], [],
            where + vm(w, coarse_rhs) + hbm(coarse_blocks, coarse_inverses) + vm(coarse_wide, coarse_coef),
        )
        w, *sends = call(
            coarse_sweep_kernel, [coarse] + coarse_sends, [], where + vm(*got, w_local, coarse_remote)
        )
    got = swap(sends)
    res, state = call(
        prolong_kernel, [field, field], [trace_room, field_room],
        where + vm(residual, state, w) + hbm(lh, ll) + parts(fine_blocks, coef) + hbm(prolong),
        block_flops + lift_flops,
    )
    state, *sends = call(
        post_kernel, [field] + faces, [field_room],
        where + vm(*got, res, state) + hbm(face_prolong) + parts(fh, fl, coef, fine_inverses), block_flops,
    )
    for i in range(POST_SWEEPS - 1):
        got = swap(sends)
        res = local(state)
        state, *sends = sweep(got, res, state, i == POST_SWEEPS - 2)
    return state


def solution(mesh):
    placed = (
        P(AXES, None, None),
        P(AXES, None, None),
        P(AXES, None, None),
        P(),
        P(AXES, None, None),
        P(AXES, None, None),
        P(AXES, None, None),
        P(),
        P(AXES, None, None),
        P(AXES, None),
        P(AXES),
    )
    return jax.shard_map(
        body,
        mesh=mesh,
        in_specs=placed,
        out_specs=P(AXES, None, None),
        check_vma=False,
    )
```

```python
import functools

import jax
import jax.numpy as jnp
import numpy as np
from jax import lax
from jax.experimental import pallas as pl
from jax.experimental.pallas import tpu as pltpu
from jax.sharding import PartitionSpec as P

NVAR = 5
NODE1 = 4
PRE_SWEEPS = 2
POST_SWEEPS = 2
COARSE_SWEEPS = 4
AXES = ("wide", "narrow")
VMEM_LIMIT = 16 * 1024 * 1024

damping = 0.8
highest = lax.Precision.HIGHEST
f32, bf16 = jnp.float32, jnp.bfloat16


def prolong_table(node_count, variables):
    points = np.array([-1.0, -1.0 / np.sqrt(5.0), 1.0 / np.sqrt(5.0), 1.0])
    linear = np.stack([(1.0 - points) / 2.0, (1.0 + points) / 2.0], axis=1)
    tensor_hat = (
        linear[:, None, None, :, None, None]
        * linear[None, :, None, None, :, None]
        * linear[None, None, :, None, None, :]
    )
    tensor_hat = tensor_hat.reshape(node_count * node_count * node_count, 8)
    return np.kron(np.eye(variables), tensor_hat).astype(np.float32)


def face_rows(node_count, variables):
    cube = node_count**3
    lattice = np.arange(cube).reshape(node_count, node_count, node_count)
    tables = []
    for face in range(6):
        layer = np.take(lattice, 0 if face % 2 == 0 else node_count - 1, axis=face // 2).reshape(-1)
        tables.append(np.concatenate([layer + v * cube for v in range(variables)]))
    return np.stack(tables)


class Fetched:
    def __init__(self, source, room, sems, base, parts):
        self.room, self.ready = room, set()
        if parts == 1:
            self.copies = [pltpu.make_async_copy(source, room, sems.at[base])]
        else:
            self.copies = [
                pltpu.make_async_copy(source.at[i], room.at[i], sems.at[base + i]) for i in range(parts)
            ]

    def start(self):
        for copy in self.copies:
            copy.start()

    def wait(self, part):
        if part not in self.ready:
            self.ready.add(part)
            self.copies[part].wait()

    def wait_all(self):
        for part in range(len(self.copies)):
            self.wait(part)

    def __getitem__(self, index):
        first = index[0] if isinstance(index, tuple) else index
        if len(self.copies) > 1 and isinstance(first, int):
            self.wait(first)
        else:
            self.wait_all()
        return self.room[index]

    @property
    def shape(self):
        return self.room.shape


def call(kernel, outs, scratch, args, flops=0):
    specs, rooms, counts = [], [], []
    for kind, a in args:
        if kind in ("smem", "vmem"):
            specs.append(pl.BlockSpec(memory_space=pltpu.SMEM if kind == "smem" else pltpu.VMEM))
        else:
            specs.append(pl.BlockSpec(memory_space=pltpu.HBM))
            rooms.append(pltpu.VMEM(a.shape, a.dtype))
            counts.append(a.shape[0] if kind == "parts" else 1)
    out_rooms = [pltpu.VMEM(shape, dtype) for kind, shape, dtype in outs if kind == "hbm"]
    out_parts = sum(shape[0] for kind, shape, _ in outs if kind == "hbm")
    n_in, n_out, n_rooms = len(args), len(outs), len(rooms)

    def wrapped(*refs):
        ins, results, rest = refs[:n_in], refs[n_in : n_in + n_out], refs[n_in + n_out :]
        in_rooms, rest = rest[:n_rooms], rest[n_rooms:]
        result_rooms, rest = rest[: len(out_rooms)], rest[len(out_rooms) :]
        sems, rest = rest[0], rest[1:]
        given, base, at = [], 0, 0
        for (kind, _), ref in zip(args, ins):
            if kind in ("smem", "vmem"):
                given.append(ref)
                continue
            item = Fetched(ref, in_rooms[at], sems, base, counts[at])
            base += counts[at]
            at += 1
            given.append(item)
        for item in given:
            if isinstance(item, Fetched):
                item.start()
        leaving, produced, at = [], [], 0
        for (kind, shape, _), ref in zip(outs, results):
            if kind == "vmem":
                produced.append(ref)
                continue
            room = result_rooms[at]
            produced.append((room, [pltpu.make_async_copy(room.at[i], ref.at[i], sems.at[base + i]) for i in range(shape[0])]))
            leaving += produced[-1][1]
            base += shape[0]
            at += 1
        kernel(*given, *produced, *rest)
        for item in given:
            if isinstance(item, Fetched):
                item.wait_all()
        for copy in leaving:
            copy.wait()

    moved = sum(int(np.prod(a.shape)) * a.dtype.itemsize for _, a in args)
    moved += sum(int(np.prod(shape)) * 4 for _, shape, _ in outs)
    return pl.pallas_call(
        wrapped,
        out_shape=[jax.ShapeDtypeStruct(shape, dtype) for _, shape, dtype in outs],
        in_specs=specs,
        out_specs=[pl.BlockSpec(memory_space=pltpu.VMEM if kind == "vmem" else pltpu.HBM) for kind, _, _ in outs],
        scratch_shapes=rooms
        + out_rooms
        + [pltpu.SemaphoreType.DMA((max(sum(counts) + out_parts, 1),))]
        + [pltpu.VMEM(shape, dtype) for shape, dtype in scratch],
        compiler_params=pltpu.CompilerParams(vmem_limit_bytes=VMEM_LIMIT),
        cost_estimate=pl.CostEstimate(flops=flops, bytes_accessed=moved, transcendentals=0),
    )(*[a for _, a in args])


def split(x):
    high = x.astype(bf16)
    return high, (x - high.astype(f32)).astype(bf16)


def dot(a, x):
    ah, al = a if isinstance(a, tuple) else split(a)
    xh, xl = split(x)
    n = x.shape[1]
    both = jnp.dot(ah, jnp.concatenate([xh, xl], axis=1), preferred_element_type=f32)
    return both[:, :n] + both[:, n:] + jnp.dot(al, xh, preferred_element_type=f32)


def small_dot(a, x):
    return jnp.dot(a, x, precision=highest, preferred_element_type=f32)


def face_of(state, e, face):
    if face == 0 or face == 1:
        start = 48 * face
        return jnp.concatenate([state[e, pl.ds(64 * v + start, 16)] for v in range(NVAR)], axis=0)
    if face >= 4:
        return state[e, pl.ds(3 * (face - 4), 80, stride=4)]
    half = 8 * (face - 2)
    first = jnp.concatenate([state[e, pl.ds(32 * m + half, 8)] for m in range(10)], axis=0)
    second = jnp.concatenate([state[e, pl.ds(32 * m + 16 + half, 8)] for m in range(10)], axis=0)
    low = lax.broadcasted_iota(jnp.int32, first.shape, 0) % 8 < 4
    if face == 2:
        return jnp.where(low, first, pltpu.roll(second, 4, 0))
    return jnp.where(low, pltpu.roll(first, 76, 0), second)


def link(ids, nbr, slots, e, face):
    g = nbr[e, face]
    owner = lax.div(g, slots)
    here = jnp.logical_and(g >= 0, owner == ids[2])
    away = jnp.logical_and(g >= 0, owner != ids[2])
    return here, away, jnp.maximum(lax.rem(g, slots), 0)


def crossing(ids, nbr, slots, face):
    found, slot = False, 0
    for e in range(slots):
        _, away, _ = link(ids, nbr, slots, e, face)
        found = jnp.logical_or(found, away)
        slot = jnp.where(away, e, slot)
    return found, slot


def swap_of(ids, face):
    return lax.rem(face % 2 + ids[face // 2] % 2 + 1, 2)


def arrived(ids, ys, f):
    a = 2 * (f // 2)
    return jnp.where(swap_of(ids, f) == 0, ys[a][...], ys[a + 1][...])


def fill_sends(ids, nbr, slots, sends, part_of):
    leaving = []
    for f in range(4):
        t = part_of(0, f)
        for e in range(1, slots):
            _, away, _ = link(ids, nbr, slots, e, f)
            t = jnp.where(away, part_of(e, f), t)
        leaving.append(t)
    for axis in range(2):
        low, high = leaving[2 * axis], leaving[2 * axis + 1]
        first = swap_of(ids, 2 * axis) == 0
        sends[2 * axis][...] = jnp.where(first, low, high)
        sends[2 * axis + 1][...] = jnp.where(first, high, low)


def fill_traces(ids, nbr, state, sends):
    fill_sends(ids, nbr, state.shape[0], sends, lambda e, f: face_of(state, e, f))


def first_kernel(ids, nbr, counts, rhs, inverses, v, *sends):
    for e in range(rhs.shape[0]):
        live = jnp.where(e < counts[0], rhs[e], 0.0)
        v[e] = damping * dot(inverses[e], live)
    fill_traces(ids, nbr, v, sends)


def local_residual(ids, nbr, rhs_of, state, blocks, lifts, coef, out, traces):
    slots = state.shape[0]
    for e in range(slots):
        for f in range(6):
            traces[f * slots + e] = face_of(state, e, f)
    for e in range(slots):
        near = []
        for f in range(6):
            here, _, s = link(ids, nbr, slots, e, f)
            t = traces[(f ^ 1) * slots + s] * coef[e, pl.ds(80 * f, 80)]
            near.append(jnp.where(here, t, 0.0))
        near = jnp.concatenate(near, axis=0)
        out[e] = rhs_of(e) - dot(blocks[e], state[e]) - dot(lifts(), near)


def lay_out(lifts_t, coefs, lh, ll, fh, fl, coef):
    faces, nface, nf = lifts_t.shape
    slots = coef.shape[0]
    whole = jnp.concatenate([lifts_t[f] for f in range(faces)], axis=0).T
    lh[...], ll[...] = split(whole)
    for f in range(4):
        fh[f], fl[f] = split(lifts_t[f].T)
    turned = coefs[...].T
    for e in range(slots):
        for f in range(faces):
            column = turned[:, f * slots + e : f * slots + e + 1]
            coef[e, nface * f : nface * (f + 1)] = jnp.broadcast_to(column, (nface, coef.shape[2]))


def first_local_kernel(
    ids, nbr, counts, state, lifts_t, coefs, blocks, rhs, out, lh, ll, fh, fl, coef, traces
):
    lay_out(lifts_t, coefs, lh, ll, fh, fl, coef)

    def rhs_of(e):
        return jnp.where(e < counts[0], rhs[e], 0.0)

    local_residual(
        ids, nbr, rhs_of, state, blocks, lambda: (lh[...], ll[...]), coef, out, traces
    )


def local_kernel(ids, nbr, counts, state, lh, ll, blocks, coef, rhs, out, traces):
    def rhs_of(e):
        return jnp.where(e < counts[0], rhs[e], 0.0)

    local_residual(ids, nbr, rhs_of, state, blocks, lambda: (lh[...], ll[...]), coef, out, traces)


def add_remote(ids, nbr, arrival, fh, fl, coef, out):
    slots = out.shape[0]
    for f in range(4):
        found, slot = crossing(ids, nbr, slots, f)
        t = arrival(f) * coef[slot, pl.ds(80 * f, 80)]
        out[slot] = out[slot] - dot((fh[f], fl[f]), jnp.where(found, t, 0.0))


def sweep_kernel(ids, nbr, y0, y1, y2, y3, res, state, fh, fl, coef, inverses, v, *rest):
    sends, work = rest[:-1], rest[-1]
    work[...] = res[...]
    add_remote(ids, nbr, functools.partial(arrived, ids, (y0, y1, y2, y3)), fh, fl, coef, work)
    for e in range(work.shape[0]):
        value = state[e] + damping * dot(inverses[e], work[e])
        if sends:
            v[e] = value
        else:
            v[0][e] = value
            v[1][e].start()
    if sends:
        fill_traces(ids, nbr, v, sends)


def restrict_kernel(ids, nbr, y0, y1, y2, y3, res, fh, fl, coef, restrict, inverses, r, rhs, w, *sends):
    r[...] = res[...]
    add_remote(ids, nbr, functools.partial(arrived, ids, (y0, y1, y2, y3)), fh, fl, coef, r)
    slots = r.shape[0]
    for e in range(slots):
        rhs[e] = 0.25 * dot(restrict[...], r[e])
        w[e] = damping * dot(inverses[e], rhs[e])
    fill_sends(ids, nbr, slots, sends, lambda e, f: w[e])


def prolong_kernel(ids, nbr, r, state, w, lh, ll, blocks, coef, prolong, out, corrected, traces, correction):
    slots = state.shape[0]
    for e in range(slots):
        correction[e] = dot(prolong[...], w[e])
        corrected[e] = state[e] + correction[e]
    local_residual(
        ids, nbr, lambda e: r[e], correction, blocks, lambda: (lh[...], ll[...]), coef, out, traces
    )


def post_kernel(
    ids, nbr, y0, y1, y2, y3, res, state, face_prolong, fh, fl, coef, inverses, v, *rest
):
    sends, work = rest[:-1], rest[-1]
    work[...] = res[...]
    ys = (y0, y1, y2, y3)
    add_remote(ids, nbr, lambda f: dot(face_prolong[f ^ 1], arrived(ids, ys, f)), fh, fl, coef, work)
    for e in range(work.shape[0]):
        v[e] = state[e] + damping * dot(inverses[e], work[e])
    fill_traces(ids, nbr, v, sends)


def coarse_setup_kernel(ids, nbr, lifts_t, coefs, inverses, hot_t, lifts, coef, remote):
    faces = lifts_t.shape[0]
    slots, nc, _ = inverses.shape
    turned = coefs[...].T
    wide = [small_dot(hot_t[f], lifts_t[f]) for f in range(faces)]
    lifts[...] = jnp.concatenate(wide, axis=0).T
    for f in range(faces):
        spread = small_dot(hot_t[f], turned)
        for e in range(slots):
            column = spread[:, f * slots + e : f * slots + e + 1]
            coef[e, nc * f : nc * (f + 1)] = jnp.broadcast_to(column, (nc, coef.shape[2]))
    for f in range(4):
        found, slot = crossing(ids, nbr, slots, f)
        scaled = wide[f] * coef[slot, nc * f : nc * (f + 1)][:, :nc]
        product = damping * small_dot(inverses[slot], scaled.T)
        remote[f] = jnp.where(found, product, 0.0)


def coarse_local_kernel(ids, nbr, w, rhs, blocks, inverses, lifts, coef, out):
    slots, nc, columns = w.shape
    near = []
    for e in range(slots):
        parts = []
        for f in range(6):
            here, _, s = link(ids, nbr, slots, e, f)
            parts.append(jnp.where(here, w[s] * coef[e, nc * f : nc * (f + 1)], 0.0))
        near.append(jnp.concatenate(parts, axis=0))
    coupled = dot(lifts[...], jnp.concatenate(near, axis=1))
    for e in range(slots):
        res = rhs[e] - dot(blocks[e], w[e]) - coupled[:, e * columns : (e + 1) * columns]
        out[e] = w[e] + damping * dot(inverses[e], res)


def coarse_sweep_kernel(ids, nbr, y0, y1, y2, y3, local, remote, w, *sends):
    w[...] = local[...]
    slots = w.shape[0]
    ys = (y0, y1, y2, y3)
    parts = [dot(remote[f], arrived(ids, ys, f)) for f in range(4)]
    for f in range(4):
        _, slot = crossing(ids, nbr, slots, f)
        w[slot] = w[slot] - parts[f]
    fill_sends(ids, nbr, slots, sends, lambda e, f: w[e])


def swap(parts):
    got = []
    for i, part in enumerate(parts):
        axis = AXES[i // 2]
        pairs = []
        for a in range(i % 2, lax.axis_size(axis) - 1, 2):
            pairs += [(a, a + 1), (a + 1, a)]
        got.append(lax.ppermute(part, axis, pairs))
    return got


def body(
    right_side,
    fine_blocks,
    fine_inverses,
    fine_lifts,
    fine_coefs,
    coarse_blocks,
    coarse_inverses,
    coarse_lifts,
    coarse_coefs,
    neighbours,
    counts,
):
    slots, nf, columns = right_side.shape
    nface = fine_lifts.shape[2]
    nc = coarse_blocks.shape[1]
    ncf = coarse_lifts.shape[2]
    wide_here, narrow_here = lax.axis_index("wide"), lax.axis_index("narrow")
    ids = jnp.stack([wide_here, narrow_here, wide_here * lax.axis_size("narrow") + narrow_here]).astype(jnp.int32)

    prolong_np = prolong_table(NODE1, NVAR)
    coarse_table = face_rows(2, NVAR)
    fine_table = face_rows(NODE1, NVAR)
    prolong = jnp.asarray(prolong_np)
    restrict = jnp.asarray(np.ascontiguousarray(prolong_np.T))
    face_prolong = jnp.asarray(np.stack([prolong_np[fine_table[f]] for f in range(4)]))
    hot_np = np.zeros((6, nc, ncf), np.float32)
    for f in range(6):
        hot_np[f, coarse_table[f ^ 1], np.arange(ncf)] = 1.0
    hot_t = jnp.asarray(hot_np)

    lifts_t = fine_lifts.transpose(0, 2, 1)
    coefs = fine_coefs.transpose(1, 0, 2).reshape(6 * slots, nface)
    coarse_lifts_t = coarse_lifts.transpose(0, 2, 1)
    coarse_coefs_t = coarse_coefs.transpose(1, 0, 2).reshape(6 * slots, ncf)

    field = ("vmem", (slots, nf, columns), f32)
    faces = [("vmem", (nface, columns), f32)] * 4
    coarse = ("vmem", (slots, nc, columns), f32)
    coarse_sends = [("vmem", (nc, columns), f32)] * 4
    trace_room = ((6 * slots, nface, columns), f32)
    field_room = (field[1], f32)
    block_flops = 3 * 2 * slots * nf * nf * columns
    lift_flops = 3 * 2 * slots * nf * 6 * nface * columns
    where = [("smem", ids), ("smem", neighbours)]
    live = where + [("smem", counts)]

    def vm(*arrays):
        return [("vmem", a) for a in arrays]

    def parts(*arrays):
        return [("parts", a) for a in arrays]

    state, *sends = call(first_kernel, [field] + faces, [], live + parts(right_side, fine_inverses), block_flops)
    got = swap(sends)
    res, lh, ll, fh, fl, coef = call(
        first_local_kernel,
        [field]
        + [("vmem", (nf, 6 * nface), bf16)] * 2
        + [("vmem", (4, nf, nface), bf16)] * 2
        + [("vmem", (slots, 6 * nface, columns), f32)],
        [trace_room],
        live + vm(state, lifts_t, coefs, fine_blocks, right_side),
        block_flops + lift_flops,
    )

    def local(state):
        return call(
            local_kernel, [field], [trace_room],
            live + vm(state, lh, ll, fine_blocks, coef, right_side), block_flops + lift_flops,
        )[0]

    def sweep(got, res, state, last):
        return call(
            sweep_kernel, [("hbm",) + field[1:]] if last else [field] + faces, [field_room],
            where + vm(*got, res, state, fh, fl, coef, fine_inverses), block_flops,
        )

    for i in range(PRE_SWEEPS - 1):
        state, *sends = sweep(got, res, state, False)
        got = swap(sends)
        res = local(state)
    coarse_wide, coarse_coef, coarse_remote = call(
        coarse_setup_kernel,
        [("vmem", (nc, 6 * nc), f32), ("vmem", (slots, 6 * nc, columns), f32), ("vmem", (4, nc, nc), f32)], [],
        where + vm(coarse_lifts_t, coarse_coefs_t, coarse_inverses, hot_t),
    )
    residual, coarse_rhs, w, *sends = call(
        restrict_kernel, [field, coarse, coarse] + coarse_sends, [],
        where + vm(*got, res, fh, fl, coef, restrict, coarse_inverses),
    )
    for _ in range(COARSE_SWEEPS - 1):
        got = swap(sends)
        (w_local,) = call(
            coarse_local_kernel, [coarse], [],
            where + vm(w, coarse_rhs, coarse_blocks, coarse_inverses, coarse_wide, coarse_coef),
        )
        w, *sends = call(
            coarse_sweep_kernel, [coarse] + coarse_sends, [], where + vm(*got, w_local, coarse_remote)
        )
    got = swap(sends)
    res, state = call(
        prolong_kernel, [field, field], [trace_room, field_room],
        where + vm(residual, state, w, lh, ll, fine_blocks, coef, prolong),
        block_flops + lift_flops,
    )
    state, *sends = call(
        post_kernel, [field] + faces, [field_room],
        where + vm(*got, res, state, face_prolong, fh, fl, coef, fine_inverses), block_flops,
    )
    for i in range(POST_SWEEPS - 1):
        got = swap(sends)
        res = local(state)
        state, *sends = sweep(got, res, state, i == POST_SWEEPS - 2)
    return state


def solution(mesh):
    placed = (
        P(AXES, None, None),
        P(AXES, None, None),
        P(AXES, None, None),
        P(),
        P(AXES, None, None),
        P(AXES, None, None),
        P(AXES, None, None),
        P(),
        P(AXES, None, None),
        P(AXES, None),
        P(AXES),
    )
    return jax.shard_map(
        body,
        mesh=mesh,
        in_specs=placed,
        out_specs=P(AXES, None, None),
        check_vma=False,
    )
```

```python
import functools

import jax
import jax.numpy as jnp
import numpy as np
from jax import lax
from jax.experimental import pallas as pl
from jax.experimental.pallas import tpu as pltpu
from jax.sharding import PartitionSpec as P

NVAR = 5
NODE1 = 4
PRE_SWEEPS = 2
POST_SWEEPS = 2
COARSE_SWEEPS = 4
AXES = ("wide", "narrow")
VMEM_LIMIT = 16 * 1024 * 1024
WHOLE_VMEM = 245 * 1024 * 256

damping = 0.8
highest = lax.Precision.HIGHEST
f32, bf16 = jnp.float32, jnp.bfloat16


def prolong_table(node_count, variables):
    points = np.array([-1.0, -1.0 / np.sqrt(5.0), 1.0 / np.sqrt(5.0), 1.0])
    linear = np.stack([(1.0 - points) / 2.0, (1.0 + points) / 2.0], axis=1)
    tensor_hat = (
        linear[:, None, None, :, None, None]
        * linear[None, :, None, None, :, None]
        * linear[None, None, :, None, None, :]
    )
    tensor_hat = tensor_hat.reshape(node_count * node_count * node_count, 8)
    return np.kron(np.eye(variables), tensor_hat).astype(np.float32)


def face_rows(node_count, variables):
    cube = node_count**3
    lattice = np.arange(cube).reshape(node_count, node_count, node_count)
    tables = []
    for face in range(6):
        layer = np.take(lattice, 0 if face % 2 == 0 else node_count - 1, axis=face // 2).reshape(-1)
        tables.append(np.concatenate([layer + v * cube for v in range(variables)]))
    return np.stack(tables)


class Fetched:
    def __init__(self, source, room, sems, base, parts):
        self.room, self.ready = room, set()
        if parts == 1:
            self.copies = [pltpu.make_async_copy(source, room, sems.at[base])]
        else:
            self.copies = [
                pltpu.make_async_copy(source.at[i], room.at[i], sems.at[base + i]) for i in range(parts)
            ]

    def start(self):
        for copy in self.copies:
            copy.start()

    def wait(self, part):
        if part not in self.ready:
            self.ready.add(part)
            self.copies[part].wait()

    def wait_all(self):
        for part in range(len(self.copies)):
            self.wait(part)

    def __getitem__(self, index):
        first = index[0] if isinstance(index, tuple) else index
        if len(self.copies) > 1 and isinstance(first, int):
            self.wait(first)
        else:
            self.wait_all()
        return self.room[index]

    @property
    def shape(self):
        return self.room.shape


def call(kernel, outs, scratch, args, flops=0, limit=VMEM_LIMIT):
    specs, rooms, counts = [], [], []
    for kind, a in args:
        if kind in ("smem", "vmem"):
            specs.append(pl.BlockSpec(memory_space=pltpu.SMEM if kind == "smem" else pltpu.VMEM))
        else:
            specs.append(pl.BlockSpec(memory_space=pltpu.HBM))
            rooms.append(pltpu.VMEM(a.shape, a.dtype))
            counts.append(a.shape[0] if kind == "parts" else 1)
    out_rooms = [pltpu.VMEM(shape, dtype) for kind, shape, dtype in outs if kind == "hbm"]
    out_parts = sum(shape[0] for kind, shape, _ in outs if kind == "hbm")
    n_in, n_out, n_rooms = len(args), len(outs), len(rooms)

    def wrapped(*refs):
        ins, results, rest = refs[:n_in], refs[n_in : n_in + n_out], refs[n_in + n_out :]
        in_rooms, rest = rest[:n_rooms], rest[n_rooms:]
        result_rooms, rest = rest[: len(out_rooms)], rest[len(out_rooms) :]
        sems, rest = rest[0], rest[1:]
        given, base, at = [], 0, 0
        for (kind, _), ref in zip(args, ins):
            if kind in ("smem", "vmem"):
                given.append(ref)
                continue
            item = Fetched(ref, in_rooms[at], sems, base, counts[at])
            base += counts[at]
            at += 1
            given.append(item)
        for item in given:
            if isinstance(item, Fetched):
                item.start()
        leaving, produced, at = [], [], 0
        for (kind, shape, _), ref in zip(outs, results):
            if kind == "vmem":
                produced.append(ref)
                continue
            room = result_rooms[at]
            produced.append((room, [pltpu.make_async_copy(room.at[i], ref.at[i], sems.at[base + i]) for i in range(shape[0])]))
            leaving += produced[-1][1]
            base += shape[0]
            at += 1
        kernel(*given, *produced, *rest)
        for item in given:
            if isinstance(item, Fetched):
                item.wait_all()
        for copy in leaving:
            copy.wait()

    moved = sum(int(np.prod(a.shape)) * a.dtype.itemsize for _, a in args)
    moved += sum(int(np.prod(shape)) * 4 for _, shape, _ in outs)
    return pl.pallas_call(
        wrapped,
        out_shape=[jax.ShapeDtypeStruct(shape, dtype) for _, shape, dtype in outs],
        in_specs=specs,
        out_specs=[pl.BlockSpec(memory_space=pltpu.VMEM if kind == "vmem" else pltpu.HBM) for kind, _, _ in outs],
        scratch_shapes=rooms
        + out_rooms
        + [pltpu.SemaphoreType.DMA((max(sum(counts) + out_parts, 1),))]
        + [pltpu.VMEM(shape, dtype) for shape, dtype in scratch],
        compiler_params=pltpu.CompilerParams(vmem_limit_bytes=limit),
        cost_estimate=pl.CostEstimate(flops=flops, bytes_accessed=moved, transcendentals=0),
    )(*[a for _, a in args])


def split(x):
    high = x.astype(bf16)
    return high, (x - high.astype(f32)).astype(bf16)


def dot(a, x):
    ah, al = a if isinstance(a, tuple) else split(a)
    xh, xl = split(x)
    n = x.shape[1]
    both = jnp.dot(ah, jnp.concatenate([xh, xl], axis=1), preferred_element_type=f32)
    return both[:, :n] + both[:, n:] + jnp.dot(al, xh, preferred_element_type=f32)


def small_dot(a, x):
    return jnp.dot(a, x, precision=highest, preferred_element_type=f32)


def face_of(state, e, face):
    if face == 0 or face == 1:
        start = 48 * face
        return jnp.concatenate([state[e, pl.ds(64 * v + start, 16)] for v in range(NVAR)], axis=0)
    if face >= 4:
        return state[e, pl.ds(3 * (face - 4), 80, stride=4)]
    half = 8 * (face - 2)
    first = jnp.concatenate([state[e, pl.ds(32 * m + half, 8)] for m in range(10)], axis=0)
    second = jnp.concatenate([state[e, pl.ds(32 * m + 16 + half, 8)] for m in range(10)], axis=0)
    low = lax.broadcasted_iota(jnp.int32, first.shape, 0) % 8 < 4
    if face == 2:
        return jnp.where(low, first, pltpu.roll(second, 4, 0))
    return jnp.where(low, pltpu.roll(first, 76, 0), second)


def link(ids, nbr, slots, e, face):
    g = nbr[e, face]
    owner = lax.div(g, slots)
    here = jnp.logical_and(g >= 0, owner == ids[2])
    away = jnp.logical_and(g >= 0, owner != ids[2])
    return here, away, jnp.maximum(lax.rem(g, slots), 0)


def crossing(ids, nbr, slots, face):
    found, slot = False, 0
    for e in range(slots):
        _, away, _ = link(ids, nbr, slots, e, face)
        found = jnp.logical_or(found, away)
        slot = jnp.where(away, e, slot)
    return found, slot


def swap_of(ids, face):
    return lax.rem(face % 2 + ids[face // 2] % 2 + 1, 2)


def arrived(ids, ys, f):
    a = 2 * (f // 2)
    return jnp.where(swap_of(ids, f) == 0, ys[a][...], ys[a + 1][...])


def fill_sends(ids, nbr, slots, sends, part_of):
    leaving = []
    for f in range(4):
        t = part_of(0, f)
        for e in range(1, slots):
            _, away, _ = link(ids, nbr, slots, e, f)
            t = jnp.where(away, part_of(e, f), t)
        leaving.append(t)
    for axis in range(2):
        low, high = leaving[2 * axis], leaving[2 * axis + 1]
        first = swap_of(ids, 2 * axis) == 0
        sends[2 * axis][...] = jnp.where(first, low, high)
        sends[2 * axis + 1][...] = jnp.where(first, high, low)


def fill_traces(ids, nbr, state, sends):
    fill_sends(ids, nbr, state.shape[0], sends, lambda e, f: face_of(state, e, f))


def first_kernel(ids, nbr, counts, rhs, inverses, v, *sends):
    for e in range(rhs.shape[0]):
        live = jnp.where(e < counts[0], rhs[e], 0.0)
        v[e] = damping * dot(inverses[e], live)
    fill_traces(ids, nbr, v, sends)


def local_residual(ids, nbr, rhs_of, state, blocks, lifts, coef, out, traces):
    slots = state.shape[0]
    for e in range(slots):
        for f in range(6):
            traces[f * slots + e] = face_of(state, e, f)
    for e in range(slots):
        near = []
        for f in range(6):
            here, _, s = link(ids, nbr, slots, e, f)
            t = traces[(f ^ 1) * slots + s] * coef[e, pl.ds(80 * f, 80)]
            near.append(jnp.where(here, t, 0.0))
        near = jnp.concatenate(near, axis=0)
        out[e] = rhs_of(e) - dot((blocks[0][e], blocks[1][e]), state[e]) - dot(lifts(), near)


def lay_out(lifts_t, coefs, lh, ll, fh, fl, coef):
    faces, nface, nf = lifts_t.shape
    slots = coef.shape[0]
    whole = jnp.concatenate([lifts_t[f] for f in range(faces)], axis=0).T
    lh[...], ll[...] = split(whole)
    for f in range(4):
        fh[f], fl[f] = split(lifts_t[f].T)
    turned = coefs[...].T
    for e in range(slots):
        for f in range(faces):
            column = turned[:, f * slots + e : f * slots + e + 1]
            coef[e, nface * f : nface * (f + 1)] = jnp.broadcast_to(column, (nface, coef.shape[2]))


def first_local_kernel(
    ids, nbr, counts, state, lifts_t, coefs, blocks, rhs, out, lh, ll, fh, fl, coef, bh, bl, traces
):
    lay_out(lifts_t, coefs, lh, ll, fh, fl, coef)
    for e in range(blocks.shape[0]):
        bh[e], bl[e] = split(blocks[e])

    def rhs_of(e):
        return jnp.where(e < counts[0], rhs[e], 0.0)

    local_residual(
        ids, nbr, rhs_of, state, (bh, bl), lambda: (lh[...], ll[...]), coef, out, traces
    )


def local_kernel(ids, nbr, counts, state, lh, ll, bh, bl, coef, rhs, out, traces):
    def rhs_of(e):
        return jnp.where(e < counts[0], rhs[e], 0.0)

    local_residual(ids, nbr, rhs_of, state, (bh, bl), lambda: (lh[...], ll[...]), coef, out, traces)


def add_remote(ids, nbr, arrival, fh, fl, coef, out):
    slots = out.shape[0]
    for f in range(4):
        found, slot = crossing(ids, nbr, slots, f)
        t = arrival(f) * coef[slot, pl.ds(80 * f, 80)]
        out[slot] = out[slot] - dot((fh[f], fl[f]), jnp.where(found, t, 0.0))


def pre_kernel(ids, nbr, y0, y1, y2, y3, res, state, fh, fl, coef, inverses, v, s0, s1, s2, s3, ih, il, work):
    for e in range(work.shape[0]):
        ih[e], il[e] = split(inverses[e])
    sweep_kernel(ids, nbr, y0, y1, y2, y3, res, state, fh, fl, coef, ih, il, v, s0, s1, s2, s3, work)


def sweep_kernel(ids, nbr, y0, y1, y2, y3, res, state, fh, fl, coef, ih, il, v, *rest):
    sends, work = rest[:-1], rest[-1]
    work[...] = res[...]
    add_remote(ids, nbr, functools.partial(arrived, ids, (y0, y1, y2, y3)), fh, fl, coef, work)
    for e in range(work.shape[0]):
        value = state[e] + damping * dot((ih[e], il[e]), work[e])
        if sends:
            v[e] = value
        else:
            v[0][e] = value
            v[1][e].start()
    if sends:
        fill_traces(ids, nbr, v, sends)


def restrict_kernel(ids, nbr, y0, y1, y2, y3, res, fh, fl, coef, restrict, inverses, r, rhs, w, *sends):
    r[...] = res[...]
    add_remote(ids, nbr, functools.partial(arrived, ids, (y0, y1, y2, y3)), fh, fl, coef, r)
    slots = r.shape[0]
    for e in range(slots):
        rhs[e] = 0.25 * dot(restrict[...], r[e])
        w[e] = damping * dot(inverses[e], rhs[e])
    fill_sends(ids, nbr, slots, sends, lambda e, f: w[e])


def prolong_kernel(ids, nbr, r, state, w, lh, ll, bh, bl, coef, prolong, out, corrected, traces, correction):
    slots = state.shape[0]
    for e in range(slots):
        correction[e] = dot(prolong[...], w[e])
        corrected[e] = state[e] + correction[e]
    local_residual(
        ids, nbr, lambda e: r[e], correction, (bh, bl), lambda: (lh[...], ll[...]), coef, out, traces
    )


def post_kernel(
    ids, nbr, y0, y1, y2, y3, res, state, face_prolong, fh, fl, coef, ih, il, v, *rest
):
    sends, work = rest[:-1], rest[-1]
    work[...] = res[...]
    ys = (y0, y1, y2, y3)
    add_remote(ids, nbr, lambda f: dot(face_prolong[f ^ 1], arrived(ids, ys, f)), fh, fl, coef, work)
    for e in range(work.shape[0]):
        v[e] = state[e] + damping * dot((ih[e], il[e]), work[e])
    fill_traces(ids, nbr, v, sends)


def coarse_setup_kernel(ids, nbr, lifts_t, coefs, inverses, hot_t, lifts, coef, remote):
    faces = lifts_t.shape[0]
    slots, nc, _ = inverses.shape
    turned = coefs[...].T
    wide = [small_dot(hot_t[f], lifts_t[f]) for f in range(faces)]
    lifts[...] = jnp.concatenate(wide, axis=0).T
    for f in range(faces):
        spread = small_dot(hot_t[f], turned)
        for e in range(slots):
            column = spread[:, f * slots + e : f * slots + e + 1]
            coef[e, nc * f : nc * (f + 1)] = jnp.broadcast_to(column, (nc, coef.shape[2]))
    for f in range(4):
        found, slot = crossing(ids, nbr, slots, f)
        scaled = wide[f] * coef[slot, nc * f : nc * (f + 1)][:, :nc]
        product = damping * small_dot(inverses[slot], scaled.T)
        remote[f] = jnp.where(found, product, 0.0)


def coarse_local_kernel(ids, nbr, w, rhs, blocks, inverses, lifts, coef, out):
    slots, nc, columns = w.shape
    near = []
    for e in range(slots):
        parts = []
        for f in range(6):
            here, _, s = link(ids, nbr, slots, e, f)
            parts.append(jnp.where(here, w[s] * coef[e, nc * f : nc * (f + 1)], 0.0))
        near.append(jnp.concatenate(parts, axis=0))
    coupled = dot(lifts[...], jnp.concatenate(near, axis=1))
    for e in range(slots):
        res = rhs[e] - dot(blocks[e], w[e]) - coupled[:, e * columns : (e + 1) * columns]
        out[e] = w[e] + damping * dot(inverses[e], res)


def coarse_sweep_kernel(ids, nbr, y0, y1, y2, y3, local, remote, w, *sends):
    w[...] = local[...]
    slots = w.shape[0]
    ys = (y0, y1, y2, y3)
    parts = [dot(remote[f], arrived(ids, ys, f)) for f in range(4)]
    for f in range(4):
        _, slot = crossing(ids, nbr, slots, f)
        w[slot] = w[slot] - parts[f]
    fill_sends(ids, nbr, slots, sends, lambda e, f: w[e])


def swap(parts):
    got = [None] * len(parts)
    for i in (3, 2, 1, 0):
        axis = AXES[i // 2]
        pairs = []
        for a in range(i % 2, lax.axis_size(axis) - 1, 2):
            pairs += [(a, a + 1), (a + 1, a)]
        got[i] = lax.ppermute(parts[i], axis, pairs)
    return got


def body(
    right_side,
    fine_blocks,
    fine_inverses,
    fine_lifts,
    fine_coefs,
    coarse_blocks,
    coarse_inverses,
    coarse_lifts,
    coarse_coefs,
    neighbours,
    counts,
):
    slots, nf, columns = right_side.shape
    nface = fine_lifts.shape[2]
    nc = coarse_blocks.shape[1]
    ncf = coarse_lifts.shape[2]
    wide_here, narrow_here = lax.axis_index("wide"), lax.axis_index("narrow")
    ids = jnp.stack([wide_here, narrow_here, wide_here * lax.axis_size("narrow") + narrow_here]).astype(jnp.int32)

    prolong_np = prolong_table(NODE1, NVAR)
    coarse_table = face_rows(2, NVAR)
    fine_table = face_rows(NODE1, NVAR)
    prolong = jnp.asarray(prolong_np)
    restrict = jnp.asarray(np.ascontiguousarray(prolong_np.T))
    face_prolong = jnp.asarray(np.stack([prolong_np[fine_table[f]] for f in range(4)]))
    hot_np = np.zeros((6, nc, ncf), np.float32)
    for f in range(6):
        hot_np[f, coarse_table[f ^ 1], np.arange(ncf)] = 1.0
    hot_t = jnp.asarray(hot_np)

    lifts_t = fine_lifts.transpose(0, 2, 1)
    coefs = fine_coefs.transpose(1, 0, 2).reshape(6 * slots, nface)
    coarse_lifts_t = coarse_lifts.transpose(0, 2, 1)
    coarse_coefs_t = coarse_coefs.transpose(1, 0, 2).reshape(6 * slots, ncf)

    field = ("vmem", (slots, nf, columns), f32)
    faces = [("vmem", (nface, columns), f32)] * 4
    coarse = ("vmem", (slots, nc, columns), f32)
    coarse_sends = [("vmem", (nc, columns), f32)] * 4
    trace_room = ((6 * slots, nface, columns), f32)
    field_room = (field[1], f32)
    block_flops = 3 * 2 * slots * nf * nf * columns
    lift_flops = 3 * 2 * slots * nf * 6 * nface * columns
    where = [("smem", ids), ("smem", neighbours)]
    live = where + [("smem", counts)]

    def vm(*arrays):
        return [("vmem", a) for a in arrays]

    def parts(*arrays):
        return [("parts", a) for a in arrays]

    state, *sends = call(first_kernel, [field] + faces, [], live + parts(right_side, fine_inverses), block_flops, WHOLE_VMEM)
    got = swap(sends)
    res, lh, ll, fh, fl, coef, bh, bl = call(
        first_local_kernel,
        [field]
        + [("vmem", (nf, 6 * nface), bf16)] * 2
        + [("vmem", (4, nf, nface), bf16)] * 2
        + [("vmem", (slots, 6 * nface, columns), f32)]
        + [("vmem", (slots, nf, nf), bf16)] * 2,
        [trace_room],
        live + vm(state, lifts_t, coefs, fine_blocks, right_side),
        block_flops + lift_flops,
    )

    def local(state):
        return call(
            local_kernel, [field], [trace_room],
            live + vm(state, lh, ll, bh, bl, coef, right_side), block_flops + lift_flops,
        )[0]

    def sweep(got, res, state, last):
        return call(
            sweep_kernel, [("hbm",) + field[1:]] if last else [field] + faces, [field_room],
            where + vm(*got, res, state, fh, fl, coef, ih, il), block_flops,
        )

    pair = [("vmem", (slots, nf, nf), bf16)] * 2
    state, *sends, ih, il = call(
        pre_kernel, [field] + faces + pair, [field_room],
        where + vm(*got, res, state, fh, fl, coef, fine_inverses), block_flops,
    )
    got = swap(sends)
    res = local(state)
    for i in range(PRE_SWEEPS - 2):
        state, *sends = sweep(got, res, state, False)
        got = swap(sends)
        res = local(state)
    coarse_wide, coarse_coef, coarse_remote = call(
        coarse_setup_kernel,
        [("vmem", (nc, 6 * nc), f32), ("vmem", (slots, 6 * nc, columns), f32), ("vmem", (4, nc, nc), f32)], [],
        where + vm(coarse_lifts_t, coarse_coefs_t, coarse_inverses, hot_t),
    )
    residual, coarse_rhs, w, *sends = call(
        restrict_kernel, [field, coarse, coarse] + coarse_sends, [],
        where + vm(*got, res, fh, fl, coef, restrict, coarse_inverses),
    )
    for _ in range(COARSE_SWEEPS - 1):
        got = swap(sends)
        (w_local,) = call(
            coarse_local_kernel, [coarse], [],
            where + vm(w, coarse_rhs, coarse_blocks, coarse_inverses, coarse_wide, coarse_coef),
        )
        w, *sends = call(
            coarse_sweep_kernel, [coarse] + coarse_sends, [], where + vm(*got, w_local, coarse_remote)
        )
    got = swap(sends)
    res, state = call(
        prolong_kernel, [field, field], [trace_room, field_room],
        where + vm(residual, state, w, lh, ll, bh, bl, coef, prolong),
        block_flops + lift_flops,
    )
    state, *sends = call(
        post_kernel, [field] + faces, [field_room],
        where + vm(*got, res, state, face_prolong, fh, fl, coef, ih, il), block_flops,
    )
    for i in range(POST_SWEEPS - 1):
        got = swap(sends)
        res = local(state)
        state, *sends = sweep(got, res, state, i == POST_SWEEPS - 2)
    return state


def solution(mesh):
    placed = (
        P(AXES, None, None),
        P(AXES, None, None),
        P(AXES, None, None),
        P(),
        P(AXES, None, None),
        P(AXES, None, None),
        P(AXES, None, None),
        P(),
        P(AXES, None, None),
        P(AXES, None),
        P(AXES),
    )
    return jax.shard_map(
        body,
        mesh=mesh,
        in_specs=placed,
        out_specs=P(AXES, None, None),
        check_vma=False,
    )
```

```python
import functools

import jax
import jax.numpy as jnp
import numpy as np
from jax import lax
from jax.experimental import pallas as pl
from jax.experimental.pallas import tpu as pltpu
from jax.sharding import PartitionSpec as P

NVAR = 5
NODE1 = 4
PRE_SWEEPS = 2
POST_SWEEPS = 2
COARSE_SWEEPS = 4
AXES = ("wide", "narrow")
LANES = 128
VMEM_LIMIT = 16 * 1024 * 1024
ORDER = (1, 3, 0, 2)

damping = 0.8
highest = lax.Precision.HIGHEST
f32, bf16 = jnp.float32, jnp.bfloat16


def prolong_table(node_count, variables):
    points = np.array([-1.0, -1.0 / np.sqrt(5.0), 1.0 / np.sqrt(5.0), 1.0])
    linear = np.stack([(1.0 - points) / 2.0, (1.0 + points) / 2.0], axis=1)
    tensor_hat = (
        linear[:, None, None, :, None, None]
        * linear[None, :, None, None, :, None]
        * linear[None, None, :, None, None, :]
    )
    tensor_hat = tensor_hat.reshape(node_count * node_count * node_count, 8)
    return np.kron(np.eye(variables), tensor_hat).astype(np.float32)


def face_rows(node_count, variables):
    cube = node_count**3
    lattice = np.arange(cube).reshape(node_count, node_count, node_count)
    tables = []
    for face in range(6):
        layer = np.take(lattice, 0 if face % 2 == 0 else node_count - 1, axis=face // 2).reshape(-1)
        tables.append(np.concatenate([layer + v * cube for v in range(variables)]))
    return np.stack(tables)


class Fetched:
    def __init__(self, source, room, sems, base, parts):
        self.room, self.ready = room, set()
        if parts == 1:
            self.copies = [pltpu.make_async_copy(source, room, sems.at[base])]
        else:
            self.copies = [
                pltpu.make_async_copy(source.at[i], room.at[i], sems.at[base + i]) for i in range(parts)
            ]

    def start(self):
        for copy in self.copies:
            copy.start()

    def wait(self, part):
        if part not in self.ready:
            self.ready.add(part)
            self.copies[part].wait()

    def wait_all(self):
        for part in range(len(self.copies)):
            self.wait(part)

    def __getitem__(self, index):
        first = index[0] if isinstance(index, tuple) else index
        if len(self.copies) > 1 and isinstance(first, int):
            self.wait(first)
        else:
            self.wait_all()
        return self.room[index]

    @property
    def shape(self):
        return self.room.shape


def call(kernel, outs, scratch, args, flops=0):
    specs, rooms, counts = [], [], []
    for kind, a in args:
        if kind in ("smem", "vmem"):
            specs.append(pl.BlockSpec(memory_space=pltpu.SMEM if kind == "smem" else pltpu.VMEM))
        else:
            specs.append(pl.BlockSpec(memory_space=pltpu.HBM))
            rooms.append(pltpu.VMEM(a.shape, a.dtype))
            counts.append(a.shape[0] if kind == "parts" else 1)
    out_rooms = [pltpu.VMEM(shape, dtype) for kind, shape, dtype in outs if kind == "hbm"]
    out_parts = sum(shape[0] for kind, shape, _ in outs if kind == "hbm")
    n_in, n_out, n_rooms = len(args), len(outs), len(rooms)

    def wrapped(*refs):
        ins, results, rest = refs[:n_in], refs[n_in : n_in + n_out], refs[n_in + n_out :]
        in_rooms, rest = rest[:n_rooms], rest[n_rooms:]
        result_rooms, rest = rest[: len(out_rooms)], rest[len(out_rooms) :]
        sems, rest = rest[0], rest[1:]
        given, base, at = [], 0, 0
        for (kind, _), ref in zip(args, ins):
            if kind in ("smem", "vmem"):
                given.append(ref)
                continue
            item = Fetched(ref, in_rooms[at], sems, base, counts[at])
            base += counts[at]
            at += 1
            given.append(item)
        for item in given:
            if isinstance(item, Fetched):
                item.start()
        leaving, produced, at = [], [], 0
        for (kind, shape, _), ref in zip(outs, results):
            if kind == "vmem":
                produced.append(ref)
                continue
            room = result_rooms[at]
            produced.append((room, [pltpu.make_async_copy(room.at[i], ref.at[i], sems.at[base + i]) for i in range(shape[0])]))
            leaving += produced[-1][1]
            base += shape[0]
            at += 1
        kernel(*given, *produced, *rest)
        for item in given:
            if isinstance(item, Fetched):
                item.wait_all()
        for copy in leaving:
            copy.wait()

    moved = sum(int(np.prod(a.shape)) * a.dtype.itemsize for _, a in args)
    moved += sum(int(np.prod(shape)) * 4 for _, shape, _ in outs)
    return pl.pallas_call(
        wrapped,
        out_shape=[jax.ShapeDtypeStruct(shape, dtype) for _, shape, dtype in outs],
        in_specs=specs,
        out_specs=[pl.BlockSpec(memory_space=pltpu.VMEM if kind == "vmem" else pltpu.HBM) for kind, _, _ in outs],
        scratch_shapes=rooms
        + out_rooms
        + [pltpu.SemaphoreType.DMA((max(sum(counts) + out_parts, 1),))]
        + [pltpu.VMEM(shape, dtype) for shape, dtype in scratch],
        compiler_params=pltpu.CompilerParams(vmem_limit_bytes=VMEM_LIMIT),
        cost_estimate=pl.CostEstimate(flops=flops, bytes_accessed=moved, transcendentals=0),
    )(*[a for _, a in args])


def split(x):
    high = x.astype(bf16)
    return high, (x - high.astype(f32)).astype(bf16)


def pad_rows(x, rows):
    return x if x.shape[0] == rows else jnp.concatenate([x, jnp.zeros((rows - x.shape[0], x.shape[1]), x.dtype)], axis=0)


def stack(a):
    room = -a.shape[1] % LANES
    if room:
        a = jnp.concatenate([a, jnp.zeros((a.shape[0], room), a.dtype)], axis=1)
    return jnp.concatenate(split(a), axis=1)


def stacked_dot(a, x):
    xh, xl = split(x)
    rows = a.shape[1] // 2
    top = pad_rows(jnp.concatenate([xh, xl], axis=1), rows)
    low = pad_rows(jnp.concatenate([xh, jnp.zeros_like(xl)], axis=1), rows)
    both = jnp.dot(a, jnp.concatenate([top, low], axis=0), preferred_element_type=f32)
    return both[:, : x.shape[1]] + both[:, x.shape[1] :]


def dot(a, x):
    ah, al = a if isinstance(a, tuple) else split(a)
    xh, xl = split(x)
    n = x.shape[1]
    both = jnp.dot(ah, jnp.concatenate([xh, xl], axis=1), preferred_element_type=f32)
    return both[:, :n] + both[:, n:] + jnp.dot(al, xh, preferred_element_type=f32)


def small_dot(a, x):
    return jnp.dot(a, x, precision=highest, preferred_element_type=f32)


def face_of(state, e, face):
    if face == 0 or face == 1:
        start = 48 * face
        return jnp.concatenate([state[e, pl.ds(64 * v + start, 16)] for v in range(NVAR)], axis=0)
    if face >= 4:
        return state[e, pl.ds(3 * (face - 4), 80, stride=4)]
    half = 8 * (face - 2)
    first = jnp.concatenate([state[e, pl.ds(32 * m + half, 8)] for m in range(10)], axis=0)
    second = jnp.concatenate([state[e, pl.ds(32 * m + 16 + half, 8)] for m in range(10)], axis=0)
    low = lax.broadcasted_iota(jnp.int32, first.shape, 0) % 8 < 4
    if face == 2:
        return jnp.where(low, first, pltpu.roll(second, 4, 0))
    return jnp.where(low, pltpu.roll(first, 76, 0), second)


def link(ids, nbr, slots, e, face):
    g = nbr[e, face]
    owner = lax.div(g, slots)
    here = jnp.logical_and(g >= 0, owner == ids[2])
    away = jnp.logical_and(g >= 0, owner != ids[2])
    return here, away, jnp.maximum(lax.rem(g, slots), 0)


def crossing(ids, nbr, slots, face):
    found, slot = False, 0
    for e in range(slots):
        _, away, _ = link(ids, nbr, slots, e, face)
        found = jnp.logical_or(found, away)
        slot = jnp.where(away, e, slot)
    return found, slot


def swap_of(ids, face):
    return lax.rem(face % 2 + ids[face // 2] % 2 + 1, 2)


def arrived(ids, ys, f):
    near, far = (ys[ORDER.index(2 * (f // 2) + i)] for i in range(2))
    return jnp.where(swap_of(ids, f) == 0, near[...], far[...])


def fill_sends(ids, nbr, slots, sends, part_of):
    leaving = []
    for f in range(4):
        t = part_of(0, f)
        for e in range(1, slots):
            _, away, _ = link(ids, nbr, slots, e, f)
            t = jnp.where(away, part_of(e, f), t)
        leaving.append(t)
    for axis in range(2):
        low, high = leaving[2 * axis], leaving[2 * axis + 1]
        first = swap_of(ids, 2 * axis) == 0
        sends[2 * axis][...] = jnp.where(first, low, high)
        sends[2 * axis + 1][...] = jnp.where(first, high, low)


def fill_traces(ids, nbr, state, sends):
    fill_sends(ids, nbr, state.shape[0], sends, lambda e, f: face_of(state, e, f))


def first_kernel(ids, nbr, counts, rhs, given, v, s0, s1, s2, s3, inverses):
    sends = (s0, s1, s2, s3)
    for e in range(rhs.shape[0]):
        live = jnp.where(e < counts[0], rhs[e], 0.0)
        inverses[e] = stack(given[e])
        v[e] = damping * stacked_dot(inverses[e], live)
    fill_traces(ids, nbr, v, sends)


def local_residual(ids, nbr, rhs_of, state, blocks, lifts, coef, out, traces):
    slots = state.shape[0]
    for e in range(slots):
        for f in range(6):
            traces[f * slots + e] = face_of(state, e, f)
    near = []
    for e in range(slots):
        parts = []
        for f in range(6):
            here, _, s = link(ids, nbr, slots, e, f)
            t = traces[(f ^ 1) * slots + s] * coef[e, pl.ds(80 * f, 80)]
            parts.append(jnp.where(here, t, 0.0))
        near.append(jnp.concatenate(parts, axis=0))
    coupled = dot(lifts, jnp.concatenate(near, axis=1))
    columns = state.shape[2]
    for e in range(slots):
        out[e] = rhs_of(e) - stacked_dot(blocks[e], state[e]) - coupled[:, e * columns : (e + 1) * columns]


def lay_out(lifts_t, coefs, lh, ll, faces_lifts, coef):
    faces, nface, nf = lifts_t.shape
    slots = coef.shape[0]
    whole = jnp.concatenate([lifts_t[f] for f in range(faces)], axis=0).T
    lh[...], ll[...] = split(whole)
    for f in range(4):
        high = lifts_t[f].astype(bf16).astype(f32)
        faces_lifts[f] = jnp.concatenate([high, lifts_t[f] - high], axis=0).T.astype(bf16)
    turned = coefs[...].T
    for e in range(slots):
        for f in range(faces):
            column = turned[:, f * slots + e : f * slots + e + 1]
            coef[e, nface * f : nface * (f + 1)] = jnp.broadcast_to(column, (nface, coef.shape[2]))


def first_local_kernel(
    ids, nbr, counts, state, lifts_t, coefs, given, rhs, out, lh, ll, face_lifts, coef, blocks, traces
):
    lay_out(lifts_t, coefs, lh, ll, face_lifts, coef)
    for e in range(given.shape[0]):
        blocks[e] = stack(given[e])

    def rhs_of(e):
        return jnp.where(e < counts[0], rhs[e], 0.0)

    local_residual(
        ids, nbr, rhs_of, state, blocks, (lh[...], ll[...]), coef, out, traces
    )


def local_kernel(ids, nbr, counts, state, lh, ll, blocks, coef, rhs, out, traces):
    def rhs_of(e):
        return jnp.where(e < counts[0], rhs[e], 0.0)

    local_residual(ids, nbr, rhs_of, state, blocks, (lh[...], ll[...]), coef, out, traces)


def add_remote(ids, nbr, arrival, face_lifts, coef, out):
    slots = out.shape[0]
    for f in range(4):
        found, slot = crossing(ids, nbr, slots, f)
        t = arrival(f) * coef[slot, pl.ds(80 * f, 80)]
        out[slot] = out[slot] - stacked_dot(face_lifts[f], jnp.where(found, t, 0.0))


def sweep_kernel(ids, nbr, y0, y1, y2, y3, res, state, face_lifts, coef, inverses, v, *rest):
    sends, work = rest[:-1], rest[-1]
    work[...] = res[...]
    add_remote(ids, nbr, functools.partial(arrived, ids, (y0, y1, y2, y3)), face_lifts, coef, work)
    for e in range(work.shape[0]):
        value = state[e] + damping * stacked_dot(inverses[e], work[e])
        if sends:
            v[e] = value
        else:
            v[0][e] = value
            v[1][e].start()
    if sends:
        fill_traces(ids, nbr, v, sends)


def restrict_kernel(ids, nbr, y0, y1, y2, y3, res, face_lifts, coef, restrict, inverses, r, rhs, w, *sends):
    r[...] = res[...]
    add_remote(ids, nbr, functools.partial(arrived, ids, (y0, y1, y2, y3)), face_lifts, coef, r)
    slots = r.shape[0]
    for e in range(slots):
        rhs[e] = 0.25 * dot(restrict[...], r[e])
        w[e] = damping * dot(inverses[e], rhs[e])
    fill_sends(ids, nbr, slots, sends, lambda e, f: w[e])


def prolong_kernel(ids, nbr, r, state, w, lh, ll, blocks, coef, prolong, out, corrected, traces, correction):
    slots = state.shape[0]
    for e in range(slots):
        correction[e] = dot(prolong[...], w[e])
        corrected[e] = state[e] + correction[e]
    local_residual(
        ids, nbr, lambda e: r[e], correction, blocks, (lh[...], ll[...]), coef, out, traces
    )


def post_kernel(
    ids, nbr, y0, y1, y2, y3, res, state, face_prolong, face_lifts, coef, inverses, v, *rest
):
    sends, work = rest[:-1], rest[-1]
    work[...] = res[...]
    ys = (y0, y1, y2, y3)
    add_remote(ids, nbr, lambda f: dot(face_prolong[f ^ 1], arrived(ids, ys, f)), face_lifts, coef, work)
    for e in range(work.shape[0]):
        v[e] = state[e] + damping * stacked_dot(inverses[e], work[e])
    fill_traces(ids, nbr, v, sends)


def coarse_setup_kernel(ids, nbr, lifts_t, coefs, inverses, hot_t, lifts, coef, remote):
    faces = lifts_t.shape[0]
    slots, nc, _ = inverses.shape
    turned = coefs[...].T
    wide = [small_dot(hot_t[f], lifts_t[f]) for f in range(faces)]
    lifts[...] = jnp.concatenate(wide, axis=0).T
    for f in range(faces):
        spread = small_dot(hot_t[f], turned)
        for e in range(slots):
            column = spread[:, f * slots + e : f * slots + e + 1]
            coef[e, nc * f : nc * (f + 1)] = jnp.broadcast_to(column, (nc, coef.shape[2]))
    meets = [crossing(ids, nbr, slots, f) for f in range(4)]
    for e in range(slots):
        scaled = []
        for f, (found, slot) in enumerate(meets):
            part = wide[f] * coef[e, nc * f : nc * (f + 1)][:, :nc]
            scaled.append(jnp.where(jnp.logical_and(found, slot == e), part, 0.0))
        rows = damping * small_dot(inverses[e], jnp.concatenate(scaled, axis=0).T)
        remote[e * nc : (e + 1) * nc] = rows


def coarse_local_kernel(ids, nbr, w, rhs, blocks, inverses, lifts, coef, out):
    slots, nc, columns = w.shape
    near = []
    for e in range(slots):
        parts = []
        for f in range(6):
            here, _, s = link(ids, nbr, slots, e, f)
            parts.append(jnp.where(here, w[s] * coef[e, nc * f : nc * (f + 1)], 0.0))
        near.append(jnp.concatenate(parts, axis=0))
    coupled = dot(lifts[...], jnp.concatenate(near, axis=1))
    for e in range(slots):
        res = rhs[e] - dot(blocks[e], w[e]) - coupled[:, e * columns : (e + 1) * columns]
        out[e] = w[e] + damping * dot(inverses[e], res)


def coarse_sweep_kernel(ids, nbr, y0, y1, y2, y3, local, remote, w, *sends):
    slots = w.shape[0]
    ys = (y0, y1, y2, y3)
    far = dot(remote[...], jnp.concatenate([arrived(ids, ys, f) for f in range(4)], axis=0))
    for e in range(slots):
        w[e] = local[e] - far[e * w.shape[1] : (e + 1) * w.shape[1]]
    fill_sends(ids, nbr, slots, sends, lambda e, f: w[e])


def swap(parts):
    got = []
    for i in ORDER:
        axis = AXES[i // 2]
        pairs = []
        for a in range(i % 2, lax.axis_size(axis) - 1, 2):
            pairs += [(a, a + 1), (a + 1, a)]
        got.append(lax.ppermute(parts[i], axis, pairs))
    return got


def body(
    right_side,
    fine_blocks,
    fine_inverses,
    fine_lifts,
    fine_coefs,
    coarse_blocks,
    coarse_inverses,
    coarse_lifts,
    coarse_coefs,
    neighbours,
    counts,
):
    slots, nf, columns = right_side.shape
    nface = fine_lifts.shape[2]
    nc = coarse_blocks.shape[1]
    ncf = coarse_lifts.shape[2]
    wide_here, narrow_here = lax.axis_index("wide"), lax.axis_index("narrow")
    ids = jnp.stack([wide_here, narrow_here, wide_here * lax.axis_size("narrow") + narrow_here]).astype(jnp.int32)

    prolong_np = prolong_table(NODE1, NVAR)
    coarse_table = face_rows(2, NVAR)
    fine_table = face_rows(NODE1, NVAR)
    prolong = jnp.asarray(prolong_np)
    restrict = jnp.asarray(np.ascontiguousarray(prolong_np.T))
    face_prolong = jnp.asarray(np.stack([prolong_np[fine_table[f]] for f in range(4)]))
    hot_np = np.zeros((6, nc, ncf), np.float32)
    for f in range(6):
        hot_np[f, coarse_table[f ^ 1], np.arange(ncf)] = 1.0
    hot_t = jnp.asarray(hot_np)

    lifts_t = fine_lifts.transpose(0, 2, 1)
    coefs = fine_coefs.transpose(1, 0, 2).reshape(6 * slots, nface)
    coarse_lifts_t = coarse_lifts.transpose(0, 2, 1)
    coarse_coefs_t = coarse_coefs.transpose(1, 0, 2).reshape(6 * slots, ncf)

    field = ("vmem", (slots, nf, columns), f32)
    faces = [("vmem", (nface, columns), f32)] * 4
    coarse = ("vmem", (slots, nc, columns), f32)
    coarse_sends = [("vmem", (nc, columns), f32)] * 4
    trace_room = ((6 * slots, nface, columns), f32)
    field_room = (field[1], f32)
    block_flops = 3 * 2 * slots * nf * nf * columns
    lift_flops = 3 * 2 * slots * nf * 6 * nface * columns
    where = [("smem", ids), ("smem", neighbours)]
    live = where + [("smem", counts)]

    def vm(*arrays):
        return [("vmem", a) for a in arrays]

    def parts(*arrays):
        return [("parts", a) for a in arrays]

    wide = 2 * (nf + -nf % LANES)
    matrix = ("vmem", (slots, nf, wide), bf16)
    state, *sends, inverses = call(first_kernel, [field] + faces + [matrix], [], live + vm(right_side, fine_inverses), block_flops)
    got = swap(sends)
    res, lh, ll, face_lifts, coef, blocks = call(
        first_local_kernel,
        [field]
        + [("vmem", (nf, 6 * nface), bf16)] * 2
        + [("vmem", (4, nf, 2 * nface), bf16), ("vmem", (slots, 6 * nface, columns), f32), matrix],
        [trace_room],
        live + vm(state, lifts_t, coefs, fine_blocks, right_side),
        block_flops + lift_flops,
    )

    def local(state):
        return call(
            local_kernel, [field], [trace_room],
            live + vm(state, lh, ll, blocks, coef, right_side), block_flops + lift_flops,
        )[0]

    def sweep(got, res, state, last):
        return call(
            sweep_kernel, [("hbm",) + field[1:]] if last else [field] + faces, [field_room],
            where + vm(*got, res, state, face_lifts, coef, inverses), block_flops,
        )

    for i in range(PRE_SWEEPS - 1):
        state, *sends = sweep(got, res, state, False)
        got = swap(sends)
        res = local(state)
    coarse_wide, coarse_coef, coarse_remote = call(
        coarse_setup_kernel,
        [("vmem", (nc, 6 * nc), f32), ("vmem", (slots, 6 * nc, columns), f32), ("vmem", (slots * nc, 4 * nc), f32)], [],
        where + vm(coarse_lifts_t, coarse_coefs_t, coarse_inverses, hot_t),
    )
    residual, coarse_rhs, w, *sends = call(
        restrict_kernel, [field, coarse, coarse] + coarse_sends, [],
        where + vm(*got, res, face_lifts, coef, restrict, coarse_inverses),
    )
    for _ in range(COARSE_SWEEPS - 1):
        got = swap(sends)
        (w_local,) = call(
            coarse_local_kernel, [coarse], [],
            where + vm(w, coarse_rhs, coarse_blocks, coarse_inverses, coarse_wide, coarse_coef),
        )
        w, *sends = call(
            coarse_sweep_kernel, [coarse] + coarse_sends, [], where + vm(*got, w_local, coarse_remote)
        )
    got = swap(sends)
    res, state = call(
        prolong_kernel, [field, field], [trace_room, field_room],
        where + vm(residual, state, w, lh, ll, blocks, coef, prolong),
        block_flops + lift_flops,
    )
    state, *sends = call(
        post_kernel, [field] + faces, [field_room],
        where + vm(*got, res, state, face_prolong, face_lifts, coef, inverses), block_flops,
    )
    for i in range(POST_SWEEPS - 1):
        got = swap(sends)
        res = local(state)
        state, *sends = sweep(got, res, state, i == POST_SWEEPS - 2)
    return state


def solution(mesh):
    placed = (
        P(AXES, None, None),
        P(AXES, None, None),
        P(AXES, None, None),
        P(),
        P(AXES, None, None),
        P(AXES, None, None),
        P(AXES, None, None),
        P(),
        P(AXES, None, None),
        P(AXES, None),
        P(AXES),
    )
    return jax.shard_map(
        body,
        mesh=mesh,
        in_specs=placed,
        out_specs=P(AXES, None, None),
        check_vma=False,
    )
```

```python
import functools

import jax
import jax.numpy as jnp
import numpy as np
from jax import lax
from jax.experimental import pallas as pl
from jax.experimental.pallas import tpu as pltpu
from jax.sharding import PartitionSpec as P

NVAR = 5
NODE1 = 4
PRE_SWEEPS = 2
POST_SWEEPS = 2
COARSE_SWEEPS = 4
AXES = ("wide", "narrow")
LANES = 128
VMEM_LIMIT = 16 * 1024 * 1024
ORDER = (0, 1, 2, 3)

damping = 0.8
highest = lax.Precision.HIGHEST
f32, bf16 = jnp.float32, jnp.bfloat16


def prolong_table(node_count, variables):
    points = np.array([-1.0, -1.0 / np.sqrt(5.0), 1.0 / np.sqrt(5.0), 1.0])
    linear = np.stack([(1.0 - points) / 2.0, (1.0 + points) / 2.0], axis=1)
    tensor_hat = (
        linear[:, None, None, :, None, None]
        * linear[None, :, None, None, :, None]
        * linear[None, None, :, None, None, :]
    )
    tensor_hat = tensor_hat.reshape(node_count * node_count * node_count, 8)
    return np.kron(np.eye(variables), tensor_hat).astype(np.float32)


def face_rows(node_count, variables):
    cube = node_count**3
    lattice = np.arange(cube).reshape(node_count, node_count, node_count)
    tables = []
    for face in range(6):
        layer = np.take(lattice, 0 if face % 2 == 0 else node_count - 1, axis=face // 2).reshape(-1)
        tables.append(np.concatenate([layer + v * cube for v in range(variables)]))
    return np.stack(tables)


class Fetched:
    def __init__(self, source, room, sems, base, parts):
        self.room, self.ready = room, set()
        if parts == 1:
            self.copies = [pltpu.make_async_copy(source, room, sems.at[base])]
        else:
            self.copies = [
                pltpu.make_async_copy(source.at[i], room.at[i], sems.at[base + i]) for i in range(parts)
            ]

    def start(self):
        for copy in self.copies:
            copy.start()

    def wait(self, part):
        if part not in self.ready:
            self.ready.add(part)
            self.copies[part].wait()

    def wait_all(self):
        for part in range(len(self.copies)):
            self.wait(part)

    def __getitem__(self, index):
        first = index[0] if isinstance(index, tuple) else index
        if len(self.copies) > 1 and isinstance(first, int):
            self.wait(first)
        else:
            self.wait_all()
        return self.room[index]

    @property
    def shape(self):
        return self.room.shape


def call(kernel, outs, scratch, args, flops=0):
    specs, rooms, counts = [], [], []
    for kind, a in args:
        if kind in ("smem", "vmem"):
            specs.append(pl.BlockSpec(memory_space=pltpu.SMEM if kind == "smem" else pltpu.VMEM))
        else:
            specs.append(pl.BlockSpec(memory_space=pltpu.HBM))
            rooms.append(pltpu.VMEM(a.shape, a.dtype))
            counts.append(a.shape[0] if kind == "parts" else 1)
    out_rooms = [pltpu.VMEM(shape, dtype) for kind, shape, dtype in outs if kind == "hbm"]
    out_parts = sum(shape[0] for kind, shape, _ in outs if kind == "hbm")
    n_in, n_out, n_rooms = len(args), len(outs), len(rooms)

    def wrapped(*refs):
        ins, results, rest = refs[:n_in], refs[n_in : n_in + n_out], refs[n_in + n_out :]
        in_rooms, rest = rest[:n_rooms], rest[n_rooms:]
        result_rooms, rest = rest[: len(out_rooms)], rest[len(out_rooms) :]
        sems, rest = rest[0], rest[1:]
        given, base, at = [], 0, 0
        for (kind, _), ref in zip(args, ins):
            if kind in ("smem", "vmem"):
                given.append(ref)
                continue
            item = Fetched(ref, in_rooms[at], sems, base, counts[at])
            base += counts[at]
            at += 1
            given.append(item)
        for item in given:
            if isinstance(item, Fetched):
                item.start()
        leaving, produced, at = [], [], 0
        for (kind, shape, _), ref in zip(outs, results):
            if kind == "vmem":
                produced.append(ref)
                continue
            room = result_rooms[at]
            produced.append((room, [pltpu.make_async_copy(room.at[i], ref.at[i], sems.at[base + i]) for i in range(shape[0])]))
            leaving += produced[-1][1]
            base += shape[0]
            at += 1
        kernel(*given, *produced, *rest)
        for item in given:
            if isinstance(item, Fetched):
                item.wait_all()
        for copy in leaving:
            copy.wait()

    moved = sum(int(np.prod(a.shape)) * a.dtype.itemsize for _, a in args)
    moved += sum(int(np.prod(shape)) * 4 for _, shape, _ in outs)
    return pl.pallas_call(
        wrapped,
        out_shape=[jax.ShapeDtypeStruct(shape, dtype) for _, shape, dtype in outs],
        in_specs=specs,
        out_specs=[pl.BlockSpec(memory_space=pltpu.VMEM if kind == "vmem" else pltpu.HBM) for kind, _, _ in outs],
        scratch_shapes=rooms
        + out_rooms
        + [pltpu.SemaphoreType.DMA((max(sum(counts) + out_parts, 1),))]
        + [pltpu.VMEM(shape, dtype) for shape, dtype in scratch],
        compiler_params=pltpu.CompilerParams(vmem_limit_bytes=VMEM_LIMIT),
        cost_estimate=pl.CostEstimate(flops=flops, bytes_accessed=moved, transcendentals=0),
    )(*[a for _, a in args])


def split(x):
    high = x.astype(bf16)
    return high, (x - high.astype(f32)).astype(bf16)


def pad_rows(x, rows):
    return x if x.shape[0] == rows else jnp.concatenate([x, jnp.zeros((rows - x.shape[0], x.shape[1]), x.dtype)], axis=0)


def stack(a):
    room = -a.shape[1] % LANES
    if room:
        a = jnp.concatenate([a, jnp.zeros((a.shape[0], room), a.dtype)], axis=1)
    return jnp.concatenate(split(a), axis=1)


def stacked_dot(a, x):
    xh, xl = split(x)
    rows = a.shape[1] // 2
    top = pad_rows(jnp.concatenate([xh, xl], axis=1), rows)
    low = pad_rows(jnp.concatenate([xh, jnp.zeros_like(xl)], axis=1), rows)
    both = jnp.dot(a, jnp.concatenate([top, low], axis=0), preferred_element_type=f32)
    return both[:, : x.shape[1]] + both[:, x.shape[1] :]


def dot(a, x):
    ah, al = a if isinstance(a, tuple) else split(a)
    xh, xl = split(x)
    n = x.shape[1]
    both = jnp.dot(ah, jnp.concatenate([xh, xl], axis=1), preferred_element_type=f32)
    return both[:, :n] + both[:, n:] + jnp.dot(al, xh, preferred_element_type=f32)


def small_dot(a, x):
    return jnp.dot(a, x, precision=highest, preferred_element_type=f32)


def face_of(state, e, face):
    if face == 0 or face == 1:
        start = 48 * face
        return jnp.concatenate([state[e, pl.ds(64 * v + start, 16)] for v in range(NVAR)], axis=0)
    if face >= 4:
        return state[e, pl.ds(3 * (face - 4), 80, stride=4)]
    half = 8 * (face - 2)
    first = jnp.concatenate([state[e, pl.ds(32 * m + half, 8)] for m in range(10)], axis=0)
    second = jnp.concatenate([state[e, pl.ds(32 * m + 16 + half, 8)] for m in range(10)], axis=0)
    low = lax.broadcasted_iota(jnp.int32, first.shape, 0) % 8 < 4
    if face == 2:
        return jnp.where(low, first, pltpu.roll(second, 4, 0))
    return jnp.where(low, pltpu.roll(first, 76, 0), second)


def link(ids, nbr, slots, e, face):
    g = nbr[e, face]
    owner = lax.div(g, slots)
    here = jnp.logical_and(g >= 0, owner == ids[2])
    away = jnp.logical_and(g >= 0, owner != ids[2])
    return here, away, jnp.maximum(lax.rem(g, slots), 0)


def crossing(ids, nbr, slots, face):
    found, slot = False, 0
    for e in range(slots):
        _, away, _ = link(ids, nbr, slots, e, face)
        found = jnp.logical_or(found, away)
        slot = jnp.where(away, e, slot)
    return found, slot


def swap_of(ids, face):
    return lax.rem(face % 2 + ids[face // 2] % 2 + 1, 2)


def arrived(ids, ys, f):
    near, far = (ys[ORDER.index(2 * (f // 2) + i)] for i in range(2))
    return jnp.where(swap_of(ids, f) == 0, near[...], far[...])


def fill_sends(ids, nbr, slots, sends, part_of):
    leaving = []
    for f in range(4):
        t = part_of(0, f)
        for e in range(1, slots):
            _, away, _ = link(ids, nbr, slots, e, f)
            t = jnp.where(away, part_of(e, f), t)
        leaving.append(t)
    for axis in range(2):
        low, high = leaving[2 * axis], leaving[2 * axis + 1]
        first = swap_of(ids, 2 * axis) == 0
        sends[2 * axis][...] = jnp.where(first, low, high)
        sends[2 * axis + 1][...] = jnp.where(first, high, low)


def fill_traces(ids, nbr, state, sends):
    fill_sends(ids, nbr, state.shape[0], sends, lambda e, f: face_of(state, e, f))


def first_kernel(ids, nbr, counts, rhs, given, v, s0, s1, s2, s3, inverses):
    sends = (s0, s1, s2, s3)
    for e in range(rhs.shape[0]):
        live = jnp.where(e < counts[0], rhs[e], 0.0)
        inverses[e] = stack(given[e])
        v[e] = damping * stacked_dot(inverses[e], live)
    fill_traces(ids, nbr, v, sends)


def local_residual(ids, nbr, rhs_of, state, blocks, lifts, coef, out, traces):
    slots = state.shape[0]
    for e in range(slots):
        for f in range(6):
            traces[f * slots + e] = face_of(state, e, f)
    near = []
    for e in range(slots):
        parts = []
        for f in range(6):
            here, _, s = link(ids, nbr, slots, e, f)
            t = traces[(f ^ 1) * slots + s] * coef[e, pl.ds(80 * f, 80)]
            parts.append(jnp.where(here, t, 0.0))
        near.append(jnp.concatenate(parts, axis=0))
    coupled = dot(lifts, jnp.concatenate(near, axis=1))
    columns = state.shape[2]
    for e in range(slots):
        out[e] = rhs_of(e) - stacked_dot(blocks[e], state[e]) - coupled[:, e * columns : (e + 1) * columns]


def lay_out(lifts_t, coefs, lh, ll, faces_lifts, coef):
    faces, nface, nf = lifts_t.shape
    slots = coef.shape[0]
    whole = jnp.concatenate([lifts_t[f] for f in range(faces)], axis=0).T
    lh[...], ll[...] = split(whole)
    for f in range(4):
        high = lifts_t[f].astype(bf16).astype(f32)
        faces_lifts[f] = jnp.concatenate([high, lifts_t[f] - high], axis=0).T.astype(bf16)
    turned = coefs[...].T
    for e in range(slots):
        for f in range(faces):
            column = turned[:, f * slots + e : f * slots + e + 1]
            coef[e, nface * f : nface * (f + 1)] = jnp.broadcast_to(column, (nface, coef.shape[2]))


def first_local_kernel(
    ids, nbr, counts, state, lifts_t, coefs, given, rhs, out, lh, ll, face_lifts, coef, blocks, traces
):
    lay_out(lifts_t, coefs, lh, ll, face_lifts, coef)
    for e in range(given.shape[0]):
        blocks[e] = stack(given[e])

    def rhs_of(e):
        return jnp.where(e < counts[0], rhs[e], 0.0)

    local_residual(
        ids, nbr, rhs_of, state, blocks, (lh[...], ll[...]), coef, out, traces
    )


def local_kernel(ids, nbr, counts, state, lh, ll, blocks, coef, rhs, out, traces):
    def rhs_of(e):
        return jnp.where(e < counts[0], rhs[e], 0.0)

    local_residual(ids, nbr, rhs_of, state, blocks, (lh[...], ll[...]), coef, out, traces)


def remote_parts(ids, nbr, arrival, face_lifts, coef):
    slots = coef.shape[0]
    parts = []
    for f in range(4):
        found, slot = crossing(ids, nbr, slots, f)
        parts.append((found, slot, stacked_dot(face_lifts[f], arrival(f) * coef[slot, pl.ds(80 * f, 80)])))
    return parts


def less_remote(res, parts, e):
    for found, slot, part in parts:
        res = res - jnp.where(jnp.logical_and(found, slot == e), part, 0.0)
    return res


def sweep_kernel(ids, nbr, y0, y1, y2, y3, res, state, face_lifts, coef, inverses, v, *rest):
    sends = rest
    parts = remote_parts(ids, nbr, functools.partial(arrived, ids, (y0, y1, y2, y3)), face_lifts, coef)
    for e in range(res.shape[0]):
        value = state[e] + damping * stacked_dot(inverses[e], less_remote(res[e], parts, e))
        if sends:
            v[e] = value
        else:
            v[0][e] = value
            v[1][e].start()
    if sends:
        fill_traces(ids, nbr, v, sends)


def restrict_kernel(ids, nbr, y0, y1, y2, y3, res, face_lifts, coef, restrict, inverses, r, rhs, w, *sends):
    parts = remote_parts(ids, nbr, functools.partial(arrived, ids, (y0, y1, y2, y3)), face_lifts, coef)
    slots = r.shape[0]
    for e in range(slots):
        left = less_remote(res[e], parts, e)
        r[e] = left
        rhs[e] = 0.25 * dot(restrict[...], left)
        w[e] = damping * dot(inverses[e], rhs[e])
    fill_sends(ids, nbr, slots, sends, lambda e, f: w[e])


def prolong_kernel(ids, nbr, r, state, w, lh, ll, blocks, coef, prolong, out, corrected, traces, correction):
    slots = state.shape[0]
    for e in range(slots):
        correction[e] = dot(prolong[...], w[e])
        corrected[e] = state[e] + correction[e]
    local_residual(
        ids, nbr, lambda e: r[e], correction, blocks, (lh[...], ll[...]), coef, out, traces
    )


def post_kernel(
    ids, nbr, y0, y1, y2, y3, res, state, face_prolong, face_lifts, coef, inverses, v, *sends
):
    ys = (y0, y1, y2, y3)
    parts = remote_parts(ids, nbr, lambda f: dot(face_prolong[f ^ 1], arrived(ids, ys, f)), face_lifts, coef)
    for e in range(res.shape[0]):
        v[e] = state[e] + damping * stacked_dot(inverses[e], less_remote(res[e], parts, e))
    fill_traces(ids, nbr, v, sends)


def coarse_setup_kernel(ids, nbr, lifts_t, coefs, inverses, hot_t, lifts, coef, remote):
    faces = lifts_t.shape[0]
    slots, nc, _ = inverses.shape
    turned = coefs[...].T
    wide = [small_dot(hot_t[f], lifts_t[f]) for f in range(faces)]
    lifts[...] = jnp.concatenate(wide, axis=0).T
    for f in range(faces):
        spread = small_dot(hot_t[f], turned)
        for e in range(slots):
            column = spread[:, f * slots + e : f * slots + e + 1]
            coef[e, nc * f : nc * (f + 1)] = jnp.broadcast_to(column, (nc, coef.shape[2]))
    meets = [crossing(ids, nbr, slots, f) for f in range(4)]
    for e in range(slots):
        scaled = []
        for f, (found, slot) in enumerate(meets):
            part = wide[f] * coef[e, nc * f : nc * (f + 1)][:, :nc]
            scaled.append(jnp.where(jnp.logical_and(found, slot == e), part, 0.0))
        rows = damping * small_dot(inverses[e], jnp.concatenate(scaled, axis=0).T)
        remote[e * nc : (e + 1) * nc] = rows


def coarse_local_kernel(ids, nbr, w, rhs, blocks, inverses, lifts, coef, out):
    slots, nc, columns = w.shape
    near = []
    for e in range(slots):
        parts = []
        for f in range(6):
            here, _, s = link(ids, nbr, slots, e, f)
            parts.append(jnp.where(here, w[s] * coef[e, nc * f : nc * (f + 1)], 0.0))
        near.append(jnp.concatenate(parts, axis=0))
    coupled = dot(lifts[...], jnp.concatenate(near, axis=1))
    for e in range(slots):
        res = rhs[e] - dot(blocks[e], w[e]) - coupled[:, e * columns : (e + 1) * columns]
        out[e] = w[e] + damping * dot(inverses[e], res)


def coarse_sweep_kernel(ids, nbr, y0, y1, y2, y3, local, remote, w, *sends):
    slots = w.shape[0]
    ys = (y0, y1, y2, y3)
    far = dot(remote[...], jnp.concatenate([arrived(ids, ys, f) for f in range(4)], axis=0))
    for e in range(slots):
        w[e] = local[e] - far[e * w.shape[1] : (e + 1) * w.shape[1]]
    fill_sends(ids, nbr, slots, sends, lambda e, f: w[e])


def swap(parts):
    got = []
    for i in ORDER:
        axis = AXES[i // 2]
        pairs = []
        for a in range(i % 2, lax.axis_size(axis) - 1, 2):
            pairs += [(a, a + 1), (a + 1, a)]
        got.append(lax.ppermute(parts[i], axis, pairs))
    return got


def body(
    right_side,
    fine_blocks,
    fine_inverses,
    fine_lifts,
    fine_coefs,
    coarse_blocks,
    coarse_inverses,
    coarse_lifts,
    coarse_coefs,
    neighbours,
    counts,
):
    slots, nf, columns = right_side.shape
    nface = fine_lifts.shape[2]
    nc = coarse_blocks.shape[1]
    ncf = coarse_lifts.shape[2]
    wide_here, narrow_here = lax.axis_index("wide"), lax.axis_index("narrow")
    ids = jnp.stack([wide_here, narrow_here, wide_here * lax.axis_size("narrow") + narrow_here]).astype(jnp.int32)

    prolong_np = prolong_table(NODE1, NVAR)
    coarse_table = face_rows(2, NVAR)
    fine_table = face_rows(NODE1, NVAR)
    prolong = jnp.asarray(prolong_np)
    restrict = jnp.asarray(np.ascontiguousarray(prolong_np.T))
    face_prolong = jnp.asarray(np.stack([prolong_np[fine_table[f]] for f in range(4)]))
    hot_np = np.zeros((6, nc, ncf), np.float32)
    for f in range(6):
        hot_np[f, coarse_table[f ^ 1], np.arange(ncf)] = 1.0
    hot_t = jnp.asarray(hot_np)

    lifts_t = fine_lifts.transpose(0, 2, 1)
    coefs = fine_coefs.transpose(1, 0, 2).reshape(6 * slots, nface)
    coarse_lifts_t = coarse_lifts.transpose(0, 2, 1)
    coarse_coefs_t = coarse_coefs.transpose(1, 0, 2).reshape(6 * slots, ncf)

    field = ("vmem", (slots, nf, columns), f32)
    faces = [("vmem", (nface, columns), f32)] * 4
    coarse = ("vmem", (slots, nc, columns), f32)
    coarse_sends = [("vmem", (nc, columns), f32)] * 4
    trace_room = ((6 * slots, nface, columns), f32)
    field_room = (field[1], f32)
    block_flops = 3 * 2 * slots * nf * nf * columns
    lift_flops = 3 * 2 * slots * nf * 6 * nface * columns
    where = [("smem", ids), ("smem", neighbours)]
    live = where + [("smem", counts)]

    def vm(*arrays):
        return [("vmem", a) for a in arrays]

    def parts(*arrays):
        return [("parts", a) for a in arrays]

    wide = 2 * (nf + -nf % LANES)
    matrix = ("vmem", (slots, nf, wide), bf16)
    state, *sends, inverses = call(first_kernel, [field] + faces + [matrix], [], live + vm(right_side, fine_inverses), block_flops)
    got = swap(sends)
    res, lh, ll, face_lifts, coef, blocks = call(
        first_local_kernel,
        [field]
        + [("vmem", (nf, 6 * nface), bf16)] * 2
        + [("vmem", (4, nf, 2 * nface), bf16), ("vmem", (slots, 6 * nface, columns), f32), matrix],
        [trace_room],
        live + vm(state, lifts_t, coefs, fine_blocks, right_side),
        block_flops + lift_flops,
    )

    def local(state):
        return call(
            local_kernel, [field], [trace_room],
            live + vm(state, lh, ll, blocks, coef, right_side), block_flops + lift_flops,
        )[0]

    def sweep(got, res, state, last):
        return call(
            sweep_kernel, [("hbm",) + field[1:]] if last else [field] + faces, [],
            where + vm(*got, res, state, face_lifts, coef, inverses), block_flops,
        )

    for i in range(PRE_SWEEPS - 1):
        state, *sends = sweep(got, res, state, False)
        got = swap(sends)
        res = local(state)
    coarse_wide, coarse_coef, coarse_remote = call(
        coarse_setup_kernel,
        [("vmem", (nc, 6 * nc), f32), ("vmem", (slots, 6 * nc, columns), f32), ("vmem", (slots * nc, 4 * nc), f32)], [],
        where + vm(coarse_lifts_t, coarse_coefs_t, coarse_inverses, hot_t),
    )
    residual, coarse_rhs, w, *sends = call(
        restrict_kernel, [field, coarse, coarse] + coarse_sends, [],
        where + vm(*got, res, face_lifts, coef, restrict, coarse_inverses),
    )
    for _ in range(COARSE_SWEEPS - 1):
        got = swap(sends)
        (w_local,) = call(
            coarse_local_kernel, [coarse], [],
            where + vm(w, coarse_rhs, coarse_blocks, coarse_inverses, coarse_wide, coarse_coef),
        )
        w, *sends = call(
            coarse_sweep_kernel, [coarse] + coarse_sends, [], where + vm(*got, w_local, coarse_remote)
        )
    got = swap(sends)
    res, state = call(
        prolong_kernel, [field, field], [trace_room, field_room],
        where + vm(residual, state, w, lh, ll, blocks, coef, prolong),
        block_flops + lift_flops,
    )
    state, *sends = call(
        post_kernel, [field] + faces, [],
        where + vm(*got, res, state, face_prolong, face_lifts, coef, inverses), block_flops,
    )
    for i in range(POST_SWEEPS - 1):
        got = swap(sends)
        res = local(state)
        state, *sends = sweep(got, res, state, i == POST_SWEEPS - 2)
    return state


def solution(mesh):
    placed = (
        P(AXES, None, None),
        P(AXES, None, None),
        P(AXES, None, None),
        P(),
        P(AXES, None, None),
        P(AXES, None, None),
        P(AXES, None, None),
        P(),
        P(AXES, None, None),
        P(AXES, None),
        P(AXES),
    )
    return jax.shard_map(
        body,
        mesh=mesh,
        in_specs=placed,
        out_specs=P(AXES, None, None),
        check_vma=False,
    )
```

```python
import functools

import jax
import jax.numpy as jnp
import numpy as np
from jax import lax
from jax.experimental import pallas as pl
from jax.experimental.pallas import tpu as pltpu
from jax.sharding import PartitionSpec as P

NVAR = 5
NODE1 = 4
PRE_SWEEPS = 2
POST_SWEEPS = 2
COARSE_SWEEPS = 4
AXES = ("wide", "narrow")
LANES = 128
VMEM_LIMIT = 16 * 1024 * 1024

damping = 0.8
highest = lax.Precision.HIGHEST
f32, bf16 = jnp.float32, jnp.bfloat16


def prolong_table(node_count, variables):
    points = np.array([-1.0, -1.0 / np.sqrt(5.0), 1.0 / np.sqrt(5.0), 1.0])
    linear = np.stack([(1.0 - points) / 2.0, (1.0 + points) / 2.0], axis=1)
    tensor_hat = (
        linear[:, None, None, :, None, None]
        * linear[None, :, None, None, :, None]
        * linear[None, None, :, None, None, :]
    )
    tensor_hat = tensor_hat.reshape(node_count * node_count * node_count, 8)
    return np.kron(np.eye(variables), tensor_hat).astype(np.float32)


def face_rows(node_count, variables):
    cube = node_count**3
    lattice = np.arange(cube).reshape(node_count, node_count, node_count)
    tables = []
    for face in range(6):
        layer = np.take(lattice, 0 if face % 2 == 0 else node_count - 1, axis=face // 2).reshape(-1)
        tables.append(np.concatenate([layer + v * cube for v in range(variables)]))
    return np.stack(tables)


class Fetched:
    def __init__(self, source, room, sems, base, parts):
        self.room, self.ready = room, set()
        if parts == 1:
            self.copies = [pltpu.make_async_copy(source, room, sems.at[base])]
        else:
            self.copies = [
                pltpu.make_async_copy(source.at[i], room.at[i], sems.at[base + i]) for i in range(parts)
            ]

    def start(self):
        for copy in self.copies:
            copy.start()

    def wait(self, part):
        if part not in self.ready:
            self.ready.add(part)
            self.copies[part].wait()

    def wait_all(self):
        for part in range(len(self.copies)):
            self.wait(part)

    def __getitem__(self, index):
        first = index[0] if isinstance(index, tuple) else index
        if len(self.copies) > 1 and isinstance(first, int):
            self.wait(first)
        else:
            self.wait_all()
        return self.room[index]

    @property
    def shape(self):
        return self.room.shape


def call(kernel, outs, scratch, args, flops=0):
    specs, rooms, counts = [], [], []
    for kind, a in args:
        if kind in ("smem", "vmem"):
            specs.append(pl.BlockSpec(memory_space=pltpu.SMEM if kind == "smem" else pltpu.VMEM))
        else:
            specs.append(pl.BlockSpec(memory_space=pltpu.HBM))
            rooms.append(pltpu.VMEM(a.shape, a.dtype))
            counts.append(a.shape[0] if kind == "parts" else 1)
    out_rooms = [pltpu.VMEM(shape, dtype) for kind, shape, dtype in outs if kind == "hbm"]
    out_parts = sum(shape[0] for kind, shape, _ in outs if kind == "hbm")
    n_in, n_out, n_rooms = len(args), len(outs), len(rooms)

    def wrapped(*refs):
        ins, results, rest = refs[:n_in], refs[n_in : n_in + n_out], refs[n_in + n_out :]
        in_rooms, rest = rest[:n_rooms], rest[n_rooms:]
        result_rooms, rest = rest[: len(out_rooms)], rest[len(out_rooms) :]
        sems, rest = rest[0], rest[1:]
        given, base, at = [], 0, 0
        for (kind, _), ref in zip(args, ins):
            if kind in ("smem", "vmem"):
                given.append(ref)
                continue
            item = Fetched(ref, in_rooms[at], sems, base, counts[at])
            base += counts[at]
            at += 1
            given.append(item)
        for item in given:
            if isinstance(item, Fetched):
                item.start()
        leaving, produced, at = [], [], 0
        for (kind, shape, _), ref in zip(outs, results):
            if kind == "vmem":
                produced.append(ref)
                continue
            room = result_rooms[at]
            produced.append((room, [pltpu.make_async_copy(room.at[i], ref.at[i], sems.at[base + i]) for i in range(shape[0])]))
            leaving += produced[-1][1]
            base += shape[0]
            at += 1
        kernel(*given, *produced, *rest)
        for item in given:
            if isinstance(item, Fetched):
                item.wait_all()
        for copy in leaving:
            copy.wait()

    moved = sum(int(np.prod(a.shape)) * a.dtype.itemsize for _, a in args)
    moved += sum(int(np.prod(shape)) * 4 for _, shape, _ in outs)
    return pl.pallas_call(
        wrapped,
        out_shape=[jax.ShapeDtypeStruct(shape, dtype) for _, shape, dtype in outs],
        in_specs=specs,
        out_specs=[pl.BlockSpec(memory_space=pltpu.VMEM if kind == "vmem" else pltpu.HBM) for kind, _, _ in outs],
        scratch_shapes=rooms
        + out_rooms
        + [pltpu.SemaphoreType.DMA((max(sum(counts) + out_parts, 1),))]
        + [pltpu.VMEM(shape, dtype) for shape, dtype in scratch],
        compiler_params=pltpu.CompilerParams(vmem_limit_bytes=VMEM_LIMIT),
        cost_estimate=pl.CostEstimate(flops=flops, bytes_accessed=moved, transcendentals=0),
    )(*[a for _, a in args])


def split(x):
    high = x.astype(bf16)
    return high, (x - high.astype(f32)).astype(bf16)


def pad_rows(x, rows):
    return x if x.shape[0] == rows else jnp.concatenate([x, jnp.zeros((rows - x.shape[0], x.shape[1]), x.dtype)], axis=0)


def stack(a):
    room = -a.shape[1] % LANES
    if room:
        a = jnp.concatenate([a, jnp.zeros((a.shape[0], room), a.dtype)], axis=1)
    return jnp.concatenate(split(a), axis=1)


def stacked_dot(a, x):
    xh, xl = split(x)
    rows = a.shape[1] // 2
    top = pad_rows(jnp.concatenate([xh, xl], axis=1), rows)
    low = pad_rows(jnp.concatenate([xh, jnp.zeros_like(xl)], axis=1), rows)
    both = jnp.dot(a, jnp.concatenate([top, low], axis=0), preferred_element_type=f32)
    return both[:, : x.shape[1]] + both[:, x.shape[1] :]


def dot(a, x):
    ah, al = a if isinstance(a, tuple) else split(a)
    xh, xl = split(x)
    n = x.shape[1]
    both = jnp.dot(ah, jnp.concatenate([xh, xl], axis=1), preferred_element_type=f32)
    return both[:, :n] + both[:, n:] + jnp.dot(al, xh, preferred_element_type=f32)


def small_dot(a, x):
    return jnp.dot(a, x, precision=highest, preferred_element_type=f32)


def face_of(state, e, face):
    if face == 0 or face == 1:
        start = 48 * face
        return jnp.concatenate([state[e, pl.ds(64 * v + start, 16)] for v in range(NVAR)], axis=0)
    if face >= 4:
        return state[e, pl.ds(3 * (face - 4), 80, stride=4)]
    half = 8 * (face - 2)
    first = jnp.concatenate([state[e, pl.ds(32 * m + half, 8)] for m in range(10)], axis=0)
    second = jnp.concatenate([state[e, pl.ds(32 * m + 16 + half, 8)] for m in range(10)], axis=0)
    low = lax.broadcasted_iota(jnp.int32, first.shape, 0) % 8 < 4
    if face == 2:
        return jnp.where(low, first, pltpu.roll(second, 4, 0))
    return jnp.where(low, pltpu.roll(first, 76, 0), second)


def link(ids, nbr, slots, e, face):
    g = nbr[e, face]
    owner = lax.div(g, slots)
    here = jnp.logical_and(g >= 0, owner == ids[2])
    away = jnp.logical_and(g >= 0, owner != ids[2])
    return here, away, jnp.maximum(lax.rem(g, slots), 0)


def crossing(ids, nbr, slots, face):
    found, slot = False, 0
    for e in range(slots):
        _, away, _ = link(ids, nbr, slots, e, face)
        found = jnp.logical_or(found, away)
        slot = jnp.where(away, e, slot)
    return found, slot


def swap_of(ids, face):
    return lax.rem(face % 2 + ids[face // 2] % 2 + 1, 2)


def fill_masks(ids, nbr, slots, masks):
    for i in range(4):
        for side in range(2):
            f = 2 * (i // 2) + side
            for e in range(slots):
                _, away, _ = link(ids, nbr, slots, e, f)
                value = jnp.where(jnp.logical_and(away, swap_of(ids, f) == i % 2), 1.0, 0.0)
                masks[(2 * i + side) * slots + e] = jnp.full(masks.shape[1:], value, f32)


def masked(mask, x):
    return (x.reshape(-1, *mask.shape) * mask).reshape(x.shape)


def meets(masks, slots, i, e):
    return masks[2 * i * slots + e] + masks[(2 * i + 1) * slots + e]


def fill_traces(masks, state, sends):
    slots = state.shape[0]
    traces = [[face_of(state, e, f) for e in range(slots)] for f in range(4)]
    for i in range(4):
        terms = [
            masked(masks[(2 * i + side) * slots + e], traces[2 * (i // 2) + side][e])
            for side in range(2)
            for e in range(slots)
        ]
        sends[i][...] = sum(terms[1:], terms[0])


def fill_elements(masks, w, sends):
    slots = w.shape[0]
    for i in range(4):
        terms = [masked(meets(masks, slots, i, e), w[e]) for e in range(slots)]
        sends[i][...] = sum(terms[1:], terms[0])


def first_kernel(ids, nbr, counts, rhs, given, v, s0, s1, s2, s3, inverses, masks):
    fill_masks(ids, nbr, rhs.shape[0], masks)
    for e in range(rhs.shape[0]):
        live = jnp.where(e < counts[0], rhs[e], 0.0)
        inverses[e] = stack(given[e])
        v[e] = damping * stacked_dot(inverses[e], live)
    fill_traces(masks, v, (s0, s1, s2, s3))


def local_residual(ids, nbr, rhs_of, state, blocks, lifts, coef, out, traces):
    slots = state.shape[0]
    for e in range(slots):
        for f in range(6):
            traces[f * slots + e] = face_of(state, e, f)
    near = []
    for e in range(slots):
        parts = []
        for f in range(6):
            here, _, s = link(ids, nbr, slots, e, f)
            t = traces[(f ^ 1) * slots + s] * coef[e, pl.ds(80 * f, 80)]
            parts.append(jnp.where(here, t, 0.0))
        near.append(jnp.concatenate(parts, axis=0))
    coupled = dot(lifts, jnp.concatenate(near, axis=1))
    columns = state.shape[2]
    for e in range(slots):
        out[e] = rhs_of(e) - stacked_dot(blocks[e], state[e]) - coupled[:, e * columns : (e + 1) * columns]


def lay_out(ids, nbr, lifts_t, coefs, lh, ll, far_lifts, coef):
    faces, nface, nf = lifts_t.shape
    slots = coef.shape[0]
    whole = jnp.concatenate([lifts_t[f] for f in range(faces)], axis=0).T
    lh[...], ll[...] = split(whole)
    turned = coefs[...].T
    for e in range(slots):
        for f in range(faces):
            column = turned[:, f * slots + e : f * slots + e + 1]
            coef[e, nface * f : nface * (f + 1)] = jnp.broadcast_to(column, (nface, coef.shape[2]))
    for i in range(4):
        low = 2 * (i // 2)
        first = swap_of(ids, low) == i % 2
        scaled = []
        for f in (low, low + 1):
            _, slot = crossing(ids, nbr, slots, f)
            scaled.append(lifts_t[f] * coef[slot, pl.ds(nface * f, nface)][:, :1])
        scaled = jnp.where(first, scaled[0], scaled[1])
        high = scaled.astype(bf16).astype(f32)
        far_lifts[i] = jnp.concatenate([high, scaled - high], axis=0).T.astype(bf16)


def first_local_kernel(
    ids, nbr, counts, state, lifts_t, coefs, given, rhs, out, lh, ll, far_lifts, coef, blocks, traces
):
    lay_out(ids, nbr, lifts_t, coefs, lh, ll, far_lifts, coef)
    for e in range(given.shape[0]):
        blocks[e] = stack(given[e])

    def rhs_of(e):
        return jnp.where(e < counts[0], rhs[e], 0.0)

    local_residual(
        ids, nbr, rhs_of, state, blocks, (lh[...], ll[...]), coef, out, traces
    )


def local_kernel(ids, nbr, counts, state, lh, ll, blocks, coef, rhs, out, traces):
    def rhs_of(e):
        return jnp.where(e < counts[0], rhs[e], 0.0)

    local_residual(ids, nbr, rhs_of, state, blocks, (lh[...], ll[...]), coef, out, traces)


def less_remote(masks, res, parts, e):
    slots = masks.shape[0] // 8
    for i, part in enumerate(parts):
        res = res - masked(meets(masks, slots, i, e), part)
    return res


def sweep_kernel(masks, y0, y1, y2, y3, res, state, far_lifts, inverses, v, *sends):
    parts = [stacked_dot(far_lifts[i], y[...]) for i, y in enumerate((y0, y1, y2, y3))]
    for e in range(res.shape[0]):
        value = state[e] + damping * stacked_dot(inverses[e], less_remote(masks, res[e], parts, e))
        if sends:
            v[e] = value
        else:
            v[0][e] = value
            v[1][e].start()
    if sends:
        fill_traces(masks, v, sends)


def restrict_kernel(masks, y0, y1, y2, y3, res, far_lifts, restrict, inverses, r, rhs, w, *sends):
    parts = [stacked_dot(far_lifts[i], y[...]) for i, y in enumerate((y0, y1, y2, y3))]
    for e in range(r.shape[0]):
        left = less_remote(masks, res[e], parts, e)
        r[e] = left
        rhs[e] = 0.25 * dot(restrict[...], left)
        w[e] = damping * dot(inverses[e], rhs[e])
    fill_elements(masks, w, sends)


def prolong_kernel(ids, nbr, r, state, w, lh, ll, blocks, coef, prolong, out, corrected, traces, correction):
    slots = state.shape[0]
    for e in range(slots):
        correction[e] = dot(prolong[...], w[e])
        corrected[e] = state[e] + correction[e]
    local_residual(
        ids, nbr, lambda e: r[e], correction, blocks, (lh[...], ll[...]), coef, out, traces
    )


def post_kernel(masks, y0, y1, y2, y3, res, state, far_prolong, far_lifts, inverses, v, *sends):
    parts = [
        stacked_dot(far_lifts[i], dot(far_prolong[i], y[...])) for i, y in enumerate((y0, y1, y2, y3))
    ]
    for e in range(res.shape[0]):
        v[e] = state[e] + damping * stacked_dot(inverses[e], less_remote(masks, res[e], parts, e))
    fill_traces(masks, v, sends)


def coarse_setup_kernel(
    ids, nbr, lifts_t, coefs, inverses, hot_t, face_prolong, lifts, coef, remote, far_prolong
):
    faces = lifts_t.shape[0]
    slots, nc, _ = inverses.shape
    turned = coefs[...].T
    wide = [small_dot(hot_t[f], lifts_t[f]) for f in range(faces)]
    lifts[...] = jnp.concatenate(wide, axis=0).T
    for f in range(faces):
        spread = small_dot(hot_t[f], turned)
        for e in range(slots):
            column = spread[:, f * slots + e : f * slots + e + 1]
            coef[e, nc * f : nc * (f + 1)] = jnp.broadcast_to(column, (nc, coef.shape[2]))
    firsts = [swap_of(ids, 2 * (i // 2)) == i % 2 for i in range(4)]
    ends = [crossing(ids, nbr, slots, f) for f in range(4)]
    for i, first in enumerate(firsts):
        low = 2 * (i // 2)
        far_prolong[i] = jnp.where(first, face_prolong[low + 1], face_prolong[low])
    for e in range(slots):
        scaled = []
        for f, (found, slot) in enumerate(ends):
            part = wide[f] * coef[e, nc * f : nc * (f + 1)][:, :nc]
            scaled.append(jnp.where(jnp.logical_and(found, slot == e), part, 0.0))
        ordered = []
        for i, first in enumerate(firsts):
            low = 2 * (i // 2)
            ordered.append(jnp.where(first, scaled[low], scaled[low + 1]))
        rows = damping * small_dot(inverses[e], jnp.concatenate(ordered, axis=0).T)
        remote[e * nc : (e + 1) * nc] = rows


def coarse_local_kernel(ids, nbr, w, rhs, blocks, inverses, lifts, coef, out):
    slots, nc, columns = w.shape
    near = []
    for e in range(slots):
        parts = []
        for f in range(6):
            here, _, s = link(ids, nbr, slots, e, f)
            parts.append(jnp.where(here, w[s] * coef[e, nc * f : nc * (f + 1)], 0.0))
        near.append(jnp.concatenate(parts, axis=0))
    coupled = dot(lifts[...], jnp.concatenate(near, axis=1))
    for e in range(slots):
        res = rhs[e] - dot(blocks[e], w[e]) - coupled[:, e * columns : (e + 1) * columns]
        out[e] = w[e] + damping * dot(inverses[e], res)


def coarse_sweep_kernel(masks, y0, y1, y2, y3, local, remote, w, *sends):
    slots, nc, _ = w.shape
    far = dot(remote[...], jnp.concatenate([y[...] for y in (y0, y1, y2, y3)], axis=0))
    for e in range(slots):
        w[e] = local[e] - far[e * nc : (e + 1) * nc]
    fill_elements(masks, w, sends)


def swap(parts):
    got = []
    for i in range(len(parts)):
        axis = AXES[i // 2]
        pairs = []
        for a in range(i % 2, lax.axis_size(axis) - 1, 2):
            pairs += [(a, a + 1), (a + 1, a)]
        got.append(lax.ppermute(parts[i], axis, pairs))
    return got


def body(
    right_side,
    fine_blocks,
    fine_inverses,
    fine_lifts,
    fine_coefs,
    coarse_blocks,
    coarse_inverses,
    coarse_lifts,
    coarse_coefs,
    neighbours,
    counts,
):
    slots, nf, columns = right_side.shape
    nface = fine_lifts.shape[2]
    nc = coarse_blocks.shape[1]
    ncf = coarse_lifts.shape[2]
    wide_here, narrow_here = lax.axis_index("wide"), lax.axis_index("narrow")
    ids = jnp.stack([wide_here, narrow_here, wide_here * lax.axis_size("narrow") + narrow_here]).astype(jnp.int32)

    prolong_np = prolong_table(NODE1, NVAR)
    coarse_table = face_rows(2, NVAR)
    fine_table = face_rows(NODE1, NVAR)
    prolong = jnp.asarray(prolong_np)
    restrict = jnp.asarray(np.ascontiguousarray(prolong_np.T))
    face_prolong = jnp.asarray(np.stack([prolong_np[fine_table[f]] for f in range(4)]))
    hot_np = np.zeros((6, nc, ncf), np.float32)
    for f in range(6):
        hot_np[f, coarse_table[f ^ 1], np.arange(ncf)] = 1.0
    hot_t = jnp.asarray(hot_np)

    lifts_t = fine_lifts.transpose(0, 2, 1)
    coefs = fine_coefs.transpose(1, 0, 2).reshape(6 * slots, nface)
    coarse_lifts_t = coarse_lifts.transpose(0, 2, 1)
    coarse_coefs_t = coarse_coefs.transpose(1, 0, 2).reshape(6 * slots, ncf)

    field = ("vmem", (slots, nf, columns), f32)
    faces = [("vmem", (nface, columns), f32)] * 4
    coarse = ("vmem", (slots, nc, columns), f32)
    coarse_sends = [("vmem", (nc, columns), f32)] * 4
    trace_room = ((6 * slots, nface, columns), f32)
    field_room = (field[1], f32)
    block_flops = 3 * 2 * slots * nf * nf * columns
    lift_flops = 3 * 2 * slots * nf * 6 * nface * columns
    where = [("smem", ids), ("smem", neighbours)]
    live = where + [("smem", counts)]

    def vm(*arrays):
        return [("vmem", a) for a in arrays]

    def parts(*arrays):
        return [("parts", a) for a in arrays]

    wide = 2 * (nf + -nf % LANES)
    matrix = ("vmem", (slots, nf, wide), bf16)
    mask_tiles = ("vmem", (8 * slots, 8, columns), f32)
    state, *sends, inverses, masks = call(first_kernel, [field] + faces + [matrix, mask_tiles], [], live + vm(right_side, fine_inverses), block_flops)
    got = swap(sends)
    res, lh, ll, far_lifts, coef, blocks = call(
        first_local_kernel,
        [field]
        + [("vmem", (nf, 6 * nface), bf16)] * 2
        + [("vmem", (4, nf, 2 * nface), bf16), ("vmem", (slots, 6 * nface, columns), f32), matrix],
        [trace_room],
        live + vm(state, lifts_t, coefs, fine_blocks, right_side),
        block_flops + lift_flops,
    )

    def local(state):
        return call(
            local_kernel, [field], [trace_room],
            live + vm(state, lh, ll, blocks, coef, right_side), block_flops + lift_flops,
        )[0]

    def sweep(got, res, state, last):
        return call(
            sweep_kernel, [("hbm",) + field[1:]] if last else [field] + faces, [],
            vm(masks, *got, res, state, far_lifts, inverses), block_flops,
        )

    for i in range(PRE_SWEEPS - 1):
        state, *sends = sweep(got, res, state, False)
        got = swap(sends)
        res = local(state)
    coarse_wide, coarse_coef, coarse_remote, far_prolong = call(
        coarse_setup_kernel,
        [("vmem", (nc, 6 * nc), f32), ("vmem", (slots, 6 * nc, columns), f32), ("vmem", (slots * nc, 4 * nc), f32),
         ("vmem", (4, nface, nc), f32)], [],
        where + vm(coarse_lifts_t, coarse_coefs_t, coarse_inverses, hot_t, face_prolong),
    )
    residual, coarse_rhs, w, *sends = call(
        restrict_kernel, [field, coarse, coarse] + coarse_sends, [],
        vm(masks, *got, res, far_lifts, restrict, coarse_inverses),
    )
    for _ in range(COARSE_SWEEPS - 1):
        got = swap(sends)
        (w_local,) = call(
            coarse_local_kernel, [coarse], [],
            where + vm(w, coarse_rhs, coarse_blocks, coarse_inverses, coarse_wide, coarse_coef),
        )
        w, *sends = call(
            coarse_sweep_kernel, [coarse] + coarse_sends, [], vm(masks, *got, w_local, coarse_remote)
        )
    got = swap(sends)
    res, state = call(
        prolong_kernel, [field, field], [trace_room, field_room],
        where + vm(residual, state, w, lh, ll, blocks, coef, prolong),
        block_flops + lift_flops,
    )
    state, *sends = call(
        post_kernel, [field] + faces, [],
        vm(masks, *got, res, state, far_prolong, far_lifts, inverses), block_flops,
    )
    for i in range(POST_SWEEPS - 1):
        got = swap(sends)
        res = local(state)
        state, *sends = sweep(got, res, state, i == POST_SWEEPS - 2)
    return state


def solution(mesh):
    placed = (
        P(AXES, None, None),
        P(AXES, None, None),
        P(AXES, None, None),
        P(),
        P(AXES, None, None),
        P(AXES, None, None),
        P(AXES, None, None),
        P(),
        P(AXES, None, None),
        P(AXES, None),
        P(AXES),
    )
    return jax.shard_map(
        body,
        mesh=mesh,
        in_specs=placed,
        out_specs=P(AXES, None, None),
        check_vma=False,
    )
```

```python
import functools

import jax
import jax.numpy as jnp
import numpy as np
from jax import lax
from jax.experimental import pallas as pl
from jax.experimental.pallas import tpu as pltpu
from jax.sharding import PartitionSpec as P

NVAR = 5
NODE1 = 4
PRE_SWEEPS = 2
POST_SWEEPS = 2
COARSE_SWEEPS = 4
AXES = ("wide", "narrow")
LANES = 128
VMEM_LIMIT = 16 * 1024 * 1024

damping = 0.8
highest = lax.Precision.HIGHEST
f32, bf16 = jnp.float32, jnp.bfloat16


def prolong_table(node_count, variables):
    points = np.array([-1.0, -1.0 / np.sqrt(5.0), 1.0 / np.sqrt(5.0), 1.0])
    linear = np.stack([(1.0 - points) / 2.0, (1.0 + points) / 2.0], axis=1)
    tensor_hat = (
        linear[:, None, None, :, None, None]
        * linear[None, :, None, None, :, None]
        * linear[None, None, :, None, None, :]
    )
    tensor_hat = tensor_hat.reshape(node_count * node_count * node_count, 8)
    return np.kron(np.eye(variables), tensor_hat).astype(np.float32)


def face_rows(node_count, variables):
    cube = node_count**3
    lattice = np.arange(cube).reshape(node_count, node_count, node_count)
    tables = []
    for face in range(6):
        layer = np.take(lattice, 0 if face % 2 == 0 else node_count - 1, axis=face // 2).reshape(-1)
        tables.append(np.concatenate([layer + v * cube for v in range(variables)]))
    return np.stack(tables)


class Fetched:
    def __init__(self, source, room, sems, base, parts):
        self.room, self.ready = room, set()
        if parts == 1:
            self.copies = [pltpu.make_async_copy(source, room, sems.at[base])]
        else:
            self.copies = [
                pltpu.make_async_copy(source.at[i], room.at[i], sems.at[base + i]) for i in range(parts)
            ]

    def start(self):
        for copy in self.copies:
            copy.start()

    def wait(self, part):
        if part not in self.ready:
            self.ready.add(part)
            self.copies[part].wait()

    def wait_all(self):
        for part in range(len(self.copies)):
            self.wait(part)

    def __getitem__(self, index):
        first = index[0] if isinstance(index, tuple) else index
        if len(self.copies) > 1 and isinstance(first, int):
            self.wait(first)
        else:
            self.wait_all()
        return self.room[index]

    @property
    def shape(self):
        return self.room.shape


def call(kernel, outs, scratch, args, flops=0):
    specs, rooms, counts = [], [], []
    for kind, a in args:
        if kind in ("smem", "vmem"):
            specs.append(pl.BlockSpec(memory_space=pltpu.SMEM if kind == "smem" else pltpu.VMEM))
        else:
            specs.append(pl.BlockSpec(memory_space=pltpu.HBM))
            rooms.append(pltpu.VMEM(a.shape, a.dtype))
            counts.append(a.shape[0] if kind == "parts" else 1)
    out_rooms = [pltpu.VMEM(shape, dtype) for kind, shape, dtype in outs if kind == "hbm"]
    out_parts = sum(shape[0] for kind, shape, _ in outs if kind == "hbm")
    n_in, n_out, n_rooms = len(args), len(outs), len(rooms)

    def wrapped(*refs):
        ins, results, rest = refs[:n_in], refs[n_in : n_in + n_out], refs[n_in + n_out :]
        in_rooms, rest = rest[:n_rooms], rest[n_rooms:]
        result_rooms, rest = rest[: len(out_rooms)], rest[len(out_rooms) :]
        sems, rest = rest[0], rest[1:]
        given, base, at = [], 0, 0
        for (kind, _), ref in zip(args, ins):
            if kind in ("smem", "vmem"):
                given.append(ref)
                continue
            item = Fetched(ref, in_rooms[at], sems, base, counts[at])
            base += counts[at]
            at += 1
            given.append(item)
        for item in given:
            if isinstance(item, Fetched):
                item.start()
        leaving, produced, at = [], [], 0
        for (kind, shape, _), ref in zip(outs, results):
            if kind == "vmem":
                produced.append(ref)
                continue
            room = result_rooms[at]
            produced.append((room, [pltpu.make_async_copy(room.at[i], ref.at[i], sems.at[base + i]) for i in range(shape[0])]))
            leaving += produced[-1][1]
            base += shape[0]
            at += 1
        kernel(*given, *produced, *rest)
        for item in given:
            if isinstance(item, Fetched):
                item.wait_all()
        for copy in leaving:
            copy.wait()

    moved = sum(int(np.prod(a.shape)) * a.dtype.itemsize for _, a in args)
    moved += sum(int(np.prod(shape)) * 4 for _, shape, _ in outs)
    return pl.pallas_call(
        wrapped,
        out_shape=[jax.ShapeDtypeStruct(shape, dtype) for _, shape, dtype in outs],
        in_specs=specs,
        out_specs=[pl.BlockSpec(memory_space=pltpu.VMEM if kind == "vmem" else pltpu.HBM) for kind, _, _ in outs],
        scratch_shapes=rooms
        + out_rooms
        + [pltpu.SemaphoreType.DMA((max(sum(counts) + out_parts, 1),))]
        + [pltpu.VMEM(shape, dtype) for shape, dtype in scratch],
        compiler_params=pltpu.CompilerParams(vmem_limit_bytes=VMEM_LIMIT),
        cost_estimate=pl.CostEstimate(flops=flops, bytes_accessed=moved, transcendentals=0),
    )(*[a for _, a in args])


def split(x):
    high = x.astype(bf16)
    return high, (x - high.astype(f32)).astype(bf16)


def pad_rows(x, rows):
    return x if x.shape[0] == rows else jnp.concatenate([x, jnp.zeros((rows - x.shape[0], x.shape[1]), x.dtype)], axis=0)


def stack(a):
    room = -a.shape[1] % LANES
    if room:
        a = jnp.concatenate([a, jnp.zeros((a.shape[0], room), a.dtype)], axis=1)
    return jnp.concatenate(split(a), axis=1)


def stacked_dot(a, x):
    xh, xl = split(x)
    rows = a.shape[1] // 2
    top = pad_rows(jnp.concatenate([xh, xl], axis=1), rows)
    low = pad_rows(jnp.concatenate([xh, jnp.zeros_like(xl)], axis=1), rows)
    both = jnp.dot(a, jnp.concatenate([top, low], axis=0), preferred_element_type=f32)
    return both[:, : x.shape[1]] + both[:, x.shape[1] :]


def dot(a, x):
    ah, al = a if isinstance(a, tuple) else split(a)
    xh, xl = split(x)
    n = x.shape[1]
    both = jnp.dot(ah, jnp.concatenate([xh, xl], axis=1), preferred_element_type=f32)
    return both[:, :n] + both[:, n:] + jnp.dot(al, xh, preferred_element_type=f32)


def small_dot(a, x):
    return jnp.dot(a, x, precision=highest, preferred_element_type=f32)


def face_of(state, e, face):
    if face == 0 or face == 1:
        start = 48 * face
        return jnp.concatenate([state[e, pl.ds(64 * v + start, 16)] for v in range(NVAR)], axis=0)
    if face >= 4:
        return state[e, pl.ds(3 * (face - 4), 80, stride=4)]
    half = 8 * (face - 2)
    first = jnp.concatenate([state[e, pl.ds(32 * m + half, 8)] for m in range(10)], axis=0)
    second = jnp.concatenate([state[e, pl.ds(32 * m + 16 + half, 8)] for m in range(10)], axis=0)
    low = lax.broadcasted_iota(jnp.int32, first.shape, 0) % 8 < 4
    if face == 2:
        return jnp.where(low, first, pltpu.roll(second, 4, 0))
    return jnp.where(low, pltpu.roll(first, 76, 0), second)


def link(ids, nbr, slots, e, face):
    g = nbr[e, face]
    owner = lax.div(g, slots)
    here = jnp.logical_and(g >= 0, owner == ids[2])
    away = jnp.logical_and(g >= 0, owner != ids[2])
    return here, away, jnp.maximum(lax.rem(g, slots), 0)


def crossing(ids, nbr, slots, face):
    found, slot = False, 0
    for e in range(slots):
        _, away, _ = link(ids, nbr, slots, e, face)
        found = jnp.logical_or(found, away)
        slot = jnp.where(away, e, slot)
    return found, slot


def swap_of(ids, face):
    return lax.rem(face % 2 + ids[face // 2] % 2 + 1, 2)


def fill_masks(ids, nbr, slots, masks):
    for i in range(4):
        for side in range(2):
            f = 2 * (i // 2) + side
            for e in range(slots):
                _, away, _ = link(ids, nbr, slots, e, f)
                value = jnp.where(jnp.logical_and(away, swap_of(ids, f) == i % 2), 1.0, 0.0)
                masks[(2 * i + side) * slots + e] = jnp.full(masks.shape[1:], value, f32)


def masked(mask, x):
    return (x.reshape(-1, *mask.shape) * mask).reshape(x.shape)


def meets(masks, slots, i, e):
    return masks[2 * i * slots + e] + masks[(2 * i + 1) * slots + e]


def fill_traces(masks, state, sends):
    slots = state.shape[0]
    traces = [[face_of(state, e, f) for e in range(slots)] for f in range(4)]
    for i in range(4):
        terms = [
            masked(masks[(2 * i + side) * slots + e], traces[2 * (i // 2) + side][e])
            for side in range(2)
            for e in range(slots)
        ]
        sends[i][...] = sum(terms[1:], terms[0])


def fill_elements(masks, w, sends):
    slots = w.shape[0]
    for i in range(4):
        terms = [masked(meets(masks, slots, i, e), w[e]) for e in range(slots)]
        sends[i][...] = sum(terms[1:], terms[0])


def first_kernel(counts, rhs, given, v, inverses):
    for e in range(rhs.shape[0]):
        live = jnp.where(e < counts[0], rhs[e], 0.0)
        inverses[e] = stack(given[e])
        v[e] = damping * stacked_dot(inverses[e], live)


def send_kernel(ids, nbr, v, s0, s1, s2, s3, masks):
    fill_masks(ids, nbr, v.shape[0], masks)
    fill_traces(masks, v, (s0, s1, s2, s3))


def local_residual(ids, nbr, rhs_of, state, blocks, lifts, coef, out, traces):
    slots = state.shape[0]
    for e in range(slots):
        for f in range(6):
            traces[f * slots + e] = face_of(state, e, f)
    near = []
    for e in range(slots):
        parts = []
        for f in range(6):
            here, _, s = link(ids, nbr, slots, e, f)
            t = traces[(f ^ 1) * slots + s] * coef[e, pl.ds(80 * f, 80)]
            parts.append(jnp.where(here, t, 0.0))
        near.append(jnp.concatenate(parts, axis=0))
    coupled = dot(lifts, jnp.concatenate(near, axis=1))
    columns = state.shape[2]
    for e in range(slots):
        out[e] = rhs_of(e) - stacked_dot(blocks[e], state[e]) - coupled[:, e * columns : (e + 1) * columns]


def lay_out(ids, nbr, lifts_t, coefs, lh, ll, far_lifts, coef):
    faces, nface, nf = lifts_t.shape
    slots = coef.shape[0]
    whole = jnp.concatenate([lifts_t[f] for f in range(faces)], axis=0).T
    lh[...], ll[...] = split(whole)
    turned = coefs[...].T
    for e in range(slots):
        for f in range(faces):
            column = turned[:, f * slots + e : f * slots + e + 1]
            coef[e, nface * f : nface * (f + 1)] = jnp.broadcast_to(column, (nface, coef.shape[2]))
    for i in range(4):
        low = 2 * (i // 2)
        first = swap_of(ids, low) == i % 2
        scaled = []
        for f in (low, low + 1):
            _, slot = crossing(ids, nbr, slots, f)
            scaled.append(lifts_t[f] * coef[slot, pl.ds(nface * f, nface)][:, :1])
        scaled = jnp.where(first, scaled[0], scaled[1])
        high = scaled.astype(bf16).astype(f32)
        far_lifts[i] = jnp.concatenate([high, scaled - high], axis=0).T.astype(bf16)


def first_local_kernel(
    ids, nbr, counts, state, lifts_t, coefs, given, rhs, out, lh, ll, far_lifts, coef, blocks, traces
):
    lay_out(ids, nbr, lifts_t, coefs, lh, ll, far_lifts, coef)
    for e in range(given.shape[0]):
        blocks[e] = stack(given[e])

    def rhs_of(e):
        return jnp.where(e < counts[0], rhs[e], 0.0)

    local_residual(
        ids, nbr, rhs_of, state, blocks, (lh[...], ll[...]), coef, out, traces
    )


def local_kernel(ids, nbr, counts, state, lh, ll, blocks, coef, rhs, out, traces):
    def rhs_of(e):
        return jnp.where(e < counts[0], rhs[e], 0.0)

    local_residual(ids, nbr, rhs_of, state, blocks, (lh[...], ll[...]), coef, out, traces)


def less_remote(masks, res, parts, e):
    slots = masks.shape[0] // 8
    for i, part in enumerate(parts):
        res = res - masked(meets(masks, slots, i, e), part)
    return res


def sweep_kernel(masks, y0, y1, y2, y3, res, state, far_lifts, inverses, v, *sends):
    parts = [stacked_dot(far_lifts[i], y[...]) for i, y in enumerate((y0, y1, y2, y3))]
    for e in range(res.shape[0]):
        value = state[e] + damping * stacked_dot(inverses[e], less_remote(masks, res[e], parts, e))
        if sends:
            v[e] = value
        else:
            v[0][e] = value
            v[1][e].start()
    if sends:
        fill_traces(masks, v, sends)


def restrict_kernel(masks, y0, y1, y2, y3, res, far_lifts, restrict, inverses, _, r, rhs, w, *sends):
    parts = [stacked_dot(far_lifts[i], y[...]) for i, y in enumerate((y0, y1, y2, y3))]
    for e in range(r.shape[0]):
        left = less_remote(masks, res[e], parts, e)
        r[e] = left
        rhs[e] = 0.25 * dot(restrict[...], left)
        w[e] = damping * dot(inverses[e], rhs[e])
    fill_elements(masks, w, sends)


def prolong_kernel(ids, nbr, r, state, w, lh, ll, blocks, coef, prolong, out, corrected, traces, correction):
    slots = state.shape[0]
    for e in range(slots):
        correction[e] = dot(prolong[...], w[e])
        corrected[e] = state[e] + correction[e]
    local_residual(
        ids, nbr, lambda e: r[e], correction, blocks, (lh[...], ll[...]), coef, out, traces
    )


def post_kernel(masks, y0, y1, y2, y3, res, state, far_prolong, inverses, v, *sends):
    parts = [stacked_dot(far_prolong[i], y[...]) for i, y in enumerate((y0, y1, y2, y3))]
    for e in range(res.shape[0]):
        v[e] = state[e] + damping * stacked_dot(inverses[e], less_remote(masks, res[e], parts, e))
    fill_traces(masks, v, sends)


def coarse_lay_out_kernel(lifts_t, coefs, hot_t, _, lifts, coef, wide):
    faces, _, nc = lifts_t.shape
    slots = coef.shape[0]
    turned = coefs[...].T
    for f in range(faces):
        wide[f] = small_dot(hot_t[f], lifts_t[f])
    lifts[...] = jnp.concatenate([wide[f] for f in range(faces)], axis=0).T
    for f in range(faces):
        spread = small_dot(hot_t[f], turned)
        for e in range(slots):
            column = spread[:, f * slots + e : f * slots + e + 1]
            coef[e, nc * f : nc * (f + 1)] = jnp.broadcast_to(column, (nc, coef.shape[2]))


def coarse_remote_kernel(masks, wide, coef, inverses, far_lifts, face_prolong, remote, far_prolong):
    slots, nc, _ = inverses.shape
    for i in range(4):
        total = None
        for side in range(2):
            on = sum(masks[(2 * i + side) * slots + e] for e in range(slots))
            term = masked(on, face_prolong[2 * (i // 2) + 1 - side])
            total = term if total is None else total + term
        far_prolong[i] = jnp.concatenate(split(stacked_dot(far_lifts[i], total)), axis=1)
    for e in range(slots):
        scaled = []
        for i in range(4):
            total = None
            for side in range(2):
                f = 2 * (i // 2) + side
                term = masked(masks[(2 * i + side) * slots + e], coef[e, nc * f : nc * (f + 1)])
                term = wide[f] * term[:, :nc]
                total = term if total is None else total + term
            scaled.append(total)
        rows = damping * small_dot(inverses[e], jnp.concatenate(scaled, axis=0).T)
        remote[e * nc : (e + 1) * nc] = rows


def coarse_local_kernel(ids, nbr, w, rhs, blocks, inverses, lifts, coef, out):
    slots, nc, columns = w.shape
    near = []
    for e in range(slots):
        parts = []
        for f in range(6):
            here, _, s = link(ids, nbr, slots, e, f)
            parts.append(jnp.where(here, w[s] * coef[e, nc * f : nc * (f + 1)], 0.0))
        near.append(jnp.concatenate(parts, axis=0))
    coupled = dot(lifts[...], jnp.concatenate(near, axis=1))
    for e in range(slots):
        res = rhs[e] - dot(blocks[e], w[e]) - coupled[:, e * columns : (e + 1) * columns]
        out[e] = w[e] + damping * dot(inverses[e], res)


def coarse_sweep_kernel(masks, y0, y1, y2, y3, local, remote, w, *sends):
    slots, nc, _ = w.shape
    far = dot(remote[...], jnp.concatenate([y[...] for y in (y0, y1, y2, y3)], axis=0))
    for e in range(slots):
        w[e] = local[e] - far[e * nc : (e + 1) * nc]
    fill_elements(masks, w, sends)


def swap(parts):
    got = []
    for i in range(len(parts)):
        axis = AXES[i // 2]
        pairs = []
        for a in range(i % 2, lax.axis_size(axis) - 1, 2):
            pairs += [(a, a + 1), (a + 1, a)]
        got.append(lax.ppermute(parts[i], axis, pairs))
    return got


def body(
    right_side,
    fine_blocks,
    fine_inverses,
    fine_lifts,
    fine_coefs,
    coarse_blocks,
    coarse_inverses,
    coarse_lifts,
    coarse_coefs,
    neighbours,
    counts,
):
    slots, nf, columns = right_side.shape
    nface = fine_lifts.shape[2]
    nc = coarse_blocks.shape[1]
    ncf = coarse_lifts.shape[2]
    wide_here, narrow_here = lax.axis_index("wide"), lax.axis_index("narrow")
    ids = jnp.stack([wide_here, narrow_here, wide_here * lax.axis_size("narrow") + narrow_here]).astype(jnp.int32)

    prolong_np = prolong_table(NODE1, NVAR)
    coarse_table = face_rows(2, NVAR)
    fine_table = face_rows(NODE1, NVAR)
    prolong = jnp.asarray(prolong_np)
    restrict = jnp.asarray(np.ascontiguousarray(prolong_np.T))
    face_prolong = np.stack([prolong_np[fine_table[f]] for f in range(4)])
    face_prolong = jnp.asarray(np.pad(face_prolong, ((0, 0), (0, 0), (0, LANES - nc))))
    hot_np = np.zeros((6, nc, ncf), np.float32)
    for f in range(6):
        hot_np[f, coarse_table[f ^ 1], np.arange(ncf)] = 1.0
    hot_t = jnp.asarray(hot_np)

    lifts_t = fine_lifts.transpose(0, 2, 1)
    coefs = fine_coefs.transpose(1, 0, 2).reshape(6 * slots, nface)
    coarse_lifts_t = coarse_lifts.transpose(0, 2, 1)
    coarse_coefs_t = coarse_coefs.transpose(1, 0, 2).reshape(6 * slots, ncf)

    field = ("vmem", (slots, nf, columns), f32)
    faces = [("vmem", (nface, columns), f32)] * 4
    coarse = ("vmem", (slots, nc, columns), f32)
    coarse_sends = [("vmem", (nc, columns), f32)] * 4
    trace_room = ((6 * slots, nface, columns), f32)
    field_room = (field[1], f32)
    block_flops = 3 * 2 * slots * nf * nf * columns
    lift_flops = 3 * 2 * slots * nf * 6 * nface * columns
    where = [("smem", ids), ("smem", neighbours)]
    live = where + [("smem", counts)]

    def vm(*arrays):
        return [("vmem", a) for a in arrays]

    def parts(*arrays):
        return [("parts", a) for a in arrays]

    wide = 2 * (nf + -nf % LANES)
    matrix = ("vmem", (slots, nf, wide), bf16)
    mask_tiles = ("vmem", (8 * slots, 8, columns), f32)
    state, inverses = call(
        first_kernel, [field, matrix], [], [("smem", counts)] + vm(right_side, fine_inverses), 8 * block_flops
    )
    *sends, masks = call(send_kernel, faces + [mask_tiles], [], where + vm(state))
    got = swap(sends)
    res, lh, ll, far_lifts, coef, blocks = call(
        first_local_kernel,
        [field]
        + [("vmem", (nf, 6 * nface), bf16)] * 2
        + [("vmem", (4, nf, 2 * nface), bf16), ("vmem", (slots, 6 * nface, columns), f32), matrix],
        [trace_room],
        live + vm(state, lifts_t, coefs, fine_blocks, right_side),
        block_flops + lift_flops,
    )

    def local(state):
        return call(
            local_kernel, [field], [trace_room],
            live + vm(state, lh, ll, blocks, coef, right_side), block_flops + lift_flops,
        )[0]

    def sweep(got, res, state, last):
        return call(
            sweep_kernel, [("hbm",) + field[1:]] if last else [field] + faces, [],
            vm(masks, *got, res, state, far_lifts, inverses), block_flops,
        )

    for i in range(PRE_SWEEPS - 1):
        state, *sends = sweep(got, res, state, False)
        got = swap(sends)
        res = local(state)
    coarse_wide, coarse_coef, coarse_faces = call(
        coarse_lay_out_kernel,
        [("vmem", (nc, 6 * nc), f32), ("vmem", (slots, 6 * nc, columns), f32), ("vmem", (6, nc, nc), f32)], [],
        vm(coarse_lifts_t, coarse_coefs_t, hot_t, state),
    )
    residual, coarse_rhs, w, *sends = call(
        restrict_kernel, [field, coarse, coarse] + coarse_sends, [],
        vm(masks, *got, res, far_lifts, restrict, coarse_inverses, coarse_wide),
    )
    coarse_remote, far_prolong = call(
        coarse_remote_kernel,
        [("vmem", (slots * nc, 4 * nc), f32), ("vmem", (4, nf, 2 * LANES), bf16)], [],
        vm(masks, coarse_faces, coarse_coef, coarse_inverses, far_lifts, face_prolong),
    )
    for _ in range(COARSE_SWEEPS - 1):
        got = swap(sends)
        (w_local,) = call(
            coarse_local_kernel, [coarse], [],
            where + vm(w, coarse_rhs, coarse_blocks, coarse_inverses, coarse_wide, coarse_coef),
        )
        w, *sends = call(
            coarse_sweep_kernel, [coarse] + coarse_sends, [], vm(masks, *got, w_local, coarse_remote)
        )
    got = swap(sends)
    res, state = call(
        prolong_kernel, [field, field], [trace_room, field_room],
        where + vm(residual, state, w, lh, ll, blocks, coef, prolong),
        block_flops + lift_flops,
    )
    state, *sends = call(
        post_kernel, [field] + faces, [],
        vm(masks, *got, res, state, far_prolong, inverses), block_flops,
    )
    for i in range(POST_SWEEPS - 1):
        got = swap(sends)
        res = local(state)
        state, *sends = sweep(got, res, state, i == POST_SWEEPS - 2)
    return state


def solution(mesh):
    placed = (
        P(AXES, None, None),
        P(AXES, None, None),
        P(AXES, None, None),
        P(),
        P(AXES, None, None),
        P(AXES, None, None),
        P(AXES, None, None),
        P(),
        P(AXES, None, None),
        P(AXES, None),
        P(AXES),
    )
    return jax.shard_map(
        body,
        mesh=mesh,
        in_specs=placed,
        out_specs=P(AXES, None, None),
        check_vma=False,
    )
```

```python
import functools

import jax
import jax.numpy as jnp
import numpy as np
from jax import lax
from jax.experimental import pallas as pl
from jax.experimental.pallas import tpu as pltpu
from jax.sharding import PartitionSpec as P

NVAR = 5
NODE1 = 4
PRE_SWEEPS = 2
POST_SWEEPS = 2
COARSE_SWEEPS = 4
AXES = ("wide", "narrow")
LANES = 128
VMEM_LIMIT = 16 * 1024 * 1024

damping = 0.8
highest = lax.Precision.HIGHEST
f32, bf16 = jnp.float32, jnp.bfloat16


def prolong_table(node_count, variables):
    points = np.array([-1.0, -1.0 / np.sqrt(5.0), 1.0 / np.sqrt(5.0), 1.0])
    linear = np.stack([(1.0 - points) / 2.0, (1.0 + points) / 2.0], axis=1)
    tensor_hat = (
        linear[:, None, None, :, None, None]
        * linear[None, :, None, None, :, None]
        * linear[None, None, :, None, None, :]
    )
    tensor_hat = tensor_hat.reshape(node_count * node_count * node_count, 8)
    return np.kron(np.eye(variables), tensor_hat).astype(np.float32)


def face_rows(node_count, variables):
    cube = node_count**3
    lattice = np.arange(cube).reshape(node_count, node_count, node_count)
    tables = []
    for face in range(6):
        layer = np.take(lattice, 0 if face % 2 == 0 else node_count - 1, axis=face // 2).reshape(-1)
        tables.append(np.concatenate([layer + v * cube for v in range(variables)]))
    return np.stack(tables)


class Late:
    def __init__(self, source, room, sem):
        self.room, self.copy, self.ready = room, pltpu.make_async_copy(source, room, sem), False
        self.copy.start()

    def wait(self):
        if not self.ready:
            self.ready = True
            self.copy.wait()

    def __getitem__(self, index):
        self.wait()
        return self.room[index]


def call(kernel, outs, scratch, args, flops=0):
    specs, rooms, counts = [], [], []
    for kind, a in args:
        if kind in ("smem", "vmem"):
            specs.append(pl.BlockSpec(memory_space=pltpu.SMEM if kind == "smem" else pltpu.VMEM))
        else:
            specs.append(pl.BlockSpec(memory_space=pl.ANY))
            rooms.append(pltpu.SMEM(a.shape, a.dtype))
            counts.append(1)
    out_rooms = [pltpu.VMEM(shape, dtype) for kind, shape, dtype in outs if kind == "hbm"]
    out_parts = sum(shape[0] for kind, shape, _ in outs if kind == "hbm")
    n_in, n_out, n_rooms = len(args), len(outs), len(rooms)

    def wrapped(*refs):
        ins, results, rest = refs[:n_in], refs[n_in : n_in + n_out], refs[n_in + n_out :]
        in_rooms, rest = rest[:n_rooms], rest[n_rooms:]
        result_rooms, rest = rest[: len(out_rooms)], rest[len(out_rooms) :]
        sems, rest = rest[0], rest[1:]
        given, base, at = [], 0, 0
        for (kind, _), ref in zip(args, ins):
            if kind in ("smem", "vmem"):
                given.append(ref)
                continue
            given.append(Late(ref, in_rooms[at], sems.at[base]))
            base += 1
            at += 1
        leaving, produced, at = [], [], 0
        for (kind, shape, _), ref in zip(outs, results):
            if kind == "vmem":
                produced.append(ref)
                continue
            room = result_rooms[at]
            produced.append((room, [pltpu.make_async_copy(room.at[i], ref.at[i], sems.at[base + i]) for i in range(shape[0])]))
            leaving += produced[-1][1]
            base += shape[0]
            at += 1
        kernel(*given, *produced, *rest)
        for item in given:
            if isinstance(item, Late):
                item.wait()
        for copy in leaving:
            copy.wait()

    moved = sum(int(np.prod(a.shape)) * a.dtype.itemsize for _, a in args)
    moved += sum(int(np.prod(shape)) * 4 for _, shape, _ in outs)
    return pl.pallas_call(
        wrapped,
        out_shape=[jax.ShapeDtypeStruct(shape, dtype) for _, shape, dtype in outs],
        in_specs=specs,
        out_specs=[pl.BlockSpec(memory_space=pltpu.VMEM if kind == "vmem" else pltpu.HBM) for kind, _, _ in outs],
        scratch_shapes=rooms
        + out_rooms
        + [pltpu.SemaphoreType.DMA((max(sum(counts) + out_parts, 1),))]
        + [pltpu.VMEM(shape, dtype) for shape, dtype in scratch],
        compiler_params=pltpu.CompilerParams(vmem_limit_bytes=VMEM_LIMIT),
        cost_estimate=pl.CostEstimate(flops=flops, bytes_accessed=moved, transcendentals=0),
    )(*[a for _, a in args])


def split(x):
    high = x.astype(bf16)
    return high, (x - high.astype(f32)).astype(bf16)


def pad_rows(x, rows):
    return x if x.shape[0] == rows else jnp.concatenate([x, jnp.zeros((rows - x.shape[0], x.shape[1]), x.dtype)], axis=0)


def stack(a):
    room = -a.shape[1] % LANES
    if room:
        a = jnp.concatenate([a, jnp.zeros((a.shape[0], room), a.dtype)], axis=1)
    return jnp.concatenate(split(a), axis=1)


def stacked_dot(a, x):
    xh, xl = split(x)
    rows = a.shape[1] // 2
    top = pad_rows(jnp.concatenate([xh, xl], axis=1), rows)
    low = pad_rows(jnp.concatenate([xh, jnp.zeros_like(xl)], axis=1), rows)
    both = jnp.dot(a, jnp.concatenate([top, low], axis=0), preferred_element_type=f32)
    return both[:, : x.shape[1]] + both[:, x.shape[1] :]


def dot(a, x):
    ah, al = a if isinstance(a, tuple) else split(a)
    xh, xl = split(x)
    n = x.shape[1]
    both = jnp.dot(ah, jnp.concatenate([xh, xl], axis=1), preferred_element_type=f32)
    return both[:, :n] + both[:, n:] + jnp.dot(al, xh, preferred_element_type=f32)


def small_dot(a, x):
    return jnp.dot(a, x, precision=highest, preferred_element_type=f32)


def face_of(state, e, face):
    if face == 0 or face == 1:
        start = 48 * face
        return jnp.concatenate([state[e, pl.ds(64 * v + start, 16)] for v in range(NVAR)], axis=0)
    if face >= 4:
        return state[e, pl.ds(3 * (face - 4), 80, stride=4)]
    half = 8 * (face - 2)
    first = jnp.concatenate([state[e, pl.ds(32 * m + half, 8)] for m in range(10)], axis=0)
    second = jnp.concatenate([state[e, pl.ds(32 * m + 16 + half, 8)] for m in range(10)], axis=0)
    low = lax.broadcasted_iota(jnp.int32, first.shape, 0) % 8 < 4
    if face == 2:
        return jnp.where(low, first, pltpu.roll(second, 4, 0))
    return jnp.where(low, pltpu.roll(first, 76, 0), second)


def link(ids, nbr, slots, e, face):
    g = nbr[e, face]
    owner = lax.div(g, slots)
    here = jnp.logical_and(g >= 0, owner == ids[2])
    away = jnp.logical_and(g >= 0, owner != ids[2])
    return here, away, jnp.maximum(lax.rem(g, slots), 0)


def crossing(ids, nbr, slots, face):
    found, slot = False, 0
    for e in range(slots):
        _, away, _ = link(ids, nbr, slots, e, face)
        found = jnp.logical_or(found, away)
        slot = jnp.where(away, e, slot)
    return found, slot


def swap_of(ids, face):
    return lax.rem(face % 2 + ids[face // 2] % 2 + 1, 2)


def fill_masks(ids, nbr, slots, masks):
    for i in range(4):
        for side in range(2):
            f = 2 * (i // 2) + side
            for e in range(slots):
                _, away, _ = link(ids, nbr, slots, e, f)
                value = jnp.where(jnp.logical_and(away, swap_of(ids, f) == i % 2), 1.0, 0.0)
                masks[(2 * i + side) * slots + e] = jnp.full(masks.shape[1:], value, f32)


def masked(mask, x):
    return (x.reshape(-1, *mask.shape) * mask).reshape(x.shape)


def meets(masks, slots, i, e):
    return masks[2 * i * slots + e] + masks[(2 * i + 1) * slots + e]


def crossing_traces(state):
    return [[face_of(state, e, f) for e in range(state.shape[0])] for f in range(4)]


def fill_traces(masks, traces, sends):
    slots = len(traces[0])
    for i in range(4):
        terms = [
            masked(masks[(2 * i + side) * slots + e], traces[2 * (i // 2) + side][e])
            for side in range(2)
            for e in range(slots)
        ]
        sends[i][...] = sum(terms[1:], terms[0])


def fill_elements(masks, w, sends):
    slots = w.shape[0]
    for i in range(4):
        terms = [masked(meets(masks, slots, i, e), w[e]) for e in range(slots)]
        sends[i][...] = sum(terms[1:], terms[0])


def first_kernel(counts, rhs, given, v, inverses):
    for e in range(rhs.shape[0]):
        live = jnp.where(e < counts[0], rhs[e], 0.0)
        inverses[e] = stack(given[e])
        v[e] = damping * stacked_dot(inverses[e], live)


def send_kernel(ids, nbr, v, s0, s1, s2, s3, masks):
    traces = crossing_traces(v)
    fill_masks(ids, nbr, v.shape[0], masks)
    fill_traces(masks, traces, (s0, s1, s2, s3))


def local_residual(ids, nbr, rhs_of, state, blocks, lifts, coef, out, traces):
    slots, _, columns = state.shape
    for e in range(slots):
        out[e] = rhs_of(e) - stacked_dot(blocks[e], state[e])
        for f in range(6):
            traces[f * slots + e] = face_of(state, e, f)
    near = []
    for e in range(slots):
        parts = []
        for f in range(6):
            here, _, s = link(ids, nbr, slots, e, f)
            t = traces[(f ^ 1) * slots + s] * coef[e, pl.ds(80 * f, 80)]
            parts.append(jnp.where(here, t, 0.0))
        near.append(jnp.concatenate(parts, axis=0))
    coupled = dot(lifts, jnp.concatenate(near, axis=1))
    for e in range(slots):
        out[e] = out[e] - coupled[:, e * columns : (e + 1) * columns]


def lay_out(lifts_t, coefs, lh, ll, coef):
    faces, nface, nf = lifts_t.shape
    slots = coef.shape[0]
    whole = jnp.concatenate([lifts_t[f] for f in range(faces)], axis=0).T
    lh[...], ll[...] = split(whole)
    turned = coefs[...].T
    for e in range(slots):
        for f in range(faces):
            column = turned[:, f * slots + e : f * slots + e + 1]
            coef[e, nface * f : nface * (f + 1)] = jnp.broadcast_to(column, (nface, coef.shape[2]))


def lay_out_far(ids, nbr, lifts_t, coef, far_lifts):
    nface, slots = lifts_t.shape[1], coef.shape[0]
    for i in range(4):
        low = 2 * (i // 2)
        first = swap_of(ids, low) == i % 2
        scaled = []
        for f in (low, low + 1):
            _, slot = crossing(ids, nbr, slots, f)
            scaled.append(lifts_t[f] * coef[slot, pl.ds(nface * f, nface)][:, :1])
        scaled = jnp.where(first, scaled[0], scaled[1])
        high = scaled.astype(bf16).astype(f32)
        far_lifts[i] = jnp.concatenate([high, scaled - high], axis=0).T.astype(bf16)


def first_local_kernel(
    ids, nbr, counts, state, lifts_t, coefs, given, rhs, out, lh, ll, far_lifts, coef, blocks, traces
):
    lay_out(lifts_t, coefs, lh, ll, coef)
    for e in range(given.shape[0]):
        blocks[e] = stack(given[e])

    def rhs_of(e):
        return jnp.where(e < counts[0], rhs[e], 0.0)

    local_residual(
        ids, nbr, rhs_of, state, blocks, (lh[...], ll[...]), coef, out, traces
    )
    lay_out_far(ids, nbr, lifts_t, coef, far_lifts)


def local_kernel(ids, nbr, counts, state, lh, ll, blocks, coef, rhs, out, traces):
    def rhs_of(e):
        return jnp.where(e < counts[0], rhs[e], 0.0)

    local_residual(ids, nbr, rhs_of, state, blocks, (lh[...], ll[...]), coef, out, traces)


def less_remote(masks, res, parts, e):
    slots = masks.shape[0] // 8
    for i, part in enumerate(parts):
        res = res - masked(meets(masks, slots, i, e), part)
    return res


def sweep_kernel(masks, y0, y1, y2, y3, res, state, far_lifts, inverses, v, *sends):
    parts = [stacked_dot(far_lifts[i], y[...]) for i, y in enumerate((y0, y1, y2, y3))]
    for e in range(res.shape[0]):
        value = state[e] + damping * stacked_dot(inverses[e], less_remote(masks, res[e], parts, e))
        if sends:
            v[e] = value
        else:
            v[0][e] = value
            v[1][e].start()
    if sends:
        fill_traces(masks, crossing_traces(v), sends)


def restrict_kernel(masks, y0, y1, y2, y3, res, far_lifts, restrict, inverses, _, r, rhs, w, *sends):
    parts = [stacked_dot(far_lifts[i], y[...]) for i, y in enumerate((y0, y1, y2, y3))]
    for e in range(r.shape[0]):
        left = less_remote(masks, res[e], parts, e)
        r[e] = left
        rhs[e] = 0.25 * dot(restrict[...], left)
        w[e] = damping * dot(inverses[e], rhs[e])
    fill_elements(masks, w, sends)


def prolong_kernel(ids, nbr, r, state, w, lh, ll, blocks, coef, prolong, out, corrected, traces, correction):
    slots = state.shape[0]
    for e in range(slots):
        correction[e] = dot(prolong[...], w[e])
        corrected[e] = state[e] + correction[e]
    local_residual(
        ids, nbr, lambda e: r[e], correction, blocks, (lh[...], ll[...]), coef, out, traces
    )


def post_kernel(masks, y0, y1, y2, y3, res, state, far_prolong, inverses, v, *sends):
    parts = [stacked_dot(far_prolong[i], y[...]) for i, y in enumerate((y0, y1, y2, y3))]
    for e in range(res.shape[0]):
        v[e] = state[e] + damping * stacked_dot(inverses[e], less_remote(masks, res[e], parts, e))
    fill_traces(masks, crossing_traces(v), sends)


def coarse_lay_out_kernel(lifts_t, coefs, hot_t, _, lifts, coef, wide):
    faces, _, nc = lifts_t.shape
    slots = coef.shape[0]
    turned = coefs[...].T
    for f in range(faces):
        wide[f] = small_dot(hot_t[f], lifts_t[f])
    lifts[...] = jnp.concatenate([wide[f] for f in range(faces)], axis=0).T
    for f in range(faces):
        spread = small_dot(hot_t[f], turned)
        for e in range(slots):
            column = spread[:, f * slots + e : f * slots + e + 1]
            coef[e, nc * f : nc * (f + 1)] = jnp.broadcast_to(column, (nc, coef.shape[2]))


def coarse_remote_kernel(masks, wide, coef, inverses, far_lifts, face_prolong, remote, far_prolong):
    slots, nc, _ = inverses.shape
    for i in range(4):
        total = None
        for side in range(2):
            on = sum(masks[(2 * i + side) * slots + e] for e in range(slots))
            term = masked(on, face_prolong[2 * (i // 2) + 1 - side])
            total = term if total is None else total + term
        far_prolong[i] = jnp.concatenate(split(stacked_dot(far_lifts[i], total)), axis=1)
    for e in range(slots):
        scaled = []
        for i in range(4):
            total = None
            for side in range(2):
                f = 2 * (i // 2) + side
                term = masked(masks[(2 * i + side) * slots + e], coef[e, nc * f : nc * (f + 1)])
                term = wide[f] * term[:, :nc]
                total = term if total is None else total + term
            scaled.append(total)
        rows = damping * small_dot(inverses[e], jnp.concatenate(scaled, axis=0).T)
        remote[e * nc : (e + 1) * nc] = rows


def coarse_local_kernel(ids, nbr, w, rhs, blocks, inverses, lifts, coef, out):
    slots, nc, columns = w.shape
    for e in range(slots):
        out[e] = rhs[e] - dot(blocks[e], w[e])
    near = []
    for e in range(slots):
        parts = []
        for f in range(6):
            here, _, s = link(ids, nbr, slots, e, f)
            parts.append(jnp.where(here, w[s] * coef[e, nc * f : nc * (f + 1)], 0.0))
        near.append(jnp.concatenate(parts, axis=0))
    coupled = dot(lifts[...], jnp.concatenate(near, axis=1))
    for e in range(slots):
        res = out[e] - coupled[:, e * columns : (e + 1) * columns]
        out[e] = w[e] + damping * dot(inverses[e], res)


def coarse_sweep_kernel(masks, y0, y1, y2, y3, local, remote, w, *sends):
    slots, nc, _ = w.shape
    far = dot(remote[...], jnp.concatenate([y[...] for y in (y0, y1, y2, y3)], axis=0))
    for e in range(slots):
        w[e] = local[e] - far[e * nc : (e + 1) * nc]
    fill_elements(masks, w, sends)


def swap(parts):
    got = []
    for i in range(len(parts)):
        axis = AXES[i // 2]
        pairs = []
        for a in range(i % 2, lax.axis_size(axis) - 1, 2):
            pairs += [(a, a + 1), (a + 1, a)]
        got.append(lax.ppermute(parts[i], axis, pairs))
    return got


def body(
    right_side,
    fine_blocks,
    fine_inverses,
    fine_lifts,
    fine_coefs,
    coarse_blocks,
    coarse_inverses,
    coarse_lifts,
    coarse_coefs,
    neighbours,
    counts,
):
    slots, nf, columns = right_side.shape
    nface = fine_lifts.shape[2]
    nc = coarse_blocks.shape[1]
    ncf = coarse_lifts.shape[2]
    wide_here, narrow_here = lax.axis_index("wide"), lax.axis_index("narrow")
    ids = jnp.stack([wide_here, narrow_here, wide_here * lax.axis_size("narrow") + narrow_here]).astype(jnp.int32)

    prolong_np = prolong_table(NODE1, NVAR)
    coarse_table = face_rows(2, NVAR)
    fine_table = face_rows(NODE1, NVAR)
    prolong = jnp.asarray(prolong_np)
    restrict = jnp.asarray(np.ascontiguousarray(prolong_np.T))
    face_prolong = np.stack([prolong_np[fine_table[f]] for f in range(4)])
    face_prolong = jnp.asarray(np.pad(face_prolong, ((0, 0), (0, 0), (0, LANES - nc))))
    hot_np = np.zeros((6, nc, ncf), np.float32)
    for f in range(6):
        hot_np[f, coarse_table[f ^ 1], np.arange(ncf)] = 1.0
    hot_t = jnp.asarray(hot_np)

    lifts_t = fine_lifts.transpose(0, 2, 1)
    coefs = fine_coefs.transpose(1, 0, 2).reshape(6 * slots, nface)
    coarse_lifts_t = coarse_lifts.transpose(0, 2, 1)
    coarse_coefs_t = coarse_coefs.transpose(1, 0, 2).reshape(6 * slots, ncf)

    field = ("vmem", (slots, nf, columns), f32)
    faces = [("vmem", (nface, columns), f32)] * 4
    coarse = ("vmem", (slots, nc, columns), f32)
    coarse_sends = [("vmem", (nc, columns), f32)] * 4
    trace_room = ((6 * slots, nface, columns), f32)
    field_room = (field[1], f32)
    block_flops = 3 * 2 * slots * nf * nf * columns
    lift_flops = 3 * 2 * slots * nf * 6 * nface * columns
    where = [("late", ids), ("late", neighbours)]
    live = where + [("smem", counts)]

    def vm(*arrays):
        return [("vmem", a) for a in arrays]

    def parts(*arrays):
        return [("parts", a) for a in arrays]

    wide = 2 * (nf + -nf % LANES)
    matrix = ("vmem", (slots, nf, wide), bf16)
    mask_tiles = ("vmem", (8 * slots, 8, columns), f32)
    state, inverses = call(
        first_kernel, [field, matrix], [], [("smem", counts)] + vm(right_side, fine_inverses), 8 * block_flops
    )
    *sends, masks = call(send_kernel, faces + [mask_tiles], [], where + vm(state))
    got = swap(sends)
    res, lh, ll, far_lifts, coef, blocks = call(
        first_local_kernel,
        [field]
        + [("vmem", (nf, 6 * nface), bf16)] * 2
        + [("vmem", (4, nf, 2 * nface), bf16), ("vmem", (slots, 6 * nface, columns), f32), matrix],
        [trace_room],
        live + vm(state, lifts_t, coefs, fine_blocks, right_side),
        block_flops + lift_flops,
    )

    def local(state):
        return call(
            local_kernel, [field], [trace_room],
            live + vm(state, lh, ll, blocks, coef, right_side), block_flops + lift_flops,
        )[0]

    def sweep(got, res, state, last):
        return call(
            sweep_kernel, [("hbm",) + field[1:]] if last else [field] + faces, [],
            vm(masks, *got, res, state, far_lifts, inverses), block_flops,
        )

    for i in range(PRE_SWEEPS - 1):
        state, *sends = sweep(got, res, state, False)
        got = swap(sends)
        res = local(state)
    coarse_wide, coarse_coef, coarse_faces = call(
        coarse_lay_out_kernel,
        [("vmem", (nc, 6 * nc), f32), ("vmem", (slots, 6 * nc, columns), f32), ("vmem", (6, nc, nc), f32)], [],
        vm(coarse_lifts_t, coarse_coefs_t, hot_t, state),
    )
    residual, coarse_rhs, w, *sends = call(
        restrict_kernel, [field, coarse, coarse] + coarse_sends, [],
        vm(masks, *got, res, far_lifts, restrict, coarse_inverses, coarse_wide),
    )
    coarse_remote, far_prolong = call(
        coarse_remote_kernel,
        [("vmem", (slots * nc, 4 * nc), f32), ("vmem", (4, nf, 2 * LANES), bf16)], [],
        vm(masks, coarse_faces, coarse_coef, coarse_inverses, far_lifts, face_prolong),
    )
    for _ in range(COARSE_SWEEPS - 1):
        got = swap(sends)
        (w_local,) = call(
            coarse_local_kernel, [coarse], [],
            where + vm(w, coarse_rhs, coarse_blocks, coarse_inverses, coarse_wide, coarse_coef),
        )
        w, *sends = call(
            coarse_sweep_kernel, [coarse] + coarse_sends, [], vm(masks, *got, w_local, coarse_remote)
        )
    got = swap(sends)
    res, state = call(
        prolong_kernel, [field, field], [trace_room, field_room],
        where + vm(residual, state, w, lh, ll, blocks, coef, prolong),
        block_flops + lift_flops,
    )
    state, *sends = call(
        post_kernel, [field] + faces, [],
        vm(masks, *got, res, state, far_prolong, inverses), block_flops,
    )
    for i in range(POST_SWEEPS - 1):
        got = swap(sends)
        res = local(state)
        state, *sends = sweep(got, res, state, i == POST_SWEEPS - 2)
    return state


def solution(mesh):
    placed = (
        P(AXES, None, None),
        P(AXES, None, None),
        P(AXES, None, None),
        P(),
        P(AXES, None, None),
        P(AXES, None, None),
        P(AXES, None, None),
        P(),
        P(AXES, None, None),
        P(AXES, None),
        P(AXES),
    )
    return jax.shard_map(
        body,
        mesh=mesh,
        in_specs=placed,
        out_specs=P(AXES, None, None),
        check_vma=False,
    )
```

```python
import functools

import jax
import jax.numpy as jnp
import numpy as np
from jax import lax
from jax.experimental import pallas as pl
from jax.experimental.pallas import tpu as pltpu
from jax.sharding import PartitionSpec as P

NVAR = 5
NODE1 = 4
PRE_SWEEPS = 2
POST_SWEEPS = 2
COARSE_SWEEPS = 4
AXES = ("wide", "narrow")
LANES = 128
VMEM_LIMIT = 16 * 1024 * 1024

damping = 0.8
highest = lax.Precision.HIGHEST
f32, bf16 = jnp.float32, jnp.bfloat16


def prolong_table(node_count, variables):
    points = np.array([-1.0, -1.0 / np.sqrt(5.0), 1.0 / np.sqrt(5.0), 1.0])
    linear = np.stack([(1.0 - points) / 2.0, (1.0 + points) / 2.0], axis=1)
    tensor_hat = (
        linear[:, None, None, :, None, None]
        * linear[None, :, None, None, :, None]
        * linear[None, None, :, None, None, :]
    )
    tensor_hat = tensor_hat.reshape(node_count * node_count * node_count, 8)
    return np.kron(np.eye(variables), tensor_hat).astype(np.float32)


def face_rows(node_count, variables):
    cube = node_count**3
    lattice = np.arange(cube).reshape(node_count, node_count, node_count)
    tables = []
    for face in range(6):
        layer = np.take(lattice, 0 if face % 2 == 0 else node_count - 1, axis=face // 2).reshape(-1)
        tables.append(np.concatenate([layer + v * cube for v in range(variables)]))
    return np.stack(tables)


class Late:
    def __init__(self, source, room, sem):
        self.room, self.copy, self.ready = room, pltpu.make_async_copy(source, room, sem), False
        self.copy.start()

    def wait(self):
        if not self.ready:
            self.ready = True
            self.copy.wait()

    def __getitem__(self, index):
        self.wait()
        return self.room[index]


def call(kernel, outs, scratch, args, flops=0):
    specs, rooms, counts = [], [], []
    for kind, a in args:
        if kind in ("smem", "vmem"):
            specs.append(pl.BlockSpec(memory_space=pltpu.SMEM if kind == "smem" else pltpu.VMEM))
        else:
            specs.append(pl.BlockSpec(memory_space=pl.ANY))
            rooms.append(pltpu.SMEM(a.shape, a.dtype))
            counts.append(1)
    out_rooms = [pltpu.VMEM(shape, dtype) for kind, shape, dtype in outs if kind == "hbm"]
    out_parts = sum(shape[0] for kind, shape, _ in outs if kind == "hbm")
    n_in, n_out, n_rooms = len(args), len(outs), len(rooms)

    def wrapped(*refs):
        ins, results, rest = refs[:n_in], refs[n_in : n_in + n_out], refs[n_in + n_out :]
        in_rooms, rest = rest[:n_rooms], rest[n_rooms:]
        result_rooms, rest = rest[: len(out_rooms)], rest[len(out_rooms) :]
        sems, rest = rest[0], rest[1:]
        given, base, at = [], 0, 0
        for (kind, _), ref in zip(args, ins):
            if kind in ("smem", "vmem"):
                given.append(ref)
                continue
            given.append(Late(ref, in_rooms[at], sems.at[base]))
            base += 1
            at += 1
        leaving, produced, at = [], [], 0
        for (kind, shape, _), ref in zip(outs, results):
            if kind == "vmem":
                produced.append(ref)
                continue
            room = result_rooms[at]
            produced.append((room, [pltpu.make_async_copy(room.at[i], ref.at[i], sems.at[base + i]) for i in range(shape[0])]))
            leaving += produced[-1][1]
            base += shape[0]
            at += 1
        kernel(*given, *produced, *rest)
        for item in given:
            if isinstance(item, Late):
                item.wait()
        for copy in leaving:
            copy.wait()

    moved = sum(int(np.prod(a.shape)) * a.dtype.itemsize for _, a in args)
    moved += sum(int(np.prod(shape)) * 4 for _, shape, _ in outs)
    return pl.pallas_call(
        wrapped,
        out_shape=[jax.ShapeDtypeStruct(shape, dtype) for _, shape, dtype in outs],
        in_specs=specs,
        out_specs=[pl.BlockSpec(memory_space=pltpu.VMEM if kind == "vmem" else pltpu.HBM) for kind, _, _ in outs],
        scratch_shapes=rooms
        + out_rooms
        + [pltpu.SemaphoreType.DMA((max(sum(counts) + out_parts, 1),))]
        + [pltpu.VMEM(shape, dtype) for shape, dtype in scratch],
        compiler_params=pltpu.CompilerParams(vmem_limit_bytes=VMEM_LIMIT),
        cost_estimate=pl.CostEstimate(flops=flops, bytes_accessed=moved, transcendentals=0),
    )(*[a for _, a in args])


def split(x):
    high = x.astype(bf16)
    return high, (x - high.astype(f32)).astype(bf16)


def pad_rows(x, rows):
    return x if x.shape[0] == rows else jnp.concatenate([x, jnp.zeros((rows - x.shape[0], x.shape[1]), x.dtype)], axis=0)


def stack(a):
    room = -a.shape[1] % LANES
    if room:
        a = jnp.concatenate([a, jnp.zeros((a.shape[0], room), a.dtype)], axis=1)
    return jnp.concatenate(split(a), axis=1)


def stacked_dot(a, x):
    xh, xl = split(x)
    rows = a.shape[1] // 2
    top = pad_rows(jnp.concatenate([xh, xl], axis=1), rows)
    low = pad_rows(jnp.concatenate([xh, jnp.zeros_like(xl)], axis=1), rows)
    both = jnp.dot(a, jnp.concatenate([top, low], axis=0), preferred_element_type=f32)
    return both[:, : x.shape[1]] + both[:, x.shape[1] :]


def dot(a, x):
    ah, al = a if isinstance(a, tuple) else split(a)
    xh, xl = split(x)
    n = x.shape[1]
    both = jnp.dot(ah, jnp.concatenate([xh, xl], axis=1), preferred_element_type=f32)
    return both[:, :n] + both[:, n:] + jnp.dot(al, xh, preferred_element_type=f32)


def small_dot(a, x):
    return jnp.dot(a, x, precision=highest, preferred_element_type=f32)


def face_of(state, e, face):
    if face == 0 or face == 1:
        start = 48 * face
        return jnp.concatenate([state[e, pl.ds(64 * v + start, 16)] for v in range(NVAR)], axis=0)
    if face >= 4:
        return state[e, pl.ds(3 * (face - 4), 80, stride=4)]
    half = 8 * (face - 2)
    first = jnp.concatenate([state[e, pl.ds(32 * m + half, 8)] for m in range(10)], axis=0)
    second = jnp.concatenate([state[e, pl.ds(32 * m + 16 + half, 8)] for m in range(10)], axis=0)
    low = lax.broadcasted_iota(jnp.int32, first.shape, 0) % 8 < 4
    if face == 2:
        return jnp.where(low, first, pltpu.roll(second, 4, 0))
    return jnp.where(low, pltpu.roll(first, 76, 0), second)


def link(ids, nbr, slots, e, face):
    g = nbr[e, face]
    owner = lax.div(g, slots)
    here = jnp.logical_and(g >= 0, owner == ids[2])
    away = jnp.logical_and(g >= 0, owner != ids[2])
    return here, away, jnp.maximum(lax.rem(g, slots), 0)


def crossing(ids, nbr, slots, face):
    found, slot = False, 0
    for e in range(slots):
        _, away, _ = link(ids, nbr, slots, e, face)
        found = jnp.logical_or(found, away)
        slot = jnp.where(away, e, slot)
    return found, slot


def swap_of(ids, face):
    return lax.rem(face % 2 + ids[face // 2] % 2 + 1, 2)


def fill_masks(ids, nbr, slots, masks):
    for i in range(4):
        for side in range(2):
            f = 2 * (i // 2) + side
            for e in range(slots):
                _, away, _ = link(ids, nbr, slots, e, f)
                value = jnp.where(jnp.logical_and(away, swap_of(ids, f) == i % 2), 1.0, 0.0)
                masks[(2 * i + side) * slots + e] = jnp.full(masks.shape[1:], value, f32)


def masked(mask, x):
    return (x.reshape(-1, *mask.shape) * mask).reshape(x.shape)


def meets(masks, slots, i, e):
    return masks[2 * i * slots + e] + masks[(2 * i + 1) * slots + e]


def crossing_traces(state):
    return [[face_of(state, e, f) for e in range(state.shape[0])] for f in range(4)]


def fill_traces(masks, traces, sends):
    slots = len(traces[0])
    for i in range(4):
        terms = [
            masked(masks[(2 * i + side) * slots + e], traces[2 * (i // 2) + side][e])
            for side in range(2)
            for e in range(slots)
        ]
        sends[i][...] = sum(terms[1:], terms[0])


def fill_elements(masks, w, sends):
    slots = w.shape[0]
    for i in range(4):
        terms = [masked(meets(masks, slots, i, e), w[e]) for e in range(slots)]
        sends[i][...] = sum(terms[1:], terms[0])


def first_kernel(counts, rhs, given, v, inverses):
    for e in range(rhs.shape[0]):
        live = jnp.where(e < counts[0], rhs[e], 0.0)
        inverses[e] = stack(given[e])
        v[e] = damping * stacked_dot(inverses[e], live)


def send_kernel(ids, nbr, v, s0, s1, s2, s3, masks):
    traces = crossing_traces(v)
    fill_masks(ids, nbr, v.shape[0], masks)
    fill_traces(masks, traces, (s0, s1, s2, s3))


def local_residual(ids, nbr, rhs_of, state, blocks, lifts, coef, out, traces):
    slots, _, columns = state.shape
    for e in range(slots):
        out[e] = rhs_of(e) - stacked_dot(blocks[e], state[e])
        for f in range(6):
            traces[f * slots + e] = face_of(state, e, f)
    near = []
    for e in range(slots):
        parts = []
        for f in range(6):
            here, _, s = link(ids, nbr, slots, e, f)
            t = traces[(f ^ 1) * slots + s] * coef[e, pl.ds(80 * f, 80)]
            parts.append(jnp.where(here, t, 0.0))
        near.append(jnp.concatenate(parts, axis=0))
    coupled = dot(lifts, jnp.concatenate(near, axis=1))
    for e in range(slots):
        out[e] = out[e] - coupled[:, e * columns : (e + 1) * columns]


def lay_out(lifts_t, coefs, lh, ll, coef):
    faces, nface, nf = lifts_t.shape
    slots = coef.shape[0]
    whole = jnp.concatenate([lifts_t[f] for f in range(faces)], axis=0).T
    lh[...], ll[...] = split(whole)
    turned = coefs[...].T
    for e in range(slots):
        for f in range(faces):
            column = turned[:, f * slots + e : f * slots + e + 1]
            coef[e, nface * f : nface * (f + 1)] = jnp.broadcast_to(column, (nface, coef.shape[2]))


def lay_out_far(ids, nbr, lifts_t, coef, far_lifts):
    nface, slots = lifts_t.shape[1], coef.shape[0]
    for i in range(4):
        low = 2 * (i // 2)
        first = swap_of(ids, low) == i % 2
        scaled = []
        for f in (low, low + 1):
            _, slot = crossing(ids, nbr, slots, f)
            scaled.append(lifts_t[f] * coef[slot, pl.ds(nface * f, nface)][:, :1])
        scaled = jnp.where(first, scaled[0], scaled[1])
        high = scaled.astype(bf16).astype(f32)
        far_lifts[i] = jnp.concatenate([high, scaled - high], axis=0).T.astype(bf16)


def first_local_kernel(
    ids, nbr, counts, state, lifts_t, coefs, given, rhs, out, lh, ll, far_lifts, coef, blocks, traces
):
    lay_out(lifts_t, coefs, lh, ll, coef)
    for e in range(given.shape[0]):
        blocks[e] = stack(given[e])

    def rhs_of(e):
        return jnp.where(e < counts[0], rhs[e], 0.0)

    local_residual(
        ids, nbr, rhs_of, state, blocks, (lh[...], ll[...]), coef, out, traces
    )
    lay_out_far(ids, nbr, lifts_t, coef, far_lifts)


def local_kernel(ids, nbr, counts, state, lh, ll, blocks, coef, rhs, out, traces):
    def rhs_of(e):
        return jnp.where(e < counts[0], rhs[e], 0.0)

    local_residual(ids, nbr, rhs_of, state, blocks, (lh[...], ll[...]), coef, out, traces)


def less_remote(masks, res, parts, e):
    slots = masks.shape[0] // 8
    for i, part in enumerate(parts):
        res = res - masked(meets(masks, slots, i, e), part)
    return res


def sweep_kernel(masks, y0, y1, y3, y2, res, state, far_lifts, inverses, v, *sends):
    parts = [stacked_dot(far_lifts[i], y[...]) for i, y in enumerate((y0, y1, y2, y3))]
    for e in range(res.shape[0]):
        value = state[e] + damping * stacked_dot(inverses[e], less_remote(masks, res[e], parts, e))
        if sends:
            v[e] = value
        else:
            v[0][e] = value
            v[1][e].start()
    if sends:
        fill_traces(masks, crossing_traces(v), sends)


def restrict_kernel(masks, y0, y1, y3, y2, res, far_lifts, restrict, inverses, _, r, rhs, w, *sends):
    parts = [stacked_dot(far_lifts[i], y[...]) for i, y in enumerate((y0, y1, y2, y3))]
    for e in range(r.shape[0]):
        left = less_remote(masks, res[e], parts, e)
        r[e] = left
        rhs[e] = 0.25 * dot(restrict[...], left)
        w[e] = damping * dot(inverses[e], rhs[e])
    fill_elements(masks, w, sends)


def prolong_kernel(ids, nbr, r, state, w, lh, ll, blocks, coef, prolong, out, corrected, traces, correction):
    slots = state.shape[0]
    for e in range(slots):
        correction[e] = dot(prolong[...], w[e])
        corrected[e] = state[e] + correction[e]
    local_residual(
        ids, nbr, lambda e: r[e], correction, blocks, (lh[...], ll[...]), coef, out, traces
    )


def post_kernel(masks, y0, y1, y3, y2, res, state, far_prolong, inverses, v, *sends):
    parts = [stacked_dot(far_prolong[i], y[...]) for i, y in enumerate((y0, y1, y2, y3))]
    for e in range(res.shape[0]):
        v[e] = state[e] + damping * stacked_dot(inverses[e], less_remote(masks, res[e], parts, e))
    fill_traces(masks, crossing_traces(v), sends)


def coarse_lay_out_kernel(lifts_t, coefs, hot_t, _, lifts, coef, wide):
    faces, _, nc = lifts_t.shape
    slots = coef.shape[0]
    turned = coefs[...].T
    for f in range(faces):
        wide[f] = small_dot(hot_t[f], lifts_t[f])
    lifts[...] = jnp.concatenate([wide[f] for f in range(faces)], axis=0).T
    for f in range(faces):
        spread = small_dot(hot_t[f], turned)
        for e in range(slots):
            column = spread[:, f * slots + e : f * slots + e + 1]
            coef[e, nc * f : nc * (f + 1)] = jnp.broadcast_to(column, (nc, coef.shape[2]))


def coarse_remote_kernel(masks, wide, coef, inverses, far_lifts, face_prolong, remote, far_prolong):
    slots, nc, _ = inverses.shape
    for i in range(4):
        total = None
        for side in range(2):
            on = sum(masks[(2 * i + side) * slots + e] for e in range(slots))
            term = masked(on, face_prolong[2 * (i // 2) + 1 - side])
            total = term if total is None else total + term
        far_prolong[i] = jnp.concatenate(split(stacked_dot(far_lifts[i], total)), axis=1)
    for e in range(slots):
        scaled = []
        for i in range(4):
            total = None
            for side in range(2):
                f = 2 * (i // 2) + side
                term = masked(masks[(2 * i + side) * slots + e], coef[e, nc * f : nc * (f + 1)])
                term = wide[f] * term[:, :nc]
                total = term if total is None else total + term
            scaled.append(total)
        rows = damping * small_dot(inverses[e], jnp.concatenate(scaled, axis=0).T)
        remote[e * nc : (e + 1) * nc] = rows


def coarse_local_kernel(ids, nbr, w, rhs, blocks, inverses, lifts, coef, out):
    slots, nc, columns = w.shape
    for e in range(slots):
        out[e] = rhs[e] - dot(blocks[e], w[e])
    near = []
    for e in range(slots):
        parts = []
        for f in range(6):
            here, _, s = link(ids, nbr, slots, e, f)
            parts.append(jnp.where(here, w[s] * coef[e, nc * f : nc * (f + 1)], 0.0))
        near.append(jnp.concatenate(parts, axis=0))
    coupled = dot(lifts[...], jnp.concatenate(near, axis=1))
    for e in range(slots):
        res = out[e] - coupled[:, e * columns : (e + 1) * columns]
        out[e] = w[e] + damping * dot(inverses[e], res)


def coarse_sweep_kernel(masks, y0, y1, y3, y2, local, remote, w, *sends):
    slots, nc, _ = w.shape
    far = dot(remote[...], jnp.concatenate([y[...] for y in (y0, y1, y2, y3)], axis=0))
    for e in range(slots):
        w[e] = local[e] - far[e * nc : (e + 1) * nc]
    fill_elements(masks, w, sends)


def swap(parts):
    got = []
    for i in (0, 1, 3, 2):
        axis = AXES[i // 2]
        pairs = []
        for a in range(i % 2, lax.axis_size(axis) - 1, 2):
            pairs += [(a, a + 1), (a + 1, a)]
        got.append(lax.ppermute(parts[i], axis, pairs))
    return got


def body(
    right_side,
    fine_blocks,
    fine_inverses,
    fine_lifts,
    fine_coefs,
    coarse_blocks,
    coarse_inverses,
    coarse_lifts,
    coarse_coefs,
    neighbours,
    counts,
):
    slots, nf, columns = right_side.shape
    nface = fine_lifts.shape[2]
    nc = coarse_blocks.shape[1]
    ncf = coarse_lifts.shape[2]
    wide_here, narrow_here = lax.axis_index("wide"), lax.axis_index("narrow")
    ids = jnp.stack([wide_here, narrow_here, wide_here * lax.axis_size("narrow") + narrow_here]).astype(jnp.int32)

    prolong_np = prolong_table(NODE1, NVAR)
    coarse_table = face_rows(2, NVAR)
    fine_table = face_rows(NODE1, NVAR)
    prolong = jnp.asarray(prolong_np)
    restrict = jnp.asarray(np.ascontiguousarray(prolong_np.T))
    face_prolong = np.stack([prolong_np[fine_table[f]] for f in range(4)])
    face_prolong = jnp.asarray(np.pad(face_prolong, ((0, 0), (0, 0), (0, LANES - nc))))
    hot_np = np.zeros((6, nc, ncf), np.float32)
    for f in range(6):
        hot_np[f, coarse_table[f ^ 1], np.arange(ncf)] = 1.0
    hot_t = jnp.asarray(hot_np)

    lifts_t = fine_lifts.transpose(0, 2, 1)
    coefs = fine_coefs.transpose(1, 0, 2).reshape(6 * slots, nface)
    coarse_lifts_t = coarse_lifts.transpose(0, 2, 1)
    coarse_coefs_t = coarse_coefs.transpose(1, 0, 2).reshape(6 * slots, ncf)

    field = ("vmem", (slots, nf, columns), f32)
    faces = [("vmem", (nface, columns), f32)] * 4
    coarse = ("vmem", (slots, nc, columns), f32)
    coarse_sends = [("vmem", (nc, columns), f32)] * 4
    trace_room = ((6 * slots, nface, columns), f32)
    field_room = (field[1], f32)
    block_flops = 3 * 2 * slots * nf * nf * columns
    lift_flops = 3 * 2 * slots * nf * 6 * nface * columns
    where = [("late", ids), ("late", neighbours)]
    live = where + [("smem", counts)]

    def vm(*arrays):
        return [("vmem", a) for a in arrays]

    def parts(*arrays):
        return [("parts", a) for a in arrays]

    wide = 2 * (nf + -nf % LANES)
    matrix = ("vmem", (slots, nf, wide), bf16)
    mask_tiles = ("vmem", (8 * slots, 8, columns), f32)
    state, inverses = call(
        first_kernel, [field, matrix], [], [("smem", counts)] + vm(right_side, fine_inverses), 8 * block_flops
    )
    *sends, masks = call(send_kernel, faces + [mask_tiles], [], where + vm(state))
    got = swap(sends)
    res, lh, ll, far_lifts, coef, blocks = call(
        first_local_kernel,
        [field]
        + [("vmem", (nf, 6 * nface), bf16)] * 2
        + [("vmem", (4, nf, 2 * nface), bf16), ("vmem", (slots, 6 * nface, columns), f32), matrix],
        [trace_room],
        live + vm(state, lifts_t, coefs, fine_blocks, right_side),
        block_flops + lift_flops,
    )

    def local(state):
        return call(
            local_kernel, [field], [trace_room],
            live + vm(state, lh, ll, blocks, coef, right_side), block_flops + lift_flops,
        )[0]

    def sweep(got, res, state, last):
        return call(
            sweep_kernel, [("hbm",) + field[1:]] if last else [field] + faces, [],
            vm(masks, *got, res, state, far_lifts, inverses), block_flops,
        )

    for i in range(PRE_SWEEPS - 1):
        state, *sends = sweep(got, res, state, False)
        got = swap(sends)
        res = local(state)
    coarse_wide, coarse_coef, coarse_faces = call(
        coarse_lay_out_kernel,
        [("vmem", (nc, 6 * nc), f32), ("vmem", (slots, 6 * nc, columns), f32), ("vmem", (6, nc, nc), f32)], [],
        vm(coarse_lifts_t, coarse_coefs_t, hot_t, state),
    )
    residual, coarse_rhs, w, *sends = call(
        restrict_kernel, [field, coarse, coarse] + coarse_sends, [],
        vm(masks, *got, res, far_lifts, restrict, coarse_inverses, coarse_wide),
    )
    coarse_remote, far_prolong = call(
        coarse_remote_kernel,
        [("vmem", (slots * nc, 4 * nc), f32), ("vmem", (4, nf, 2 * LANES), bf16)], [],
        vm(masks, coarse_faces, coarse_coef, coarse_inverses, far_lifts, face_prolong),
    )
    for _ in range(COARSE_SWEEPS - 1):
        got = swap(sends)
        (w_local,) = call(
            coarse_local_kernel, [coarse], [],
            where + vm(w, coarse_rhs, coarse_blocks, coarse_inverses, coarse_wide, coarse_coef),
        )
        w, *sends = call(
            coarse_sweep_kernel, [coarse] + coarse_sends, [], vm(masks, *got, w_local, coarse_remote)
        )
    got = swap(sends)
    res, state = call(
        prolong_kernel, [field, field], [trace_room, field_room],
        where + vm(residual, state, w, lh, ll, blocks, coef, prolong),
        block_flops + lift_flops,
    )
    state, *sends = call(
        post_kernel, [field] + faces, [],
        vm(masks, *got, res, state, far_prolong, inverses), block_flops,
    )
    for i in range(POST_SWEEPS - 1):
        got = swap(sends)
        res = local(state)
        state, *sends = sweep(got, res, state, i == POST_SWEEPS - 2)
    return state


def solution(mesh):
    placed = (
        P(AXES, None, None),
        P(AXES, None, None),
        P(AXES, None, None),
        P(),
        P(AXES, None, None),
        P(AXES, None, None),
        P(AXES, None, None),
        P(),
        P(AXES, None, None),
        P(AXES, None),
        P(AXES),
    )
    return jax.shard_map(
        body,
        mesh=mesh,
        in_specs=placed,
        out_specs=P(AXES, None, None),
        check_vma=False,
    )
```

```python
import functools

import jax
import jax.numpy as jnp
import numpy as np
from jax import lax
from jax.experimental import pallas as pl
from jax.experimental.pallas import tpu as pltpu
from jax.sharding import PartitionSpec as P

NVAR = 5
NODE1 = 4
PRE_SWEEPS = 2
POST_SWEEPS = 2
COARSE_SWEEPS = 4
AXES = ("wide", "narrow")
LANES = 128
VMEM_LIMIT = 16 * 1024 * 1024

damping = 0.8
highest = lax.Precision.HIGHEST
f32, bf16 = jnp.float32, jnp.bfloat16


def prolong_table(node_count, variables):
    points = np.array([-1.0, -1.0 / np.sqrt(5.0), 1.0 / np.sqrt(5.0), 1.0])
    linear = np.stack([(1.0 - points) / 2.0, (1.0 + points) / 2.0], axis=1)
    tensor_hat = (
        linear[:, None, None, :, None, None]
        * linear[None, :, None, None, :, None]
        * linear[None, None, :, None, None, :]
    )
    tensor_hat = tensor_hat.reshape(node_count * node_count * node_count, 8)
    return np.kron(np.eye(variables), tensor_hat).astype(np.float32)


def face_rows(node_count, variables):
    cube = node_count**3
    lattice = np.arange(cube).reshape(node_count, node_count, node_count)
    tables = []
    for face in range(6):
        layer = np.take(lattice, 0 if face % 2 == 0 else node_count - 1, axis=face // 2).reshape(-1)
        tables.append(np.concatenate([layer + v * cube for v in range(variables)]))
    return np.stack(tables)


class Late:
    def __init__(self, source, room, sem):
        self.room, self.copy, self.ready = room, pltpu.make_async_copy(source, room, sem), False
        self.copy.start()

    def wait(self):
        if not self.ready:
            self.ready = True
            self.copy.wait()

    def __getitem__(self, index):
        self.wait()
        return self.room[index]


def call(kernel, outs, scratch, args, flops=0):
    specs, rooms, counts = [], [], []
    for kind, a in args:
        if kind in ("smem", "vmem"):
            specs.append(pl.BlockSpec(memory_space=pltpu.SMEM if kind == "smem" else pltpu.VMEM))
        else:
            specs.append(pl.BlockSpec(memory_space=pl.ANY))
            rooms.append(pltpu.SMEM(a.shape, a.dtype))
            counts.append(1)
    out_rooms = [pltpu.VMEM(shape, dtype) for kind, shape, dtype in outs if kind == "hbm"]
    out_parts = sum(shape[0] for kind, shape, _ in outs if kind == "hbm")
    n_in, n_out, n_rooms = len(args), len(outs), len(rooms)

    def wrapped(*refs):
        ins, results, rest = refs[:n_in], refs[n_in : n_in + n_out], refs[n_in + n_out :]
        in_rooms, rest = rest[:n_rooms], rest[n_rooms:]
        result_rooms, rest = rest[: len(out_rooms)], rest[len(out_rooms) :]
        sems, rest = rest[0], rest[1:]
        given, base, at = [], 0, 0
        for (kind, _), ref in zip(args, ins):
            if kind in ("smem", "vmem"):
                given.append(ref)
                continue
            given.append(Late(ref, in_rooms[at], sems.at[base]))
            base += 1
            at += 1
        leaving, produced, at = [], [], 0
        for (kind, shape, _), ref in zip(outs, results):
            if kind == "vmem":
                produced.append(ref)
                continue
            room = result_rooms[at]
            produced.append((room, [pltpu.make_async_copy(room.at[i], ref.at[i], sems.at[base + i]) for i in range(shape[0])]))
            leaving += produced[-1][1]
            base += shape[0]
            at += 1
        kernel(*given, *produced, *rest)
        for item in given:
            if isinstance(item, Late):
                item.wait()
        for copy in leaving:
            copy.wait()

    moved = sum(int(np.prod(a.shape)) * a.dtype.itemsize for _, a in args)
    moved += sum(int(np.prod(shape)) * 4 for _, shape, _ in outs)
    return pl.pallas_call(
        wrapped,
        out_shape=[jax.ShapeDtypeStruct(shape, dtype) for _, shape, dtype in outs],
        in_specs=specs,
        out_specs=[pl.BlockSpec(memory_space=pltpu.VMEM if kind == "vmem" else pltpu.HBM) for kind, _, _ in outs],
        scratch_shapes=rooms
        + out_rooms
        + [pltpu.SemaphoreType.DMA((max(sum(counts) + out_parts, 1),))]
        + [pltpu.VMEM(shape, dtype) for shape, dtype in scratch],
        compiler_params=pltpu.CompilerParams(vmem_limit_bytes=VMEM_LIMIT),
        cost_estimate=pl.CostEstimate(flops=flops, bytes_accessed=moved, transcendentals=0),
    )(*[a for _, a in args])


def split(x):
    high = x.astype(bf16)
    return high, (x - high.astype(f32)).astype(bf16)


def pad_rows(x, rows):
    return x if x.shape[0] == rows else jnp.concatenate([x, jnp.zeros((rows - x.shape[0], x.shape[1]), x.dtype)], axis=0)


def stack(a):
    room = -a.shape[1] % LANES
    if room:
        a = jnp.concatenate([a, jnp.zeros((a.shape[0], room), a.dtype)], axis=1)
    return jnp.concatenate(split(a), axis=1)


def stacked_dot(a, x):
    xh, xl = split(x)
    rows = a.shape[1] // 2
    top = pad_rows(jnp.concatenate([xh, xl], axis=1), rows)
    low = pad_rows(jnp.concatenate([xh, jnp.zeros_like(xl)], axis=1), rows)
    both = jnp.dot(a, jnp.concatenate([top, low], axis=0), preferred_element_type=f32)
    return both[:, : x.shape[1]] + both[:, x.shape[1] :]


def dot(a, x):
    ah, al = a if isinstance(a, tuple) else split(a)
    xh, xl = split(x)
    n = x.shape[1]
    both = jnp.dot(ah, jnp.concatenate([xh, xl], axis=1), preferred_element_type=f32)
    return both[:, :n] + both[:, n:] + jnp.dot(al, xh, preferred_element_type=f32)


def small_dot(a, x):
    return jnp.dot(a, x, precision=highest, preferred_element_type=f32)


def face_of(state, e, face):
    if face == 0 or face == 1:
        start = 48 * face
        return jnp.concatenate([state[e, pl.ds(64 * v + start, 16)] for v in range(NVAR)], axis=0)
    if face >= 4:
        return state[e, pl.ds(3 * (face - 4), 80, stride=4)]
    half = 8 * (face - 2)
    first = jnp.concatenate([state[e, pl.ds(32 * m + half, 8)] for m in range(10)], axis=0)
    second = jnp.concatenate([state[e, pl.ds(32 * m + 16 + half, 8)] for m in range(10)], axis=0)
    low = lax.broadcasted_iota(jnp.int32, first.shape, 0) % 8 < 4
    if face == 2:
        return jnp.where(low, first, pltpu.roll(second, 4, 0))
    return jnp.where(low, pltpu.roll(first, 76, 0), second)


def link(ids, nbr, slots, e, face):
    g = nbr[e, face]
    owner = lax.div(g, slots)
    here = jnp.logical_and(g >= 0, owner == ids[2])
    away = jnp.logical_and(g >= 0, owner != ids[2])
    return here, away, jnp.maximum(lax.rem(g, slots), 0)


def crossing(ids, nbr, slots, face):
    found, slot = False, 0
    for e in range(slots):
        _, away, _ = link(ids, nbr, slots, e, face)
        found = jnp.logical_or(found, away)
        slot = jnp.where(away, e, slot)
    return found, slot


def swap_of(ids, face):
    return lax.rem(face % 2 + ids[face // 2] % 2 + 1, 2)


def fill_masks(ids, nbr, slots, masks):
    for i in range(4):
        for side in range(2):
            f = 2 * (i // 2) + side
            for e in range(slots):
                _, away, _ = link(ids, nbr, slots, e, f)
                value = jnp.where(jnp.logical_and(away, swap_of(ids, f) == i % 2), 1.0, 0.0)
                masks[(2 * i + side) * slots + e] = jnp.full(masks.shape[1:], value, f32)


def masked(mask, x):
    return (x.reshape(-1, *mask.shape) * mask).reshape(x.shape)


def meets(masks, slots, i, e):
    return masks[2 * i * slots + e] + masks[(2 * i + 1) * slots + e]


def crossing_traces(state):
    return [[face_of(state, e, f) for e in range(state.shape[0])] for f in range(4)]


def fill_traces(masks, traces, sends):
    slots = len(traces[0])
    for i in range(4):
        terms = [
            masked(masks[(2 * i + side) * slots + e], traces[2 * (i // 2) + side][e])
            for side in range(2)
            for e in range(slots)
        ]
        sends[i][...] = sum(terms[1:], terms[0])


def fill_elements(masks, w, sends):
    slots = w.shape[0]
    for i in range(4):
        terms = [masked(meets(masks, slots, i, e), w[e]) for e in range(slots)]
        sends[i][...] = sum(terms[1:], terms[0])


def first_kernel(rhs, given, v, inverses):
    for e in range(rhs.shape[0]):
        inverses[e] = stack(given[e])
        v[e] = damping * stacked_dot(inverses[e], rhs[e])


def send_kernel(ids, nbr, v, s0, s1, s2, s3, masks):
    traces = crossing_traces(v)
    fill_masks(ids, nbr, v.shape[0], masks)
    fill_traces(masks, traces, (s0, s1, s2, s3))


def local_residual(ids, nbr, rhs, state, blocks, lifts, coef, out, traces):
    slots, _, columns = state.shape
    for e in range(slots):
        out[e] = rhs[e] - stacked_dot(blocks[e], state[e])
        for f in range(6):
            traces[f * slots + e] = face_of(state, e, f)
    near = []
    for e in range(slots):
        parts = []
        for f in range(6):
            here, _, s = link(ids, nbr, slots, e, f)
            t = traces[(f ^ 1) * slots + s] * coef[e, pl.ds(80 * f, 80)]
            parts.append(jnp.where(here, t, 0.0))
        near.append(jnp.concatenate(parts, axis=0))
    coupled = dot(lifts, jnp.concatenate(near, axis=1))
    for e in range(slots):
        out[e] = out[e] - coupled[:, e * columns : (e + 1) * columns]


def lay_out(lifts_t, coefs, lh, ll, coef):
    faces, nface, nf = lifts_t.shape
    slots = coef.shape[0]
    whole = jnp.concatenate([lifts_t[f] for f in range(faces)], axis=0).T
    lh[...], ll[...] = split(whole)
    turned = coefs[...].T
    for e in range(slots):
        for f in range(faces):
            column = turned[:, f * slots + e : f * slots + e + 1]
            coef[e, nface * f : nface * (f + 1)] = jnp.broadcast_to(column, (nface, coef.shape[2]))


def lay_out_far(ids, nbr, lifts_t, coef, far_lifts):
    nface, slots = lifts_t.shape[1], coef.shape[0]
    for i in range(4):
        low = 2 * (i // 2)
        first = swap_of(ids, low) == i % 2
        scaled = []
        for f in (low, low + 1):
            _, slot = crossing(ids, nbr, slots, f)
            scaled.append(lifts_t[f] * coef[slot, pl.ds(nface * f, nface)][:, :1])
        scaled = jnp.where(first, scaled[0], scaled[1])
        high = scaled.astype(bf16).astype(f32)
        far_lifts[i] = jnp.concatenate([high, scaled - high], axis=0).T.astype(bf16)


def first_local_kernel(
    ids, nbr, state, lifts_t, coefs, given, rhs, out, lh, ll, far_lifts, coef, blocks, traces
):
    lay_out(lifts_t, coefs, lh, ll, coef)
    for e in range(given.shape[0]):
        blocks[e] = stack(given[e])

    local_residual(
        ids, nbr, rhs, state, blocks, (lh[...], ll[...]), coef, out, traces
    )
    lay_out_far(ids, nbr, lifts_t, coef, far_lifts)


def local_kernel(ids, nbr, state, lh, ll, blocks, coef, rhs, out, traces):
    local_residual(ids, nbr, rhs, state, blocks, (lh[...], ll[...]), coef, out, traces)


def less_remote(masks, res, parts, e):
    slots = masks.shape[0] // 8
    for i, part in enumerate(parts):
        res = res - masked(meets(masks, slots, i, e), part)
    return res


def sweep_kernel(masks, y0, y1, y3, y2, res, state, far_lifts, inverses, v, *sends):
    parts = [stacked_dot(far_lifts[i], y[...]) for i, y in enumerate((y0, y1, y2, y3))]
    for e in range(res.shape[0]):
        value = state[e] + damping * stacked_dot(inverses[e], less_remote(masks, res[e], parts, e))
        if sends:
            v[e] = value
        else:
            v[0][e] = value
            v[1][e].start()
    if sends:
        fill_traces(masks, crossing_traces(v), sends)


def restrict_kernel(masks, y0, y1, y3, y2, res, far_lifts, restrict, inverses, _, r, rhs, w, *sends):
    parts = [stacked_dot(far_lifts[i], y[...]) for i, y in enumerate((y0, y1, y2, y3))]
    for e in range(r.shape[0]):
        left = less_remote(masks, res[e], parts, e)
        r[e] = left
        rhs[e] = 0.25 * dot(restrict[...], left)
        w[e] = damping * dot(inverses[e], rhs[e])
    fill_elements(masks, w, sends)


def prolong_kernel(ids, nbr, r, state, w, lh, ll, blocks, coef, prolong, out, corrected, traces, correction):
    slots = state.shape[0]
    columns = state.shape[2]
    raised = dot(prolong[...], jnp.concatenate([w[e] for e in range(slots)], axis=1))
    for e in range(slots):
        correction[e] = raised[:, e * columns : (e + 1) * columns]
        corrected[e] = state[e] + correction[e]
    local_residual(
        ids, nbr, r, correction, blocks, (lh[...], ll[...]), coef, out, traces
    )


def post_kernel(masks, y0, y1, y3, y2, res, state, far_prolong, inverses, v, *sends):
    parts = [stacked_dot(far_prolong[i], y[...]) for i, y in enumerate((y0, y1, y2, y3))]
    for e in range(res.shape[0]):
        v[e] = state[e] + damping * stacked_dot(inverses[e], less_remote(masks, res[e], parts, e))
    fill_traces(masks, crossing_traces(v), sends)


def coarse_lay_out_kernel(lifts_t, coefs, hot_lifts, hot_coefs, _, lifts, coef, wide):
    faces, _, nc = lifts_t.shape
    slots = coef.shape[0]
    spread = small_dot(hot_coefs[...], coefs[...].T)
    rows = small_dot(hot_lifts[...], jnp.concatenate([lifts_t[f] for f in range(faces)], axis=0))
    lifts[...] = rows.T
    for f in range(faces):
        wide[f] = rows[nc * f : nc * (f + 1)]
        for e in range(slots):
            column = spread[nc * f : nc * (f + 1), f * slots + e : f * slots + e + 1]
            coef[e, nc * f : nc * (f + 1)] = jnp.broadcast_to(column, (nc, coef.shape[2]))


def far_prolong_kernel(masks, far_lifts, face_prolong, _, far_prolong):
    slots = masks.shape[0] // 8
    for i in range(4):
        total = None
        for side in range(2):
            on = sum(masks[(2 * i + side) * slots + e] for e in range(slots))
            term = masked(on, face_prolong[2 * (i // 2) + 1 - side])
            total = term if total is None else total + term
        far_prolong[i] = jnp.concatenate(split(stacked_dot(far_lifts[i], total)), axis=1)


def coarse_remote_kernel(masks, wide, coef, inverses, remote):
    slots, nc, _ = inverses.shape
    for e in range(slots):
        scaled = []
        for i in range(4):
            total = None
            for side in range(2):
                f = 2 * (i // 2) + side
                term = masked(masks[(2 * i + side) * slots + e], coef[e, nc * f : nc * (f + 1)])
                term = wide[f] * term[:, :nc]
                total = term if total is None else total + term
            scaled.append(total)
        rows = damping * small_dot(inverses[e], jnp.concatenate(scaled, axis=0).T)
        remote[e * nc : (e + 1) * nc] = rows


def coarse_local_kernel(ids, nbr, w, rhs, blocks, inverses, lifts, coef, out):
    slots, nc, columns = w.shape
    for e in range(slots):
        out[e] = rhs[e] - dot(blocks[e], w[e])
    near = []
    for e in range(slots):
        parts = []
        for f in range(6):
            here, _, s = link(ids, nbr, slots, e, f)
            parts.append(jnp.where(here, w[s] * coef[e, nc * f : nc * (f + 1)], 0.0))
        near.append(jnp.concatenate(parts, axis=0))
    coupled = dot(lifts[...], jnp.concatenate(near, axis=1))
    for e in range(slots):
        res = out[e] - coupled[:, e * columns : (e + 1) * columns]
        out[e] = w[e] + damping * dot(inverses[e], res)


def coarse_sweep_kernel(masks, y0, y1, y3, y2, local, remote, w, *sends):
    slots, nc, _ = w.shape
    far = dot(remote[...], jnp.concatenate([y[...] for y in (y0, y1, y2, y3)], axis=0))
    for e in range(slots):
        w[e] = local[e] - far[e * nc : (e + 1) * nc]
    fill_elements(masks, w, sends)


def swap(parts):
    got = []
    for i in (0, 1, 3, 2):
        axis = AXES[i // 2]
        pairs = []
        for a in range(i % 2, lax.axis_size(axis) - 1, 2):
            pairs += [(a, a + 1), (a + 1, a)]
        got.append(lax.ppermute(parts[i], axis, pairs))
    return got


def body(
    right_side,
    fine_blocks,
    fine_inverses,
    fine_lifts,
    fine_coefs,
    coarse_blocks,
    coarse_inverses,
    coarse_lifts,
    coarse_coefs,
    neighbours,
    counts,
):
    slots, nf, columns = right_side.shape
    nface = fine_lifts.shape[2]
    nc = coarse_blocks.shape[1]
    ncf = coarse_lifts.shape[2]
    wide_here, narrow_here = lax.axis_index("wide"), lax.axis_index("narrow")
    ids = jnp.stack([wide_here, narrow_here, wide_here * lax.axis_size("narrow") + narrow_here]).astype(jnp.int32)

    live = (jnp.arange(slots) < counts[0]).astype(f32)
    rhs_live = right_side * live[:, None, None]

    prolong_np = prolong_table(NODE1, NVAR)
    coarse_table = face_rows(2, NVAR)
    fine_table = face_rows(NODE1, NVAR)
    prolong = jnp.asarray(prolong_np)
    restrict = jnp.asarray(np.ascontiguousarray(prolong_np.T))
    face_prolong = np.stack([prolong_np[fine_table[f]] for f in range(4)])
    face_prolong = jnp.asarray(np.pad(face_prolong, ((0, 0), (0, 0), (0, LANES - nc))))
    hot_lifts = np.zeros((6, nc, 6, ncf), np.float32)
    hot_coefs = np.zeros((6, nc, ncf), np.float32)
    for f in range(6):
        hot_lifts[f, coarse_table[f ^ 1], f, np.arange(ncf)] = 1.0
        hot_coefs[f, coarse_table[f ^ 1], np.arange(ncf)] = 1.0
    hot_lifts = jnp.asarray(hot_lifts.reshape(6 * nc, 6 * ncf))
    hot_coefs = jnp.asarray(hot_coefs.reshape(6 * nc, ncf))

    lifts_t = fine_lifts.transpose(0, 2, 1)
    coefs = fine_coefs.transpose(1, 0, 2).reshape(6 * slots, nface)
    coarse_lifts_t = coarse_lifts.transpose(0, 2, 1)
    coarse_coefs_t = coarse_coefs.transpose(1, 0, 2).reshape(6 * slots, ncf)

    field = ("vmem", (slots, nf, columns), f32)
    faces = [("vmem", (nface, columns), f32)] * 4
    coarse = ("vmem", (slots, nc, columns), f32)
    coarse_sends = [("vmem", (nc, columns), f32)] * 4
    trace_room = ((6 * slots, nface, columns), f32)
    field_room = (field[1], f32)
    block_flops = 3 * 2 * slots * nf * nf * columns
    lift_flops = 3 * 2 * slots * nf * 6 * nface * columns
    where = [("late", ids), ("late", neighbours)]

    def vm(*arrays):
        return [("vmem", a) for a in arrays]

    def parts(*arrays):
        return [("parts", a) for a in arrays]

    wide = 2 * (nf + -nf % LANES)
    matrix = ("vmem", (slots, nf, wide), bf16)
    mask_tiles = ("vmem", (8 * slots, 8, columns), f32)
    state, inverses = call(
        first_kernel, [field, matrix], [], vm(rhs_live, fine_inverses), 8 * block_flops
    )
    *sends, masks = call(send_kernel, faces + [mask_tiles], [], where + vm(state))
    got = swap(sends)
    res, lh, ll, far_lifts, coef, blocks = call(
        first_local_kernel,
        [field]
        + [("vmem", (nf, 6 * nface), bf16)] * 2
        + [("vmem", (4, nf, 2 * nface), bf16), ("vmem", (slots, 6 * nface, columns), f32), matrix],
        [trace_room],
        where + vm(state, lifts_t, coefs, fine_blocks, rhs_live),
        block_flops + lift_flops,
    )

    def local(state):
        return call(
            local_kernel, [field], [trace_room],
            where + vm(state, lh, ll, blocks, coef, rhs_live), block_flops + lift_flops,
        )[0]

    def sweep(got, res, state, last):
        return call(
            sweep_kernel, [("hbm",) + field[1:]] if last else [field] + faces, [],
            vm(masks, *got, res, state, far_lifts, inverses), block_flops,
        )

    for i in range(PRE_SWEEPS - 1):
        state, *sends = sweep(got, res, state, False)
        got = swap(sends)
        res = local(state)
    coarse_wide, coarse_coef, coarse_faces = call(
        coarse_lay_out_kernel,
        [("vmem", (nc, 6 * nc), f32), ("vmem", (slots, 6 * nc, columns), f32), ("vmem", (6, nc, nc), f32)], [],
        vm(coarse_lifts_t, coarse_coefs_t, hot_lifts, hot_coefs, state),
    )
    residual, coarse_rhs, w, *sends = call(
        restrict_kernel, [field, coarse, coarse] + coarse_sends, [],
        vm(masks, *got, res, far_lifts, restrict, coarse_inverses, coarse_wide),
    )
    (coarse_remote,) = call(
        coarse_remote_kernel, [("vmem", (slots * nc, 4 * nc), f32)], [],
        vm(masks, coarse_faces, coarse_coef, coarse_inverses),
    )
    far_prolong = None
    for _ in range(COARSE_SWEEPS - 1):
        got = swap(sends)
        (w_local,) = call(
            coarse_local_kernel, [coarse], [],
            where + vm(w, coarse_rhs, coarse_blocks, coarse_inverses, coarse_wide, coarse_coef),
        )
        w, *sends = call(
            coarse_sweep_kernel, [coarse] + coarse_sends, [], vm(masks, *got, w_local, coarse_remote)
        )
        if far_prolong is None:
            (far_prolong,) = call(
                far_prolong_kernel, [("vmem", (4, nf, 2 * LANES), bf16)], [], vm(masks, far_lifts, face_prolong, w)
            )
    got = swap(sends)
    res, state = call(
        prolong_kernel, [field, field], [trace_room, field_room],
        where + vm(residual, state, w, lh, ll, blocks, coef, prolong),
        block_flops + lift_flops,
    )
    state, *sends = call(
        post_kernel, [field] + faces, [],
        vm(masks, *got, res, state, far_prolong, inverses), block_flops,
    )
    for i in range(POST_SWEEPS - 1):
        got = swap(sends)
        res = local(state)
        state, *sends = sweep(got, res, state, i == POST_SWEEPS - 2)
    return state


def solution(mesh):
    placed = (
        P(AXES, None, None),
        P(AXES, None, None),
        P(AXES, None, None),
        P(),
        P(AXES, None, None),
        P(AXES, None, None),
        P(AXES, None, None),
        P(),
        P(AXES, None, None),
        P(AXES, None),
        P(AXES),
    )
    return jax.shard_map(
        body,
        mesh=mesh,
        in_specs=placed,
        out_specs=P(AXES, None, None),
        check_vma=False,
    )
```

```python
import functools

import jax
import jax.numpy as jnp
import numpy as np
from jax import lax
from jax.experimental import pallas as pl
from jax.experimental.pallas import tpu as pltpu
from jax.sharding import PartitionSpec as P

NVAR = 5
NODE1 = 4
PRE_SWEEPS = 2
POST_SWEEPS = 2
COARSE_SWEEPS = 4
AXES = ("wide", "narrow")
LANES = 128
VMEM_LIMIT = 16 * 1024 * 1024

damping = 0.8
highest = lax.Precision.HIGHEST
f32, bf16 = jnp.float32, jnp.bfloat16


def prolong_table(node_count, variables):
    points = np.array([-1.0, -1.0 / np.sqrt(5.0), 1.0 / np.sqrt(5.0), 1.0])
    linear = np.stack([(1.0 - points) / 2.0, (1.0 + points) / 2.0], axis=1)
    tensor_hat = (
        linear[:, None, None, :, None, None]
        * linear[None, :, None, None, :, None]
        * linear[None, None, :, None, None, :]
    )
    tensor_hat = tensor_hat.reshape(node_count * node_count * node_count, 8)
    return np.kron(np.eye(variables), tensor_hat).astype(np.float32)


def face_rows(node_count, variables):
    cube = node_count**3
    lattice = np.arange(cube).reshape(node_count, node_count, node_count)
    tables = []
    for face in range(6):
        layer = np.take(lattice, 0 if face % 2 == 0 else node_count - 1, axis=face // 2).reshape(-1)
        tables.append(np.concatenate([layer + v * cube for v in range(variables)]))
    return np.stack(tables)


class Late:
    def __init__(self, source, room, sem):
        self.room, self.copy, self.ready = room, pltpu.make_async_copy(source, room, sem), False
        self.copy.start()

    def wait(self):
        if not self.ready:
            self.ready = True
            self.copy.wait()

    def __getitem__(self, index):
        self.wait()
        return self.room[index]


def call(kernel, outs, scratch, args, flops=0):
    specs, rooms, counts = [], [], []
    for kind, a in args:
        if kind in ("smem", "vmem"):
            specs.append(pl.BlockSpec(memory_space=pltpu.SMEM if kind == "smem" else pltpu.VMEM))
        else:
            specs.append(pl.BlockSpec(memory_space=pl.ANY))
            rooms.append(pltpu.SMEM(a.shape, a.dtype))
            counts.append(1)
    out_rooms = [pltpu.VMEM(shape, dtype) for kind, shape, dtype in outs if kind == "hbm"]
    out_parts = sum(shape[0] for kind, shape, _ in outs if kind == "hbm")
    n_in, n_out, n_rooms = len(args), len(outs), len(rooms)

    def wrapped(*refs):
        ins, results, rest = refs[:n_in], refs[n_in : n_in + n_out], refs[n_in + n_out :]
        in_rooms, rest = rest[:n_rooms], rest[n_rooms:]
        result_rooms, rest = rest[: len(out_rooms)], rest[len(out_rooms) :]
        sems, rest = rest[0], rest[1:]
        given, base, at = [], 0, 0
        for (kind, _), ref in zip(args, ins):
            if kind in ("smem", "vmem"):
                given.append(ref)
                continue
            given.append(Late(ref, in_rooms[at], sems.at[base]))
            base += 1
            at += 1
        leaving, produced, at = [], [], 0
        for (kind, shape, _), ref in zip(outs, results):
            if kind == "vmem":
                produced.append(ref)
                continue
            room = result_rooms[at]
            produced.append((room, [pltpu.make_async_copy(room.at[i], ref.at[i], sems.at[base + i]) for i in range(shape[0])]))
            leaving += produced[-1][1]
            base += shape[0]
            at += 1
        kernel(*given, *produced, *rest)
        for item in given:
            if isinstance(item, Late):
                item.wait()
        for copy in leaving:
            copy.wait()

    moved = sum(int(np.prod(a.shape)) * a.dtype.itemsize for _, a in args)
    moved += sum(int(np.prod(shape)) * 4 for _, shape, _ in outs)
    return pl.pallas_call(
        wrapped,
        out_shape=[jax.ShapeDtypeStruct(shape, dtype) for _, shape, dtype in outs],
        in_specs=specs,
        out_specs=[pl.BlockSpec(memory_space=pltpu.VMEM if kind == "vmem" else pltpu.HBM) for kind, _, _ in outs],
        scratch_shapes=rooms
        + out_rooms
        + [pltpu.SemaphoreType.DMA((max(sum(counts) + out_parts, 1),))]
        + [pltpu.VMEM(shape, dtype) for shape, dtype in scratch],
        compiler_params=pltpu.CompilerParams(vmem_limit_bytes=VMEM_LIMIT),
        cost_estimate=pl.CostEstimate(flops=flops, bytes_accessed=moved, transcendentals=0),
    )(*[a for _, a in args])


def split(x):
    high = x.astype(bf16)
    return high, (x - high.astype(f32)).astype(bf16)


def pad_rows(x, rows):
    return x if x.shape[0] == rows else jnp.concatenate([x, jnp.zeros((rows - x.shape[0], x.shape[1]), x.dtype)], axis=0)


def stack(a):
    room = -a.shape[1] % LANES
    if room:
        a = jnp.concatenate([a, jnp.zeros((a.shape[0], room), a.dtype)], axis=1)
    return jnp.concatenate(split(a), axis=1)


def stacked_dot(a, x):
    xh, xl = split(x)
    rows = a.shape[1] // 2
    top = pad_rows(jnp.concatenate([xh, xl], axis=1), rows)
    low = pad_rows(jnp.concatenate([xh, jnp.zeros_like(xl)], axis=1), rows)
    both = jnp.dot(a, jnp.concatenate([top, low], axis=0), preferred_element_type=f32)
    return both[:, : x.shape[1]] + both[:, x.shape[1] :]


def dot(a, x):
    ah, al = a if isinstance(a, tuple) else split(a)
    xh, xl = split(x)
    n = x.shape[1]
    both = jnp.dot(ah, jnp.concatenate([xh, xl], axis=1), preferred_element_type=f32)
    return both[:, :n] + both[:, n:] + jnp.dot(al, xh, preferred_element_type=f32)


def small_dot(a, x):
    return jnp.dot(a, x, precision=highest, preferred_element_type=f32)


def face_of(state, e, face):
    if face == 0 or face == 1:
        start = 48 * face
        return jnp.concatenate([state[e, pl.ds(64 * v + start, 16)] for v in range(NVAR)], axis=0)
    if face >= 4:
        return state[e, pl.ds(3 * (face - 4), 80, stride=4)]
    half = 8 * (face - 2)
    first = jnp.concatenate([state[e, pl.ds(32 * m + half, 8)] for m in range(10)], axis=0)
    second = jnp.concatenate([state[e, pl.ds(32 * m + 16 + half, 8)] for m in range(10)], axis=0)
    low = lax.broadcasted_iota(jnp.int32, first.shape, 0) % 8 < 4
    if face == 2:
        return jnp.where(low, first, pltpu.roll(second, 4, 0))
    return jnp.where(low, pltpu.roll(first, 76, 0), second)


def link(ids, nbr, slots, e, face):
    g = nbr[e, face]
    owner = lax.div(g, slots)
    here = jnp.logical_and(g >= 0, owner == ids[2])
    away = jnp.logical_and(g >= 0, owner != ids[2])
    return here, away, jnp.maximum(lax.rem(g, slots), 0)


def crossing(ids, nbr, slots, face):
    found, slot = False, 0
    for e in range(slots):
        _, away, _ = link(ids, nbr, slots, e, face)
        found = jnp.logical_or(found, away)
        slot = jnp.where(away, e, slot)
    return found, slot


def swap_of(ids, face):
    return lax.rem(face % 2 + ids[face // 2] % 2 + 1, 2)


def fill_masks(ids, nbr, slots, masks):
    for i in range(4):
        for side in range(2):
            f = 2 * (i // 2) + side
            for e in range(slots):
                _, away, _ = link(ids, nbr, slots, e, f)
                value = jnp.where(jnp.logical_and(away, swap_of(ids, f) == i % 2), 1.0, 0.0)
                masks[(2 * i + side) * slots + e] = jnp.full(masks.shape[1:], value, f32)


def masked(mask, x):
    return (x.reshape(-1, *mask.shape) * mask).reshape(x.shape)


def meets(masks, slots, i, e):
    return masks[2 * i * slots + e] + masks[(2 * i + 1) * slots + e]


def crossing_traces(state):
    return [[face_of(state, e, f) for e in range(state.shape[0])] for f in range(4)]


def fill_traces(masks, traces, sends):
    slots = len(traces[0])
    for i in range(4):
        terms = [
            masked(masks[(2 * i + side) * slots + e], traces[2 * (i // 2) + side][e])
            for side in range(2)
            for e in range(slots)
        ]
        sends[i][...] = sum(terms[1:], terms[0])


def fill_elements(masks, w, sends):
    slots = w.shape[0]
    for i in range(4):
        terms = [masked(meets(masks, slots, i, e), w[e]) for e in range(slots)]
        sends[i][...] = sum(terms[1:], terms[0])


def mask_kernel(ids, nbr, masks):
    fill_masks(ids, nbr, nbr.room.shape[0], masks)


def first_kernel(counts, masks, rhs, given, v, live, inverses, *sends):
    for e in range(rhs.shape[0]):
        live[e] = jnp.where(e < counts[0], rhs[e], 0.0)
        inverses[e] = stack(given[e])
        v[e] = damping * stacked_dot(inverses[e], live[e])
    fill_traces(masks, crossing_traces(v), sends)


def local_residual(ids, nbr, rhs, state, blocks, lifts, coef, out, traces):
    slots, _, columns = state.shape
    for e in range(slots):
        out[e] = rhs[e] - stacked_dot(blocks[e], state[e])
        for f in range(6):
            traces[f * slots + e] = face_of(state, e, f)
    near = []
    for e in range(slots):
        parts = []
        for f in range(6):
            here, _, s = link(ids, nbr, slots, e, f)
            t = traces[(f ^ 1) * slots + s] * coef[e, pl.ds(80 * f, 80)]
            parts.append(jnp.where(here, t, 0.0))
        near.append(jnp.concatenate(parts, axis=0))
    coupled = dot(lifts, jnp.concatenate(near, axis=1))
    for e in range(slots):
        out[e] = out[e] - coupled[:, e * columns : (e + 1) * columns]


def lay_out(lifts_t, coefs, lh, ll, coef):
    faces, nface, nf = lifts_t.shape
    slots = coef.shape[0]
    whole = jnp.concatenate([lifts_t[f] for f in range(faces)], axis=0).T
    lh[...], ll[...] = split(whole)
    turned = coefs[...].T
    for e in range(slots):
        for f in range(faces):
            column = turned[:, f * slots + e : f * slots + e + 1]
            coef[e, nface * f : nface * (f + 1)] = jnp.broadcast_to(column, (nface, coef.shape[2]))


def lay_out_far(ids, nbr, lifts_t, coef, far_lifts):
    nface, slots = lifts_t.shape[1], coef.shape[0]
    for i in range(4):
        low = 2 * (i // 2)
        first = swap_of(ids, low) == i % 2
        scaled = []
        for f in (low, low + 1):
            _, slot = crossing(ids, nbr, slots, f)
            scaled.append(lifts_t[f] * coef[slot, pl.ds(nface * f, nface)][:, :1])
        scaled = jnp.where(first, scaled[0], scaled[1])
        high = scaled.astype(bf16).astype(f32)
        far_lifts[i] = jnp.concatenate([high, scaled - high], axis=0).T.astype(bf16)


def first_local_kernel(
    ids, nbr, state, lifts_t, coefs, given, rhs, out, lh, ll, far_lifts, coef, blocks, traces
):
    lay_out(lifts_t, coefs, lh, ll, coef)
    for e in range(given.shape[0]):
        blocks[e] = stack(given[e])

    local_residual(
        ids, nbr, rhs, state, blocks, (lh[...], ll[...]), coef, out, traces
    )
    lay_out_far(ids, nbr, lifts_t, coef, far_lifts)


def local_kernel(ids, nbr, state, lh, ll, blocks, coef, rhs, out, traces):
    local_residual(ids, nbr, rhs, state, blocks, (lh[...], ll[...]), coef, out, traces)


def less_remote(masks, res, parts, e):
    slots = masks.shape[0] // 8
    for i, part in enumerate(parts):
        res = res - masked(meets(masks, slots, i, e), part)
    return res


def sweep_kernel(masks, y0, y1, y3, y2, res, state, far_lifts, inverses, v, *sends):
    parts = [stacked_dot(far_lifts[i], y[...]) for i, y in enumerate((y0, y1, y2, y3))]
    for e in range(res.shape[0]):
        value = state[e] + damping * stacked_dot(inverses[e], less_remote(masks, res[e], parts, e))
        if sends:
            v[e] = value
        else:
            v[0][e] = value
            v[1][e].start()
    if sends:
        fill_traces(masks, crossing_traces(v), sends)


def restrict_kernel(masks, y0, y1, y3, y2, res, far_lifts, restrict, inverses, _, r, rhs, w, *sends):
    parts = [stacked_dot(far_lifts[i], y[...]) for i, y in enumerate((y0, y1, y2, y3))]
    for e in range(r.shape[0]):
        left = less_remote(masks, res[e], parts, e)
        r[e] = left
        rhs[e] = 0.25 * dot(restrict[...], left)
        w[e] = damping * dot(inverses[e], rhs[e])
    fill_elements(masks, w, sends)


def prolong_kernel(ids, nbr, r, state, w, lh, ll, blocks, coef, prolong, out, corrected, traces, correction):
    slots = state.shape[0]
    columns = state.shape[2]
    raised = dot(prolong[...], jnp.concatenate([w[e] for e in range(slots)], axis=1))
    for e in range(slots):
        correction[e] = raised[:, e * columns : (e + 1) * columns]
        corrected[e] = state[e] + correction[e]
    local_residual(
        ids, nbr, r, correction, blocks, (lh[...], ll[...]), coef, out, traces
    )


def post_kernel(masks, y0, y1, y3, y2, res, state, far_prolong, inverses, v, *sends):
    parts = [stacked_dot(far_prolong[i], y[...]) for i, y in enumerate((y0, y1, y2, y3))]
    for e in range(res.shape[0]):
        v[e] = state[e] + damping * stacked_dot(inverses[e], less_remote(masks, res[e], parts, e))
    fill_traces(masks, crossing_traces(v), sends)


def coarse_lay_out_kernel(lifts_t, coefs, hot_lifts, hot_coefs, _, lifts, coef, wide):
    faces, _, nc = lifts_t.shape
    slots = coef.shape[0]
    spread = small_dot(hot_coefs[...], coefs[...].T)
    rows = small_dot(hot_lifts[...], jnp.concatenate([lifts_t[f] for f in range(faces)], axis=0))
    lifts[...] = rows.T
    for f in range(faces):
        wide[f] = rows[nc * f : nc * (f + 1)]
        for e in range(slots):
            column = spread[nc * f : nc * (f + 1), f * slots + e : f * slots + e + 1]
            coef[e, nc * f : nc * (f + 1)] = jnp.broadcast_to(column, (nc, coef.shape[2]))


def far_prolong_kernel(masks, far_lifts, face_prolong, _, far_prolong):
    slots = masks.shape[0] // 8
    for i in range(4):
        total = None
        for side in range(2):
            on = sum(masks[(2 * i + side) * slots + e] for e in range(slots))
            term = masked(on, face_prolong[2 * (i // 2) + 1 - side])
            total = term if total is None else total + term
        far_prolong[i] = jnp.concatenate(split(stacked_dot(far_lifts[i], total)), axis=1)


def coarse_remote_kernel(masks, wide, coef, inverses, remote):
    slots, nc, _ = inverses.shape
    for e in range(slots):
        scaled = []
        for i in range(4):
            total = None
            for side in range(2):
                f = 2 * (i // 2) + side
                term = masked(masks[(2 * i + side) * slots + e], coef[e, nc * f : nc * (f + 1)])
                term = wide[f] * term[:, :nc]
                total = term if total is None else total + term
            scaled.append(total)
        rows = damping * small_dot(inverses[e], jnp.concatenate(scaled, axis=0).T)
        remote[e * nc : (e + 1) * nc] = rows


def coarse_local_kernel(ids, nbr, w, rhs, blocks, inverses, lifts, coef, out):
    slots, nc, columns = w.shape
    for e in range(slots):
        out[e] = rhs[e] - dot(blocks[e], w[e])
    near = []
    for e in range(slots):
        parts = []
        for f in range(6):
            here, _, s = link(ids, nbr, slots, e, f)
            parts.append(jnp.where(here, w[s] * coef[e, nc * f : nc * (f + 1)], 0.0))
        near.append(jnp.concatenate(parts, axis=0))
    coupled = dot(lifts[...], jnp.concatenate(near, axis=1))
    for e in range(slots):
        res = out[e] - coupled[:, e * columns : (e + 1) * columns]
        out[e] = w[e] + damping * dot(inverses[e], res)


def coarse_sweep_kernel(masks, y0, y1, y3, y2, local, remote, w, *sends):
    slots, nc, _ = w.shape
    far = dot(remote[...], jnp.concatenate([y[...] for y in (y0, y1, y2, y3)], axis=0))
    for e in range(slots):
        w[e] = local[e] - far[e * nc : (e + 1) * nc]
    fill_elements(masks, w, sends)


def swap(parts):
    got = []
    for i in (0, 1, 3, 2):
        axis = AXES[i // 2]
        pairs = []
        for a in range(i % 2, lax.axis_size(axis) - 1, 2):
            pairs += [(a, a + 1), (a + 1, a)]
        got.append(lax.ppermute(parts[i], axis, pairs))
    return got


def body(
    right_side,
    fine_blocks,
    fine_inverses,
    fine_lifts,
    fine_coefs,
    coarse_blocks,
    coarse_inverses,
    coarse_lifts,
    coarse_coefs,
    neighbours,
    counts,
):
    slots, nf, columns = right_side.shape
    nface = fine_lifts.shape[2]
    nc = coarse_blocks.shape[1]
    ncf = coarse_lifts.shape[2]
    wide_here, narrow_here = lax.axis_index("wide"), lax.axis_index("narrow")
    ids = jnp.stack([wide_here, narrow_here, wide_here * lax.axis_size("narrow") + narrow_here]).astype(jnp.int32)

    prolong_np = prolong_table(NODE1, NVAR)
    coarse_table = face_rows(2, NVAR)
    fine_table = face_rows(NODE1, NVAR)
    prolong = jnp.asarray(prolong_np)
    restrict = jnp.asarray(np.ascontiguousarray(prolong_np.T))
    face_prolong = np.stack([prolong_np[fine_table[f]] for f in range(4)])
    face_prolong = jnp.asarray(np.pad(face_prolong, ((0, 0), (0, 0), (0, LANES - nc))))
    hot_lifts = np.zeros((6, nc, 6, ncf), np.float32)
    hot_coefs = np.zeros((6, nc, ncf), np.float32)
    for f in range(6):
        hot_lifts[f, coarse_table[f ^ 1], f, np.arange(ncf)] = 1.0
        hot_coefs[f, coarse_table[f ^ 1], np.arange(ncf)] = 1.0
    hot_lifts = jnp.asarray(hot_lifts.reshape(6 * nc, 6 * ncf))
    hot_coefs = jnp.asarray(hot_coefs.reshape(6 * nc, ncf))

    lifts_t = fine_lifts.transpose(0, 2, 1)
    coefs = fine_coefs.transpose(1, 0, 2).reshape(6 * slots, nface)
    coarse_lifts_t = coarse_lifts.transpose(0, 2, 1)
    coarse_coefs_t = coarse_coefs.transpose(1, 0, 2).reshape(6 * slots, ncf)

    field = ("vmem", (slots, nf, columns), f32)
    faces = [("vmem", (nface, columns), f32)] * 4
    coarse = ("vmem", (slots, nc, columns), f32)
    coarse_sends = [("vmem", (nc, columns), f32)] * 4
    trace_room = ((6 * slots, nface, columns), f32)
    field_room = (field[1], f32)
    block_flops = 3 * 2 * slots * nf * nf * columns
    lift_flops = 3 * 2 * slots * nf * 6 * nface * columns
    where = [("late", ids), ("late", neighbours)]

    def vm(*arrays):
        return [("vmem", a) for a in arrays]

    def parts(*arrays):
        return [("parts", a) for a in arrays]

    wide = 2 * (nf + -nf % LANES)
    matrix = ("vmem", (slots, nf, wide), bf16)
    mask_tiles = ("vmem", (8 * slots, 8, columns), f32)
    (masks,) = call(mask_kernel, [mask_tiles], [], where, 8 * block_flops)
    state, rhs_live, inverses, *sends = call(
        first_kernel, [field, field, matrix] + faces, [],
        [("smem", counts)] + vm(masks, right_side, fine_inverses), 8 * block_flops,
    )
    got = swap(sends)
    res, lh, ll, far_lifts, coef, blocks = call(
        first_local_kernel,
        [field]
        + [("vmem", (nf, 6 * nface), bf16)] * 2
        + [("vmem", (4, nf, 2 * nface), bf16), ("vmem", (slots, 6 * nface, columns), f32), matrix],
        [trace_room],
        where + vm(state, lifts_t, coefs, fine_blocks, rhs_live),
        block_flops + lift_flops,
    )

    def local(state):
        return call(
            local_kernel, [field], [trace_room],
            where + vm(state, lh, ll, blocks, coef, rhs_live), block_flops + lift_flops,
        )[0]

    def sweep(got, res, state, last):
        return call(
            sweep_kernel, [("hbm",) + field[1:]] if last else [field] + faces, [],
            vm(masks, *got, res, state, far_lifts, inverses), block_flops,
        )

    for i in range(PRE_SWEEPS - 1):
        state, *sends = sweep(got, res, state, False)
        got = swap(sends)
        res = local(state)
    coarse_wide, coarse_coef, coarse_faces = call(
        coarse_lay_out_kernel,
        [("vmem", (nc, 6 * nc), f32), ("vmem", (slots, 6 * nc, columns), f32), ("vmem", (6, nc, nc), f32)], [],
        vm(coarse_lifts_t, coarse_coefs_t, hot_lifts, hot_coefs, state),
    )
    residual, coarse_rhs, w, *sends = call(
        restrict_kernel, [field, coarse, coarse] + coarse_sends, [],
        vm(masks, *got, res, far_lifts, restrict, coarse_inverses, coarse_wide),
    )
    (coarse_remote,) = call(
        coarse_remote_kernel, [("vmem", (slots * nc, 4 * nc), f32)], [],
        vm(masks, coarse_faces, coarse_coef, coarse_inverses),
    )
    far_prolong = None
    for _ in range(COARSE_SWEEPS - 1):
        got = swap(sends)
        (w_local,) = call(
            coarse_local_kernel, [coarse], [],
            where + vm(w, coarse_rhs, coarse_blocks, coarse_inverses, coarse_wide, coarse_coef),
        )
        w, *sends = call(
            coarse_sweep_kernel, [coarse] + coarse_sends, [], vm(masks, *got, w_local, coarse_remote)
        )
        if far_prolong is None:
            (far_prolong,) = call(
                far_prolong_kernel, [("vmem", (4, nf, 2 * LANES), bf16)], [], vm(masks, far_lifts, face_prolong, w)
            )
    got = swap(sends)
    res, state = call(
        prolong_kernel, [field, field], [trace_room, field_room],
        where + vm(residual, state, w, lh, ll, blocks, coef, prolong),
        block_flops + lift_flops,
    )
    state, *sends = call(
        post_kernel, [field] + faces, [],
        vm(masks, *got, res, state, far_prolong, inverses), block_flops,
    )
    for i in range(POST_SWEEPS - 1):
        got = swap(sends)
        res = local(state)
        state, *sends = sweep(got, res, state, i == POST_SWEEPS - 2)
    return state


def solution(mesh):
    placed = (
        P(AXES, None, None),
        P(AXES, None, None),
        P(AXES, None, None),
        P(),
        P(AXES, None, None),
        P(AXES, None, None),
        P(AXES, None, None),
        P(),
        P(AXES, None, None),
        P(AXES, None),
        P(AXES),
    )
    return jax.shard_map(
        body,
        mesh=mesh,
        in_specs=placed,
        out_specs=P(AXES, None, None),
        check_vma=False,
    )
```

```python
import functools

import jax
import jax.numpy as jnp
import ml_dtypes
import numpy as np
from jax import lax
from jax.experimental import pallas as pl
from jax.experimental.pallas import tpu as pltpu
from jax.sharding import PartitionSpec as P

NVAR = 5
NODE1 = 4
PRE_SWEEPS = 2
POST_SWEEPS = 2
COARSE_SWEEPS = 4
AXES = ("wide", "narrow")
LANES = 128
VMEM_LIMIT = 16 * 1024 * 1024

damping = 0.8
highest = lax.Precision.HIGHEST
f32, bf16 = jnp.float32, jnp.bfloat16


def prolong_table(node_count, variables):
    points = np.array([-1.0, -1.0 / np.sqrt(5.0), 1.0 / np.sqrt(5.0), 1.0])
    linear = np.stack([(1.0 - points) / 2.0, (1.0 + points) / 2.0], axis=1)
    tensor_hat = (
        linear[:, None, None, :, None, None]
        * linear[None, :, None, None, :, None]
        * linear[None, None, :, None, None, :]
    )
    tensor_hat = tensor_hat.reshape(node_count * node_count * node_count, 8)
    return np.kron(np.eye(variables), tensor_hat).astype(np.float32)


def host_stack(table):
    table = np.pad(table, ((0, 0), (0, -table.shape[1] % LANES)))
    high = table.astype(ml_dtypes.bfloat16)
    low = (table - high.astype(np.float32)).astype(ml_dtypes.bfloat16)
    return jnp.asarray(np.concatenate([high, low], axis=1))


def face_rows(node_count, variables):
    cube = node_count**3
    lattice = np.arange(cube).reshape(node_count, node_count, node_count)
    tables = []
    for face in range(6):
        layer = np.take(lattice, 0 if face % 2 == 0 else node_count - 1, axis=face // 2).reshape(-1)
        tables.append(np.concatenate([layer + v * cube for v in range(variables)]))
    return np.stack(tables)


class Late:
    def __init__(self, source, room, sem):
        self.room, self.copy, self.ready = room, pltpu.make_async_copy(source, room, sem), False
        self.copy.start()

    def wait(self):
        if not self.ready:
            self.ready = True
            self.copy.wait()

    def __getitem__(self, index):
        self.wait()
        return self.room[index]


def call(kernel, outs, scratch, args, flops=0):
    specs, rooms, counts = [], [], []
    for kind, a in args:
        if kind in ("smem", "vmem"):
            specs.append(pl.BlockSpec(memory_space=pltpu.SMEM if kind == "smem" else pltpu.VMEM))
        else:
            specs.append(pl.BlockSpec(memory_space=pl.ANY))
            rooms.append(pltpu.SMEM(a.shape, a.dtype))
            counts.append(1)
    out_rooms = [pltpu.VMEM(shape, dtype) for kind, shape, dtype in outs if kind == "hbm"]
    out_parts = sum(shape[0] for kind, shape, _ in outs if kind == "hbm")
    n_in, n_out, n_rooms = len(args), len(outs), len(rooms)

    def wrapped(*refs):
        ins, results, rest = refs[:n_in], refs[n_in : n_in + n_out], refs[n_in + n_out :]
        in_rooms, rest = rest[:n_rooms], rest[n_rooms:]
        result_rooms, rest = rest[: len(out_rooms)], rest[len(out_rooms) :]
        sems, rest = rest[0], rest[1:]
        given, base, at = [], 0, 0
        for (kind, _), ref in zip(args, ins):
            if kind in ("smem", "vmem"):
                given.append(ref)
                continue
            given.append(Late(ref, in_rooms[at], sems.at[base]))
            base += 1
            at += 1
        leaving, produced, at = [], [], 0
        for (kind, shape, _), ref in zip(outs, results):
            if kind == "vmem":
                produced.append(ref)
                continue
            room = result_rooms[at]
            produced.append((room, [pltpu.make_async_copy(room.at[i], ref.at[i], sems.at[base + i]) for i in range(shape[0])]))
            leaving += produced[-1][1]
            base += shape[0]
            at += 1
        kernel(*given, *produced, *rest)
        for item in given:
            if isinstance(item, Late):
                item.wait()
        for copy in leaving:
            copy.wait()

    moved = sum(int(np.prod(a.shape)) * a.dtype.itemsize for _, a in args)
    moved += sum(int(np.prod(shape)) * 4 for _, shape, _ in outs)
    return pl.pallas_call(
        wrapped,
        out_shape=[jax.ShapeDtypeStruct(shape, dtype) for _, shape, dtype in outs],
        in_specs=specs,
        out_specs=[pl.BlockSpec(memory_space=pltpu.VMEM if kind == "vmem" else pltpu.HBM) for kind, _, _ in outs],
        scratch_shapes=rooms
        + out_rooms
        + [pltpu.SemaphoreType.DMA((max(sum(counts) + out_parts, 1),))]
        + [pltpu.VMEM(shape, dtype) for shape, dtype in scratch],
        compiler_params=pltpu.CompilerParams(vmem_limit_bytes=VMEM_LIMIT),
        cost_estimate=pl.CostEstimate(flops=flops, bytes_accessed=moved, transcendentals=0),
    )(*[a for _, a in args])


def split(x):
    high = x.astype(bf16)
    return high, (x - high.astype(f32)).astype(bf16)


def pad_rows(x, rows):
    return x if x.shape[0] == rows else jnp.concatenate([x, jnp.zeros((rows - x.shape[0], x.shape[1]), x.dtype)], axis=0)


def stack(a):
    room = -a.shape[1] % LANES
    if room:
        a = jnp.concatenate([a, jnp.zeros((a.shape[0], room), a.dtype)], axis=1)
    return jnp.concatenate(split(a), axis=1)


def stacked_dot(a, x):
    xh, xl = split(x)
    rows = a.shape[1] // 2
    top = pad_rows(jnp.concatenate([xh, xl], axis=1), rows)
    low = pad_rows(jnp.concatenate([xh, jnp.zeros_like(xl)], axis=1), rows)
    both = jnp.dot(a, jnp.concatenate([top, low], axis=0), preferred_element_type=f32)
    return both[:, : x.shape[1]] + both[:, x.shape[1] :]


def dot(a, x):
    ah, al = a if isinstance(a, tuple) else split(a)
    xh, xl = split(x)
    n = x.shape[1]
    both = jnp.dot(ah, jnp.concatenate([xh, xl], axis=1), preferred_element_type=f32)
    return both[:, :n] + both[:, n:] + jnp.dot(al, xh, preferred_element_type=f32)


def small_dot(a, x):
    return jnp.dot(a, x, precision=highest, preferred_element_type=f32)


def face_of(state, e, face):
    if face == 0 or face == 1:
        start = 48 * face
        return jnp.concatenate([state[e, pl.ds(64 * v + start, 16)] for v in range(NVAR)], axis=0)
    if face >= 4:
        return state[e, pl.ds(3 * (face - 4), 80, stride=4)]
    half = 8 * (face - 2)
    first = jnp.concatenate([state[e, pl.ds(32 * m + half, 8)] for m in range(10)], axis=0)
    second = jnp.concatenate([state[e, pl.ds(32 * m + 16 + half, 8)] for m in range(10)], axis=0)
    low = lax.broadcasted_iota(jnp.int32, first.shape, 0) % 8 < 4
    if face == 2:
        return jnp.where(low, first, pltpu.roll(second, 4, 0))
    return jnp.where(low, pltpu.roll(first, 76, 0), second)


def link(ids, nbr, slots, e, face):
    g = nbr[e, face]
    owner = lax.div(g, slots)
    here = jnp.logical_and(g >= 0, owner == ids[2])
    away = jnp.logical_and(g >= 0, owner != ids[2])
    return here, away, jnp.maximum(lax.rem(g, slots), 0)


def crossing(ids, nbr, slots, face):
    found, slot = False, 0
    for e in range(slots):
        _, away, _ = link(ids, nbr, slots, e, face)
        found = jnp.logical_or(found, away)
        slot = jnp.where(away, e, slot)
    return found, slot


def swap_of(ids, face):
    return lax.rem(face % 2 + ids[face // 2] % 2 + 1, 2)


def fill_masks(ids, nbr, slots, masks):
    for i in range(4):
        for side in range(2):
            f = 2 * (i // 2) + side
            for e in range(slots):
                _, away, _ = link(ids, nbr, slots, e, f)
                value = jnp.where(jnp.logical_and(away, swap_of(ids, f) == i % 2), 1.0, 0.0)
                masks[(2 * i + side) * slots + e] = jnp.full(masks.shape[1:], value, f32)


def masked(mask, x):
    return (x.reshape(-1, *mask.shape) * mask).reshape(x.shape)


def meets(masks, slots, i, e):
    return masks[2 * i * slots + e] + masks[(2 * i + 1) * slots + e]


def crossing_traces(state):
    return [[face_of(state, e, f) for e in range(state.shape[0])] for f in range(4)]


def fill_traces(masks, traces, sends):
    slots = len(traces[0])
    for i in range(4):
        terms = [
            masked(masks[(2 * i + side) * slots + e], traces[2 * (i // 2) + side][e])
            for side in range(2)
            for e in range(slots)
        ]
        sends[i][...] = sum(terms[1:], terms[0])


def fill_elements(masks, w, sends):
    slots = w.shape[0]
    for i in range(4):
        terms = [masked(meets(masks, slots, i, e), w[e]) for e in range(slots)]
        sends[i][...] = sum(terms[1:], terms[0])


def mask_kernel(ids, nbr, masks):
    fill_masks(ids, nbr, nbr.room.shape[0], masks)


def first_kernel(counts, masks, rhs, given, _, v, live, inverses, *sends):
    for e in range(rhs.shape[0]):
        live[e] = jnp.where(e < counts[0], rhs[e], 0.0)
        inverses[e] = stack(given[e])
        v[e] = damping * stacked_dot(inverses[e], live[e])
    fill_traces(masks, crossing_traces(v), sends)


def local_residual(ids, nbr, rhs, state, blocks, lifts, coef, out, traces):
    slots, _, columns = state.shape
    for e in range(slots):
        out[e] = rhs[e] - stacked_dot(blocks[e], state[e])
        for f in range(6):
            traces[f * slots + e] = face_of(state, e, f)
    near = []
    for e in range(slots):
        parts = []
        for f in range(6):
            here, _, s = link(ids, nbr, slots, e, f)
            t = traces[(f ^ 1) * slots + s] * coef[e, pl.ds(80 * f, 80)]
            parts.append(jnp.where(here, t, 0.0))
        near.append(jnp.concatenate(parts, axis=0))
    coupled = dot(lifts, jnp.concatenate(near, axis=1))
    for e in range(slots):
        out[e] = out[e] - coupled[:, e * columns : (e + 1) * columns]


def lay_out(lifts_t, coefs, lh, ll, coef):
    faces, nface, nf = lifts_t.shape
    slots = coef.shape[0]
    whole = jnp.concatenate([lifts_t[f] for f in range(faces)], axis=0).T
    lh[...], ll[...] = split(whole)
    turned = coefs[...].T
    for e in range(slots):
        for f in range(faces):
            column = turned[:, f * slots + e : f * slots + e + 1]
            coef[e, nface * f : nface * (f + 1)] = jnp.broadcast_to(column, (nface, coef.shape[2]))


def lay_out_far(ids, nbr, lifts_t, coef, far_lifts):
    nface, slots = lifts_t.shape[1], coef.shape[0]
    for i in range(4):
        low = 2 * (i // 2)
        first = swap_of(ids, low) == i % 2
        factors = []
        for f in (low, low + 1):
            _, slot = crossing(ids, nbr, slots, f)
            factors.append(coef[slot, pl.ds(nface * f, nface)][:, :1])
        factor = jnp.where(first, factors[0], factors[1])
        scaled = jnp.where(first, lifts_t[low], lifts_t[low + 1]) * factor
        high = scaled.astype(bf16).astype(f32)
        far_lifts[i] = jnp.concatenate([high, scaled - high], axis=0).T.astype(bf16)


def first_local_kernel(
    ids, nbr, state, lifts_t, coefs, given, rhs, out, lh, ll, far_lifts, coef, blocks, traces
):
    lay_out(lifts_t, coefs, lh, ll, coef)
    for e in range(given.shape[0]):
        blocks[e] = stack(given[e])

    local_residual(
        ids, nbr, rhs, state, blocks, (lh[...], ll[...]), coef, out, traces
    )
    lay_out_far(ids, nbr, lifts_t, coef, far_lifts)


def local_kernel(ids, nbr, state, lh, ll, blocks, coef, rhs, out, traces):
    local_residual(ids, nbr, rhs, state, blocks, (lh[...], ll[...]), coef, out, traces)


def less_remote(masks, res, parts, e):
    slots = masks.shape[0] // 8
    for i, part in enumerate(parts):
        res = res - masked(meets(masks, slots, i, e), part)
    return res


def sweep_kernel(masks, y0, y1, y3, y2, res, state, far_lifts, inverses, v, *sends):
    parts = [stacked_dot(far_lifts[i], y[...]) for i, y in enumerate((y0, y1, y2, y3))]
    for e in range(res.shape[0]):
        value = state[e] + damping * stacked_dot(inverses[e], less_remote(masks, res[e], parts, e))
        if sends:
            v[e] = value
        else:
            v[0][e] = value
            v[1][e].start()
    if sends:
        fill_traces(masks, crossing_traces(v), sends)


def restrict_kernel(masks, y0, y1, y3, y2, res, far_lifts, restrict, inverses, r, rhs, w, *sends):
    parts = [stacked_dot(far_lifts[i], y[...]) for i, y in enumerate((y0, y1, y2, y3))]
    for e in range(r.shape[0]):
        left = less_remote(masks, res[e], parts, e)
        r[e] = left
        rhs[e] = 0.25 * stacked_dot(restrict[...], left)
        w[e] = damping * dot(inverses[e], rhs[e])
    fill_elements(masks, w, sends)


def prolong_kernel(ids, nbr, r, state, w, lh, ll, blocks, coef, prolong, out, corrected, traces, correction):
    slots = state.shape[0]
    columns = state.shape[2]
    raised = stacked_dot(prolong[...], jnp.concatenate([w[e] for e in range(slots)], axis=1))
    for e in range(slots):
        correction[e] = raised[:, e * columns : (e + 1) * columns]
        corrected[e] = state[e] + correction[e]
    local_residual(
        ids, nbr, r, correction, blocks, (lh[...], ll[...]), coef, out, traces
    )


def post_kernel(masks, y0, y1, y3, y2, res, state, far_prolong, inverses, v, *sends):
    parts = [stacked_dot(far_prolong[i], y[...]) for i, y in enumerate((y0, y1, y2, y3))]
    for e in range(res.shape[0]):
        v[e] = state[e] + damping * stacked_dot(inverses[e], less_remote(masks, res[e], parts, e))
    fill_traces(masks, crossing_traces(v), sends)


def coarse_lay_out_kernel(lifts_t, coefs, hot_lifts, hot_coefs, _, lifts, coef, wide):
    faces, _, nc = lifts_t.shape
    slots = coef.shape[0]
    spread = small_dot(hot_coefs[...], coefs[...].T)
    rows = small_dot(hot_lifts[...], jnp.concatenate([lifts_t[f] for f in range(faces)], axis=0))
    lifts[...] = rows.T
    for f in range(faces):
        wide[f] = rows[nc * f : nc * (f + 1)]
        for e in range(slots):
            column = spread[nc * f : nc * (f + 1), f * slots + e : f * slots + e + 1]
            coef[e, nc * f : nc * (f + 1)] = jnp.broadcast_to(column, (nc, coef.shape[2]))


def far_prolong_kernel(masks, far_lifts, face_prolong, _, far_prolong):
    slots = masks.shape[0] // 8
    for i in range(4):
        total = None
        for side in range(2):
            on = sum(masks[(2 * i + side) * slots + e] for e in range(slots))
            term = masked(on, face_prolong[2 * (i // 2) + 1 - side])
            total = term if total is None else total + term
        far_prolong[i] = jnp.concatenate(split(stacked_dot(far_lifts[i], total)), axis=1)


def coarse_remote_kernel(masks, wide, coef, inverses, remote):
    slots, nc, _ = inverses.shape
    for e in range(slots):
        scaled = []
        for i in range(4):
            total = None
            for side in range(2):
                f = 2 * (i // 2) + side
                term = masked(masks[(2 * i + side) * slots + e], coef[e, nc * f : nc * (f + 1)])
                term = wide[f] * term[:, :nc]
                total = term if total is None else total + term
            scaled.append(total)
        rows = damping * small_dot(inverses[e], jnp.concatenate(scaled, axis=0).T)
        remote[e * nc : (e + 1) * nc] = rows


def coarse_local_kernel(ids, nbr, w, rhs, blocks, inverses, lifts, coef, out):
    slots, nc, columns = w.shape
    for e in range(slots):
        out[e] = rhs[e] - dot(blocks[e], w[e])
    near = []
    for e in range(slots):
        parts = []
        for f in range(6):
            here, _, s = link(ids, nbr, slots, e, f)
            parts.append(jnp.where(here, w[s] * coef[e, nc * f : nc * (f + 1)], 0.0))
        near.append(jnp.concatenate(parts, axis=0))
    coupled = dot(lifts[...], jnp.concatenate(near, axis=1))
    for e in range(slots):
        res = out[e] - coupled[:, e * columns : (e + 1) * columns]
        out[e] = w[e] + damping * dot(inverses[e], res)


def coarse_sweep_kernel(masks, y0, y1, y3, y2, local, remote, w, *sends):
    slots, nc, _ = w.shape
    far = dot(remote[...], jnp.concatenate([y[...] for y in (y0, y1, y2, y3)], axis=0))
    for e in range(slots):
        w[e] = local[e] - far[e * nc : (e + 1) * nc]
    fill_elements(masks, w, sends)


def swap(parts):
    got = []
    for i in (0, 1, 3, 2):
        axis = AXES[i // 2]
        pairs = []
        for a in range(i % 2, lax.axis_size(axis) - 1, 2):
            pairs += [(a, a + 1), (a + 1, a)]
        got.append(lax.ppermute(parts[i], axis, pairs))
    return got


def body(
    right_side,
    fine_blocks,
    fine_inverses,
    fine_lifts,
    fine_coefs,
    coarse_blocks,
    coarse_inverses,
    coarse_lifts,
    coarse_coefs,
    neighbours,
    counts,
):
    slots, nf, columns = right_side.shape
    nface = fine_lifts.shape[2]
    nc = coarse_blocks.shape[1]
    ncf = coarse_lifts.shape[2]
    wide_here, narrow_here = lax.axis_index("wide"), lax.axis_index("narrow")
    ids = jnp.stack([wide_here, narrow_here, wide_here * lax.axis_size("narrow") + narrow_here]).astype(jnp.int32)

    prolong_np = prolong_table(NODE1, NVAR)
    coarse_table = face_rows(2, NVAR)
    fine_table = face_rows(NODE1, NVAR)
    prolong = host_stack(prolong_np)
    restrict = host_stack(np.ascontiguousarray(prolong_np.T))
    face_prolong = np.stack([prolong_np[fine_table[f]] for f in range(4)])
    face_prolong = jnp.asarray(np.pad(face_prolong, ((0, 0), (0, 0), (0, LANES - nc))))
    hot_lifts = np.zeros((6, nc, 6, ncf), np.float32)
    hot_coefs = np.zeros((6, nc, ncf), np.float32)
    for f in range(6):
        hot_lifts[f, coarse_table[f ^ 1], f, np.arange(ncf)] = 1.0
        hot_coefs[f, coarse_table[f ^ 1], np.arange(ncf)] = 1.0
    hot_lifts = jnp.asarray(hot_lifts.reshape(6 * nc, 6 * ncf))
    hot_coefs = jnp.asarray(hot_coefs.reshape(6 * nc, ncf))

    lifts_t = fine_lifts.transpose(0, 2, 1)
    coefs = fine_coefs.transpose(1, 0, 2).reshape(6 * slots, nface)
    coarse_lifts_t = coarse_lifts.transpose(0, 2, 1)
    coarse_coefs_t = coarse_coefs.transpose(1, 0, 2).reshape(6 * slots, ncf)

    field = ("vmem", (slots, nf, columns), f32)
    faces = [("vmem", (nface, columns), f32)] * 4
    coarse = ("vmem", (slots, nc, columns), f32)
    coarse_sends = [("vmem", (nc, columns), f32)] * 4
    trace_room = ((6 * slots, nface, columns), f32)
    field_room = (field[1], f32)
    block_flops = 3 * 2 * slots * nf * nf * columns
    lift_flops = 3 * 2 * slots * nf * 6 * nface * columns
    where = [("late", ids), ("late", neighbours)]

    def vm(*arrays):
        return [("vmem", a) for a in arrays]

    def parts(*arrays):
        return [("parts", a) for a in arrays]

    wide = 2 * (nf + -nf % LANES)
    matrix = ("vmem", (slots, nf, wide), bf16)
    mask_tiles = ("vmem", (8 * slots, 8, columns), f32)
    (masks,) = call(mask_kernel, [mask_tiles], [], where, 8 * block_flops)
    coarse_wide, coarse_coef, coarse_faces = call(
        coarse_lay_out_kernel,
        [("vmem", (nc, 6 * nc), f32), ("vmem", (slots, 6 * nc, columns), f32), ("vmem", (6, nc, nc), f32)], [],
        vm(coarse_lifts_t, coarse_coefs_t, hot_lifts, hot_coefs, masks),
    )
    state, rhs_live, inverses, *sends = call(
        first_kernel, [field, field, matrix] + faces, [],
        [("smem", counts)] + vm(masks, right_side, fine_inverses, coarse_wide), 8 * block_flops,
    )
    got = swap(sends)
    res, lh, ll, far_lifts, coef, blocks = call(
        first_local_kernel,
        [field]
        + [("vmem", (nf, 6 * nface), bf16)] * 2
        + [("vmem", (4, nf, 2 * nface), bf16), ("vmem", (slots, 6 * nface, columns), f32), matrix],
        [trace_room],
        where + vm(state, lifts_t, coefs, fine_blocks, rhs_live),
        block_flops + lift_flops,
    )

    def local(state):
        return call(
            local_kernel, [field], [trace_room],
            where + vm(state, lh, ll, blocks, coef, rhs_live), block_flops + lift_flops,
        )[0]

    def sweep(got, res, state, last):
        return call(
            sweep_kernel, [("hbm",) + field[1:]] if last else [field] + faces, [],
            vm(masks, *got, res, state, far_lifts, inverses), block_flops,
        )

    for i in range(PRE_SWEEPS - 1):
        state, *sends = sweep(got, res, state, False)
        got = swap(sends)
        res = local(state)
    residual, coarse_rhs, w, *sends = call(
        restrict_kernel, [field, coarse, coarse] + coarse_sends, [],
        vm(masks, *got, res, far_lifts, restrict, coarse_inverses),
    )
    (coarse_remote,) = call(
        coarse_remote_kernel, [("vmem", (slots * nc, 4 * nc), f32)], [],
        vm(masks, coarse_faces, coarse_coef, coarse_inverses),
    )
    far_prolong = None
    for _ in range(COARSE_SWEEPS - 1):
        got = swap(sends)
        (w_local,) = call(
            coarse_local_kernel, [coarse], [],
            where + vm(w, coarse_rhs, coarse_blocks, coarse_inverses, coarse_wide, coarse_coef),
        )
        w, *sends = call(
            coarse_sweep_kernel, [coarse] + coarse_sends, [], vm(masks, *got, w_local, coarse_remote)
        )
        if far_prolong is None:
            (far_prolong,) = call(
                far_prolong_kernel, [("vmem", (4, nf, 2 * LANES), bf16)], [], vm(masks, far_lifts, face_prolong, w)
            )
    got = swap(sends)
    res, state = call(
        prolong_kernel, [field, field], [trace_room, field_room],
        where + vm(residual, state, w, lh, ll, blocks, coef, prolong),
        block_flops + lift_flops,
    )
    state, *sends = call(
        post_kernel, [field] + faces, [],
        vm(masks, *got, res, state, far_prolong, inverses), block_flops,
    )
    for i in range(POST_SWEEPS - 1):
        got = swap(sends)
        res = local(state)
        state, *sends = sweep(got, res, state, i == POST_SWEEPS - 2)
    return state


def solution(mesh):
    placed = (
        P(AXES, None, None),
        P(AXES, None, None),
        P(AXES, None, None),
        P(),
        P(AXES, None, None),
        P(AXES, None, None),
        P(AXES, None, None),
        P(),
        P(AXES, None, None),
        P(AXES, None),
        P(AXES),
    )
    return jax.shard_map(
        body,
        mesh=mesh,
        in_specs=placed,
        out_specs=P(AXES, None, None),
        check_vma=False,
    )
```

```python
import functools

import jax
import jax.numpy as jnp
import ml_dtypes
import numpy as np
from jax import lax
from jax.experimental import pallas as pl
from jax.experimental.pallas import tpu as pltpu
from jax.sharding import PartitionSpec as P

NVAR = 5
NODE1 = 4
PRE_SWEEPS = 2
POST_SWEEPS = 2
COARSE_SWEEPS = 4
AXES = ("wide", "narrow")
LANES = 128
VMEM_LIMIT = 16 * 1024 * 1024

damping = 0.8
highest = lax.Precision.HIGHEST
f32, bf16 = jnp.float32, jnp.bfloat16


def prolong_table(node_count, variables):
    points = np.array([-1.0, -1.0 / np.sqrt(5.0), 1.0 / np.sqrt(5.0), 1.0])
    linear = np.stack([(1.0 - points) / 2.0, (1.0 + points) / 2.0], axis=1)
    tensor_hat = (
        linear[:, None, None, :, None, None]
        * linear[None, :, None, None, :, None]
        * linear[None, None, :, None, None, :]
    )
    tensor_hat = tensor_hat.reshape(node_count * node_count * node_count, 8)
    return np.kron(np.eye(variables), tensor_hat).astype(np.float32)


def host_split(table):
    high = table.astype(ml_dtypes.bfloat16)
    return high, (table - high.astype(np.float32)).astype(ml_dtypes.bfloat16)


def host_stack(table):
    return jnp.asarray(np.concatenate(host_split(np.pad(table, ((0, 0), (0, -table.shape[1] % LANES)))), axis=1))


def face_rows(node_count, variables):
    cube = node_count**3
    lattice = np.arange(cube).reshape(node_count, node_count, node_count)
    tables = []
    for face in range(6):
        layer = np.take(lattice, 0 if face % 2 == 0 else node_count - 1, axis=face // 2).reshape(-1)
        tables.append(np.concatenate([layer + v * cube for v in range(variables)]))
    return np.stack(tables)


class Late:
    def __init__(self, source, room, sem):
        self.room, self.copy, self.ready = room, pltpu.make_async_copy(source, room, sem), False
        self.copy.start()

    def wait(self):
        if not self.ready:
            self.ready = True
            self.copy.wait()

    def __getitem__(self, index):
        self.wait()
        return self.room[index]


def call(kernel, outs, scratch, args, flops=0):
    specs, rooms, counts = [], [], []
    for kind, a in args:
        if kind in ("smem", "vmem"):
            specs.append(pl.BlockSpec(memory_space=pltpu.SMEM if kind == "smem" else pltpu.VMEM))
        else:
            specs.append(pl.BlockSpec(memory_space=pl.ANY))
            rooms.append(pltpu.SMEM(a.shape, a.dtype))
            counts.append(1)
    out_rooms = [pltpu.VMEM(shape, dtype) for kind, shape, dtype in outs if kind == "hbm"]
    out_parts = sum(shape[0] for kind, shape, _ in outs if kind == "hbm")
    n_in, n_out, n_rooms = len(args), len(outs), len(rooms)

    def wrapped(*refs):
        ins, results, rest = refs[:n_in], refs[n_in : n_in + n_out], refs[n_in + n_out :]
        in_rooms, rest = rest[:n_rooms], rest[n_rooms:]
        result_rooms, rest = rest[: len(out_rooms)], rest[len(out_rooms) :]
        sems, rest = rest[0], rest[1:]
        given, base, at = [], 0, 0
        for (kind, _), ref in zip(args, ins):
            if kind in ("smem", "vmem"):
                given.append(ref)
                continue
            given.append(Late(ref, in_rooms[at], sems.at[base]))
            base += 1
            at += 1
        leaving, produced, at = [], [], 0
        for (kind, shape, _), ref in zip(outs, results):
            if kind == "vmem":
                produced.append(ref)
                continue
            room = result_rooms[at]
            produced.append((room, [pltpu.make_async_copy(room.at[i], ref.at[i], sems.at[base + i]) for i in range(shape[0])]))
            leaving += produced[-1][1]
            base += shape[0]
            at += 1
        kernel(*given, *produced, *rest)
        for item in given:
            if isinstance(item, Late):
                item.wait()
        for copy in leaving:
            copy.wait()

    moved = sum(int(np.prod(a.shape)) * a.dtype.itemsize for _, a in args)
    moved += sum(int(np.prod(shape)) * 4 for _, shape, _ in outs)
    return pl.pallas_call(
        wrapped,
        out_shape=[jax.ShapeDtypeStruct(shape, dtype) for _, shape, dtype in outs],
        in_specs=specs,
        out_specs=[pl.BlockSpec(memory_space=pltpu.VMEM if kind == "vmem" else pltpu.HBM) for kind, _, _ in outs],
        scratch_shapes=rooms
        + out_rooms
        + [pltpu.SemaphoreType.DMA((max(sum(counts) + out_parts, 1),))]
        + [pltpu.VMEM(shape, dtype) for shape, dtype in scratch],
        compiler_params=pltpu.CompilerParams(vmem_limit_bytes=VMEM_LIMIT),
        cost_estimate=pl.CostEstimate(flops=flops, bytes_accessed=moved, transcendentals=0),
    )(*[a for _, a in args])


def split(x):
    high = x.astype(bf16)
    return high, (x - high.astype(f32)).astype(bf16)


def pad_rows(x, rows):
    return x if x.shape[0] == rows else jnp.concatenate([x, jnp.zeros((rows - x.shape[0], x.shape[1]), x.dtype)], axis=0)


def stack(a):
    room = -a.shape[1] % LANES
    if room:
        a = jnp.concatenate([a, jnp.zeros((a.shape[0], room), a.dtype)], axis=1)
    return jnp.concatenate(split(a), axis=1)


def stacked_dot(a, x):
    xh, xl = split(x)
    rows = a.shape[1] // 2
    top = pad_rows(jnp.concatenate([xh, xl], axis=1), rows)
    low = pad_rows(jnp.concatenate([xh, jnp.zeros_like(xl)], axis=1), rows)
    both = jnp.dot(a, jnp.concatenate([top, low], axis=0), preferred_element_type=f32)
    return both[:, : x.shape[1]] + both[:, x.shape[1] :]


def dot(a, x):
    ah, al = a if isinstance(a, tuple) else split(a)
    xh, xl = split(x)
    n = x.shape[1]
    both = jnp.dot(ah, jnp.concatenate([xh, xl], axis=1), preferred_element_type=f32)
    return both[:, :n] + both[:, n:] + jnp.dot(al, xh, preferred_element_type=f32)


def small_dot(a, x):
    return jnp.dot(a, x, precision=highest, preferred_element_type=f32)


def face_of(state, e, face):
    if face == 0 or face == 1:
        start = 48 * face
        return jnp.concatenate([state[e, pl.ds(64 * v + start, 16)] for v in range(NVAR)], axis=0)
    if face >= 4:
        return state[e, pl.ds(3 * (face - 4), 80, stride=4)]
    half = 8 * (face - 2)
    first = jnp.concatenate([state[e, pl.ds(32 * m + half, 8)] for m in range(10)], axis=0)
    second = jnp.concatenate([state[e, pl.ds(32 * m + 16 + half, 8)] for m in range(10)], axis=0)
    low = lax.broadcasted_iota(jnp.int32, first.shape, 0) % 8 < 4
    if face == 2:
        return jnp.where(low, first, pltpu.roll(second, 4, 0))
    return jnp.where(low, pltpu.roll(first, 76, 0), second)


def link(ids, nbr, slots, e, face):
    g = nbr[e, face]
    owner = lax.div(g, slots)
    here = jnp.logical_and(g >= 0, owner == ids[2])
    away = jnp.logical_and(g >= 0, owner != ids[2])
    return here, away, jnp.maximum(lax.rem(g, slots), 0)


def crossing(ids, nbr, slots, face):
    found, slot = False, 0
    for e in range(slots):
        _, away, _ = link(ids, nbr, slots, e, face)
        found = jnp.logical_or(found, away)
        slot = jnp.where(away, e, slot)
    return found, slot


def swap_of(ids, face):
    return lax.rem(face % 2 + ids[face // 2] % 2 + 1, 2)


def fill_masks(ids, nbr, slots, masks):
    for i in range(4):
        for side in range(2):
            f = 2 * (i // 2) + side
            for e in range(slots):
                _, away, _ = link(ids, nbr, slots, e, f)
                value = jnp.where(jnp.logical_and(away, swap_of(ids, f) == i % 2), 1.0, 0.0)
                masks[(2 * i + side) * slots + e] = jnp.full(masks.shape[1:], value, f32)


def masked(mask, x):
    return (x.reshape(-1, *mask.shape) * mask).reshape(x.shape)


def meets(masks, slots, i, e):
    return masks[2 * i * slots + e] + masks[(2 * i + 1) * slots + e]


def crossing_traces(state):
    return [[face_of(state, e, f) for e in range(state.shape[0])] for f in range(4)]


def fill_traces(masks, traces, sends):
    slots = len(traces[0])
    for i in range(4):
        terms = [
            masked(masks[(2 * i + side) * slots + e], traces[2 * (i // 2) + side][e])
            for side in range(2)
            for e in range(slots)
        ]
        sends[i][...] = sum(terms[1:], terms[0])


def fill_elements(masks, w, sends):
    slots = w.shape[0]
    for i in range(4):
        terms = [masked(meets(masks, slots, i, e), w[e]) for e in range(slots)]
        sends[i][...] = sum(terms[1:], terms[0])


def mask_kernel(ids, nbr, masks):
    fill_masks(ids, nbr, nbr.room.shape[0], masks)


def first_kernel(counts, masks, rhs, given, _, v, live, inverses, *sends):
    for e in range(rhs.shape[0]):
        live[e] = jnp.where(e < counts[0], rhs[e], 0.0)
        inverses[e] = stack(given[e])
        v[e] = damping * stacked_dot(inverses[e], live[e])
    fill_traces(masks, crossing_traces(v), sends)


def local_residual(ids, nbr, rhs, state, blocks, lifts, coef, out, traces):
    slots, _, columns = state.shape
    for e in range(slots):
        out[e] = rhs[e] - stacked_dot(blocks[e], state[e])
        for f in range(6):
            traces[f * slots + e] = face_of(state, e, f)
    near = []
    for e in range(slots):
        parts = []
        for f in range(6):
            here, _, s = link(ids, nbr, slots, e, f)
            t = traces[(f ^ 1) * slots + s] * coef[e, pl.ds(80 * f, 80)]
            parts.append(jnp.where(here, t, 0.0))
        near.append(jnp.concatenate(parts, axis=0))
    coupled = dot(lifts, jnp.concatenate(near, axis=1))
    for e in range(slots):
        out[e] = out[e] - coupled[:, e * columns : (e + 1) * columns]


def lay_out(lifts_t, coefs, lh, ll, coef):
    faces, nface, nf = lifts_t.shape
    slots = coef.shape[0]
    whole = jnp.concatenate([lifts_t[f] for f in range(faces)], axis=0).T
    lh[...], ll[...] = split(whole)
    turned = coefs[...].T
    for e in range(slots):
        for f in range(faces):
            column = turned[:, f * slots + e : f * slots + e + 1]
            coef[e, nface * f : nface * (f + 1)] = jnp.broadcast_to(column, (nface, coef.shape[2]))


def lay_out_far(ids, nbr, lifts_t, coef, far_lifts):
    nface, slots = lifts_t.shape[1], coef.shape[0]
    for i in range(4):
        low = 2 * (i // 2)
        first = swap_of(ids, low) == i % 2
        factors = []
        for f in (low, low + 1):
            _, slot = crossing(ids, nbr, slots, f)
            factors.append(coef[slot, pl.ds(nface * f, nface)][:, :1])
        factor = jnp.where(first, factors[0], factors[1])
        scaled = jnp.where(first, lifts_t[low], lifts_t[low + 1]) * factor
        high = scaled.astype(bf16).astype(f32)
        far_lifts[i] = jnp.concatenate([high, scaled - high], axis=0).T.astype(bf16)


def first_local_kernel(
    ids, nbr, state, lifts_t, coefs, given, rhs, out, lh, ll, far_lifts, coef, blocks, traces
):
    lay_out(lifts_t, coefs, lh, ll, coef)
    for e in range(given.shape[0]):
        blocks[e] = stack(given[e])

    local_residual(
        ids, nbr, rhs, state, blocks, (lh[...], ll[...]), coef, out, traces
    )
    lay_out_far(ids, nbr, lifts_t, coef, far_lifts)


def local_kernel(ids, nbr, state, lh, ll, blocks, coef, rhs, out, traces):
    local_residual(ids, nbr, rhs, state, blocks, (lh[...], ll[...]), coef, out, traces)


def less_remote(masks, res, parts, e):
    slots = masks.shape[0] // 8
    for i, part in enumerate(parts):
        res = res - masked(meets(masks, slots, i, e), part)
    return res


def sweep_kernel(masks, y0, y1, y3, y2, res, state, far_lifts, inverses, v, *sends):
    parts = [stacked_dot(far_lifts[i], y[...]) for i, y in enumerate((y0, y1, y2, y3))]
    for e in range(res.shape[0]):
        value = state[e] + damping * stacked_dot(inverses[e], less_remote(masks, res[e], parts, e))
        if sends:
            v[e] = value
        else:
            v[0][e] = value
            v[1][e].start()
    if sends:
        fill_traces(masks, crossing_traces(v), sends)


def restrict_kernel(masks, y0, y1, y3, y2, res, far_lifts, high, low, inverses, r, rhs, w, *sends):
    parts = [stacked_dot(far_lifts[i], y[...]) for i, y in enumerate((y0, y1, y2, y3))]
    for e in range(r.shape[0]):
        left = less_remote(masks, res[e], parts, e)
        r[e] = left
        rhs[e] = 0.25 * dot((high[...], low[...]), left)
        w[e] = damping * dot(inverses[e], rhs[e])
    fill_elements(masks, w, sends)


def prolong_kernel(ids, nbr, r, state, w, lh, ll, blocks, coef, prolong, out, corrected, traces, correction):
    slots = state.shape[0]
    columns = state.shape[2]
    raised = stacked_dot(prolong[...], jnp.concatenate([w[e] for e in range(slots)], axis=1))
    for e in range(slots):
        correction[e] = raised[:, e * columns : (e + 1) * columns]
        corrected[e] = state[e] + correction[e]
    local_residual(
        ids, nbr, r, correction, blocks, (lh[...], ll[...]), coef, out, traces
    )


def post_kernel(masks, y0, y1, y3, y2, res, state, far_prolong, inverses, v, *sends):
    parts = [stacked_dot(far_prolong[i], y[...]) for i, y in enumerate((y0, y1, y2, y3))]
    for e in range(res.shape[0]):
        v[e] = state[e] + damping * stacked_dot(inverses[e], less_remote(masks, res[e], parts, e))
    fill_traces(masks, crossing_traces(v), sends)


def coarse_lay_out_kernel(lifts_t, coefs, hot_lifts, hot_coefs, _, lifts, coef, wide):
    faces, _, nc = lifts_t.shape
    slots = coef.shape[0]
    spread = small_dot(hot_coefs[...], coefs[...].T)
    rows = small_dot(hot_lifts[...], jnp.concatenate([lifts_t[f] for f in range(faces)], axis=0))
    lifts[...] = rows.T
    for f in range(faces):
        wide[f] = rows[nc * f : nc * (f + 1)]
        for e in range(slots):
            column = spread[nc * f : nc * (f + 1), f * slots + e : f * slots + e + 1]
            coef[e, nc * f : nc * (f + 1)] = jnp.broadcast_to(column, (nc, coef.shape[2]))


def far_prolong_kernel(masks, far_lifts, face_prolong, _, far_prolong):
    slots = masks.shape[0] // 8
    for i in range(4):
        total = None
        for side in range(2):
            on = sum(masks[(2 * i + side) * slots + e] for e in range(slots))
            term = masked(on, face_prolong[2 * (i // 2) + 1 - side])
            total = term if total is None else total + term
        far_prolong[i] = jnp.concatenate(split(stacked_dot(far_lifts[i], total)), axis=1)


def coarse_remote_kernel(masks, wide, coef, inverses, remote):
    slots, nc, _ = inverses.shape
    for e in range(slots):
        scaled = []
        for i in range(4):
            total = None
            for side in range(2):
                f = 2 * (i // 2) + side
                term = masked(masks[(2 * i + side) * slots + e], coef[e, nc * f : nc * (f + 1)])
                term = wide[f] * term[:, :nc]
                total = term if total is None else total + term
            scaled.append(total)
        rows = damping * small_dot(inverses[e], jnp.concatenate(scaled, axis=0).T)
        remote[e * nc : (e + 1) * nc] = rows


def coarse_local_kernel(ids, nbr, w, rhs, blocks, inverses, lifts, coef, out):
    slots, nc, columns = w.shape
    for e in range(slots):
        out[e] = rhs[e] - dot(blocks[e], w[e])
    near = []
    for e in range(slots):
        parts = []
        for f in range(6):
            here, _, s = link(ids, nbr, slots, e, f)
            parts.append(jnp.where(here, w[s] * coef[e, nc * f : nc * (f + 1)], 0.0))
        near.append(jnp.concatenate(parts, axis=0))
    coupled = dot(lifts[...], jnp.concatenate(near, axis=1))
    for e in range(slots):
        res = out[e] - coupled[:, e * columns : (e + 1) * columns]
        out[e] = w[e] + damping * dot(inverses[e], res)


def coarse_sweep_kernel(masks, y0, y1, y3, y2, local, remote, w, *sends):
    slots, nc, _ = w.shape
    far = dot(remote[...], jnp.concatenate([y[...] for y in (y0, y1, y2, y3)], axis=0))
    for e in range(slots):
        w[e] = local[e] - far[e * nc : (e + 1) * nc]
    fill_elements(masks, w, sends)


def swap(parts):
    got = []
    for i in (0, 1, 3, 2):
        axis = AXES[i // 2]
        pairs = []
        for a in range(i % 2, lax.axis_size(axis) - 1, 2):
            pairs += [(a, a + 1), (a + 1, a)]
        got.append(lax.ppermute(parts[i], axis, pairs))
    return got


def body(
    right_side,
    fine_blocks,
    fine_inverses,
    fine_lifts,
    fine_coefs,
    coarse_blocks,
    coarse_inverses,
    coarse_lifts,
    coarse_coefs,
    neighbours,
    counts,
):
    slots, nf, columns = right_side.shape
    nface = fine_lifts.shape[2]
    nc = coarse_blocks.shape[1]
    ncf = coarse_lifts.shape[2]
    wide_here, narrow_here = lax.axis_index("wide"), lax.axis_index("narrow")
    ids = jnp.stack([wide_here, narrow_here, wide_here * lax.axis_size("narrow") + narrow_here]).astype(jnp.int32)

    prolong_np = prolong_table(NODE1, NVAR)
    coarse_table = face_rows(2, NVAR)
    fine_table = face_rows(NODE1, NVAR)
    prolong = host_stack(prolong_np)
    restrict = [jnp.asarray(np.ascontiguousarray(part.T)) for part in host_split(prolong_np)]
    face_prolong = np.stack([prolong_np[fine_table[f]] for f in range(4)])
    face_prolong = jnp.asarray(np.pad(face_prolong, ((0, 0), (0, 0), (0, LANES - nc))))
    hot_lifts = np.zeros((6, nc, 6, ncf), np.float32)
    hot_coefs = np.zeros((6, nc, ncf), np.float32)
    for f in range(6):
        hot_lifts[f, coarse_table[f ^ 1], f, np.arange(ncf)] = 1.0
        hot_coefs[f, coarse_table[f ^ 1], np.arange(ncf)] = 1.0
    hot_lifts = jnp.asarray(hot_lifts.reshape(6 * nc, 6 * ncf))
    hot_coefs = jnp.asarray(hot_coefs.reshape(6 * nc, ncf))

    lifts_t = fine_lifts.transpose(0, 2, 1)
    coefs = fine_coefs.transpose(1, 0, 2).reshape(6 * slots, nface)
    coarse_lifts_t = coarse_lifts.transpose(0, 2, 1)
    coarse_coefs_t = coarse_coefs.transpose(1, 0, 2).reshape(6 * slots, ncf)

    field = ("vmem", (slots, nf, columns), f32)
    faces = [("vmem", (nface, columns), f32)] * 4
    coarse = ("vmem", (slots, nc, columns), f32)
    coarse_sends = [("vmem", (nc, columns), f32)] * 4
    trace_room = ((6 * slots, nface, columns), f32)
    field_room = (field[1], f32)
    block_flops = 3 * 2 * slots * nf * nf * columns
    lift_flops = 3 * 2 * slots * nf * 6 * nface * columns
    where = [("late", ids), ("late", neighbours)]

    def vm(*arrays):
        return [("vmem", a) for a in arrays]

    def parts(*arrays):
        return [("parts", a) for a in arrays]

    wide = 2 * (nf + -nf % LANES)
    matrix = ("vmem", (slots, nf, wide), bf16)
    mask_tiles = ("vmem", (8 * slots, 8, columns), f32)
    (masks,) = call(mask_kernel, [mask_tiles], [], where, 8 * block_flops)
    coarse_wide, coarse_coef, coarse_faces = call(
        coarse_lay_out_kernel,
        [("vmem", (nc, 6 * nc), f32), ("vmem", (slots, 6 * nc, columns), f32), ("vmem", (6, nc, nc), f32)], [],
        vm(coarse_lifts_t, coarse_coefs_t, hot_lifts, hot_coefs, masks),
    )
    state, rhs_live, inverses, *sends = call(
        first_kernel, [field, field, matrix] + faces, [],
        [("smem", counts)] + vm(masks, right_side, fine_inverses, coarse_wide), 8 * block_flops,
    )
    got = swap(sends)
    res, lh, ll, far_lifts, coef, blocks = call(
        first_local_kernel,
        [field]
        + [("vmem", (nf, 6 * nface), bf16)] * 2
        + [("vmem", (4, nf, 2 * nface), bf16), ("vmem", (slots, 6 * nface, columns), f32), matrix],
        [trace_room],
        where + vm(state, lifts_t, coefs, fine_blocks, rhs_live),
        block_flops + lift_flops,
    )

    def local(state):
        return call(
            local_kernel, [field], [trace_room],
            where + vm(state, lh, ll, blocks, coef, rhs_live), block_flops + lift_flops,
        )[0]

    def sweep(got, res, state, last):
        return call(
            sweep_kernel, [("hbm",) + field[1:]] if last else [field] + faces, [],
            vm(masks, *got, res, state, far_lifts, inverses), block_flops,
        )

    for i in range(PRE_SWEEPS - 1):
        state, *sends = sweep(got, res, state, False)
        got = swap(sends)
        res = local(state)
    residual, coarse_rhs, w, *sends = call(
        restrict_kernel, [field, coarse, coarse] + coarse_sends, [],
        vm(masks, *got, res, far_lifts, *restrict, coarse_inverses),
    )
    (coarse_remote,) = call(
        coarse_remote_kernel, [("vmem", (slots * nc, 4 * nc), f32)], [],
        vm(masks, coarse_faces, coarse_coef, coarse_inverses),
    )
    far_prolong = None
    for _ in range(COARSE_SWEEPS - 1):
        got = swap(sends)
        (w_local,) = call(
            coarse_local_kernel, [coarse], [],
            where + vm(w, coarse_rhs, coarse_blocks, coarse_inverses, coarse_wide, coarse_coef),
        )
        w, *sends = call(
            coarse_sweep_kernel, [coarse] + coarse_sends, [], vm(masks, *got, w_local, coarse_remote)
        )
        if far_prolong is None:
            (far_prolong,) = call(
                far_prolong_kernel, [("vmem", (4, nf, 2 * LANES), bf16)], [], vm(masks, far_lifts, face_prolong, w)
            )
    got = swap(sends)
    res, state = call(
        prolong_kernel, [field, field], [trace_room, field_room],
        where + vm(residual, state, w, lh, ll, blocks, coef, prolong),
        block_flops + lift_flops,
    )
    state, *sends = call(
        post_kernel, [field] + faces, [],
        vm(masks, *got, res, state, far_prolong, inverses), block_flops,
    )
    for i in range(POST_SWEEPS - 1):
        got = swap(sends)
        res = local(state)
        state, *sends = sweep(got, res, state, i == POST_SWEEPS - 2)
    return state


def solution(mesh):
    placed = (
        P(AXES, None, None),
        P(AXES, None, None),
        P(AXES, None, None),
        P(),
        P(AXES, None, None),
        P(AXES, None, None),
        P(AXES, None, None),
        P(),
        P(AXES, None, None),
        P(AXES, None),
        P(AXES),
    )
    return jax.shard_map(
        body,
        mesh=mesh,
        in_specs=placed,
        out_specs=P(AXES, None, None),
        check_vma=False,
    )
```

```python
import functools

import jax
import jax.numpy as jnp
import numpy as np
from jax import lax
from jax.experimental import pallas as pl
from jax.experimental.pallas import tpu as pltpu
from jax.sharding import PartitionSpec as P

NVAR = 5
NODE1 = 4
PRE_SWEEPS = 2
POST_SWEEPS = 2
COARSE_SWEEPS = 4
AXES = ("wide", "narrow")
LANES = 128
VMEM_LIMIT = 16 * 1024 * 1024

damping = 0.8
highest = lax.Precision.HIGHEST
f32, bf16 = jnp.float32, jnp.bfloat16


def prolong_table(node_count, variables):
    points = np.array([-1.0, -1.0 / np.sqrt(5.0), 1.0 / np.sqrt(5.0), 1.0])
    linear = np.stack([(1.0 - points) / 2.0, (1.0 + points) / 2.0], axis=1)
    tensor_hat = (
        linear[:, None, None, :, None, None]
        * linear[None, :, None, None, :, None]
        * linear[None, None, :, None, None, :]
    )
    tensor_hat = tensor_hat.reshape(node_count * node_count * node_count, 8)
    return np.kron(np.eye(variables), tensor_hat).astype(np.float32)


def face_rows(node_count, variables):
    cube = node_count**3
    lattice = np.arange(cube).reshape(node_count, node_count, node_count)
    tables = []
    for face in range(6):
        layer = np.take(lattice, 0 if face % 2 == 0 else node_count - 1, axis=face // 2).reshape(-1)
        tables.append(np.concatenate([layer + v * cube for v in range(variables)]))
    return np.stack(tables)


class Late:
    def __init__(self, source, room, sem):
        self.room, self.copy, self.ready = room, pltpu.make_async_copy(source, room, sem), False
        self.copy.start()

    def wait(self):
        if not self.ready:
            self.ready = True
            self.copy.wait()

    def __getitem__(self, index):
        self.wait()
        return self.room[index]


def call(kernel, outs, scratch, args, flops=0):
    specs, rooms, counts = [], [], []
    for kind, a in args:
        if kind in ("smem", "vmem"):
            specs.append(pl.BlockSpec(memory_space=pltpu.SMEM if kind == "smem" else pltpu.VMEM))
        else:
            specs.append(pl.BlockSpec(memory_space=pl.ANY))
            rooms.append(pltpu.SMEM(a.shape, a.dtype))
            counts.append(1)
    out_rooms = [pltpu.VMEM(shape, dtype) for kind, shape, dtype in outs if kind == "hbm"]
    out_parts = sum(shape[0] for kind, shape, _ in outs if kind == "hbm")
    n_in, n_out, n_rooms = len(args), len(outs), len(rooms)

    def wrapped(*refs):
        ins, results, rest = refs[:n_in], refs[n_in : n_in + n_out], refs[n_in + n_out :]
        in_rooms, rest = rest[:n_rooms], rest[n_rooms:]
        result_rooms, rest = rest[: len(out_rooms)], rest[len(out_rooms) :]
        sems, rest = rest[0], rest[1:]
        given, base, at = [], 0, 0
        for (kind, _), ref in zip(args, ins):
            if kind in ("smem", "vmem"):
                given.append(ref)
                continue
            given.append(Late(ref, in_rooms[at], sems.at[base]))
            base += 1
            at += 1
        leaving, produced, at = [], [], 0
        for (kind, shape, _), ref in zip(outs, results):
            if kind == "vmem":
                produced.append(ref)
                continue
            room = result_rooms[at]
            produced.append((room, [pltpu.make_async_copy(room.at[i], ref.at[i], sems.at[base + i]) for i in range(shape[0])]))
            leaving += produced[-1][1]
            base += shape[0]
            at += 1
        kernel(*given, *produced, *rest)
        for item in given:
            if isinstance(item, Late):
                item.wait()
        for copy in leaving:
            copy.wait()

    moved = sum(int(np.prod(a.shape)) * a.dtype.itemsize for _, a in args)
    moved += sum(int(np.prod(shape)) * 4 for _, shape, _ in outs)
    return pl.pallas_call(
        wrapped,
        out_shape=[jax.ShapeDtypeStruct(shape, dtype) for _, shape, dtype in outs],
        in_specs=specs,
        out_specs=[pl.BlockSpec(memory_space=pltpu.VMEM if kind == "vmem" else pltpu.HBM) for kind, _, _ in outs],
        scratch_shapes=rooms
        + out_rooms
        + [pltpu.SemaphoreType.DMA((max(sum(counts) + out_parts, 1),))]
        + [pltpu.VMEM(shape, dtype) for shape, dtype in scratch],
        compiler_params=pltpu.CompilerParams(vmem_limit_bytes=VMEM_LIMIT),
        cost_estimate=pl.CostEstimate(flops=flops, bytes_accessed=moved, transcendentals=0),
    )(*[a for _, a in args])


def split(x):
    high = x.astype(bf16)
    return high, (x - high.astype(f32)).astype(bf16)


def pad_rows(x, rows):
    return x if x.shape[0] == rows else jnp.concatenate([x, jnp.zeros((rows - x.shape[0], x.shape[1]), x.dtype)], axis=0)


def stack(a):
    room = -a.shape[1] % LANES
    if room:
        a = jnp.concatenate([a, jnp.zeros((a.shape[0], room), a.dtype)], axis=1)
    return jnp.concatenate(split(a), axis=1)


def stacked_dot(a, x):
    xh, xl = split(x)
    rows = a.shape[1] // 2
    top = pad_rows(jnp.concatenate([xh, xl], axis=1), rows)
    low = pad_rows(jnp.concatenate([xh, jnp.zeros_like(xl)], axis=1), rows)
    both = jnp.dot(a, jnp.concatenate([top, low], axis=0), preferred_element_type=f32)
    return both[:, : x.shape[1]] + both[:, x.shape[1] :]


def dot(a, x):
    ah, al = a if isinstance(a, tuple) else split(a)
    xh, xl = split(x)
    n = x.shape[1]
    both = jnp.dot(ah, jnp.concatenate([xh, xl], axis=1), preferred_element_type=f32)
    return both[:, :n] + both[:, n:] + jnp.dot(al, xh, preferred_element_type=f32)


def small_dot(a, x):
    return jnp.dot(a, x, precision=highest, preferred_element_type=f32)


def face_of(state, e, face):
    if face == 0 or face == 1:
        start = 48 * face
        return jnp.concatenate([state[e, pl.ds(64 * v + start, 16)] for v in range(NVAR)], axis=0)
    if face >= 4:
        return state[e, pl.ds(3 * (face - 4), 80, stride=4)]
    half = 8 * (face - 2)
    first = jnp.concatenate([state[e, pl.ds(32 * m + half, 8)] for m in range(10)], axis=0)
    second = jnp.concatenate([state[e, pl.ds(32 * m + 16 + half, 8)] for m in range(10)], axis=0)
    low = lax.broadcasted_iota(jnp.int32, first.shape, 0) % 8 < 4
    if face == 2:
        return jnp.where(low, first, pltpu.roll(second, 4, 0))
    return jnp.where(low, pltpu.roll(first, 76, 0), second)


def link(ids, nbr, slots, e, face):
    g = nbr[e, face]
    owner = lax.div(g, slots)
    here = jnp.logical_and(g >= 0, owner == ids[2])
    away = jnp.logical_and(g >= 0, owner != ids[2])
    return here, away, jnp.maximum(lax.rem(g, slots), 0)


def crossing(ids, nbr, slots, face):
    found, slot = False, 0
    for e in range(slots):
        _, away, _ = link(ids, nbr, slots, e, face)
        found = jnp.logical_or(found, away)
        slot = jnp.where(away, e, slot)
    return found, slot


def swap_of(ids, face):
    return lax.rem(face % 2 + ids[face // 2] % 2 + 1, 2)


def fill_masks(ids, nbr, slots, masks):
    for i in range(4):
        for side in range(2):
            f = 2 * (i // 2) + side
            for e in range(slots):
                _, away, _ = link(ids, nbr, slots, e, f)
                value = jnp.where(jnp.logical_and(away, swap_of(ids, f) == i % 2), 1.0, 0.0)
                masks[(2 * i + side) * slots + e] = jnp.full(masks.shape[1:], value, f32)


def masked(mask, x):
    return (x.reshape(-1, *mask.shape) * mask).reshape(x.shape)


def meets(masks, slots, i, e):
    return masks[2 * i * slots + e] + masks[(2 * i + 1) * slots + e]


def crossing_traces(state):
    return [[face_of(state, e, f) for e in range(state.shape[0])] for f in range(4)]


def fill_traces(masks, traces, sends):
    slots = len(traces[0])
    for i in range(4):
        terms = [
            masked(masks[(2 * i + side) * slots + e], traces[2 * (i // 2) + side][e])
            for side in range(2)
            for e in range(slots)
        ]
        sends[i][...] = sum(terms[1:], terms[0])


def fill_elements(masks, w, sends):
    slots = w.shape[0]
    for i in range(4):
        terms = [masked(meets(masks, slots, i, e), w[e]) for e in range(slots)]
        sends[i][...] = sum(terms[1:], terms[0])


def live_kernel(counts, live):
    for e in range(live.shape[0]):
        live[e] = jnp.full(live.shape[1:], jnp.where(e < counts[0], 1.0, 0.0), f32)


def mask_kernel(ids, nbr, _, masks):
    fill_masks(ids, nbr, nbr.room.shape[0], masks)


def first_kernel(on, masks, rhs, given, v, live, inverses, *sends):
    for e in range(rhs.shape[0]):
        live[e] = masked(on[e], rhs[e])
        inverses[e] = stack(given[e])
        v[e] = damping * stacked_dot(inverses[e], live[e])
    fill_traces(masks, crossing_traces(v), sends)


def local_residual(ids, nbr, rhs, state, blocks, lifts, coef, out, traces):
    slots, _, columns = state.shape
    for e in range(slots):
        out[e] = rhs[e] - stacked_dot(blocks[e], state[e])
        for f in range(6):
            traces[f * slots + e] = face_of(state, e, f)
    near = []
    for e in range(slots):
        parts = []
        for f in range(6):
            here, _, s = link(ids, nbr, slots, e, f)
            t = traces[(f ^ 1) * slots + s] * coef[e, pl.ds(80 * f, 80)]
            parts.append(jnp.where(here, t, 0.0))
        near.append(jnp.concatenate(parts, axis=0))
    coupled = dot(lifts, jnp.concatenate(near, axis=1))
    for e in range(slots):
        out[e] = out[e] - coupled[:, e * columns : (e + 1) * columns]


def lay_out(lifts_t, coefs, lh, ll, coef):
    faces, nface, nf = lifts_t.shape
    slots = coef.shape[0]
    whole = jnp.concatenate([lifts_t[f] for f in range(faces)], axis=0).T
    lh[...], ll[...] = split(whole)
    turned = coefs[...].T
    for e in range(slots):
        for f in range(faces):
            column = turned[:, f * slots + e : f * slots + e + 1]
            coef[e, nface * f : nface * (f + 1)] = jnp.broadcast_to(column, (nface, coef.shape[2]))


def lay_out_far(ids, nbr, lifts_t, coef, far_lifts):
    nface, slots = lifts_t.shape[1], coef.shape[0]
    for i in range(4):
        low = 2 * (i // 2)
        first = swap_of(ids, low) == i % 2
        scaled = []
        for f in (low, low + 1):
            _, slot = crossing(ids, nbr, slots, f)
            scaled.append(lifts_t[f] * coef[slot, pl.ds(nface * f, nface)][:, :1])
        scaled = jnp.where(first, scaled[0], scaled[1])
        high = scaled.astype(bf16).astype(f32)
        far_lifts[i] = jnp.concatenate([high, scaled - high], axis=0).T.astype(bf16)


def first_local_kernel(
    ids, nbr, state, lifts_t, coefs, given, rhs, out, lh, ll, far_lifts, coef, blocks, traces
):
    lay_out(lifts_t, coefs, lh, ll, coef)
    for e in range(given.shape[0]):
        blocks[e] = stack(given[e])

    local_residual(
        ids, nbr, rhs, state, blocks, (lh[...], ll[...]), coef, out, traces
    )
    lay_out_far(ids, nbr, lifts_t, coef, far_lifts)


def local_kernel(ids, nbr, state, lh, ll, blocks, coef, rhs, out, traces):
    local_residual(ids, nbr, rhs, state, blocks, (lh[...], ll[...]), coef, out, traces)


def less_remote(masks, res, parts, e):
    slots = masks.shape[0] // 8
    for i, part in enumerate(parts):
        res = res - masked(meets(masks, slots, i, e), part)
    return res


def sweep_kernel(masks, y0, y1, y3, y2, res, state, far_lifts, inverses, v, *sends):
    parts = [stacked_dot(far_lifts[i], y[...]) for i, y in enumerate((y0, y1, y2, y3))]
    for e in range(res.shape[0]):
        value = state[e] + damping * stacked_dot(inverses[e], less_remote(masks, res[e], parts, e))
        if sends:
            v[e] = value
        else:
            v[0][e] = value
            v[1][e].start()
    if sends:
        fill_traces(masks, crossing_traces(v), sends)


def restrict_kernel(masks, y0, y1, y3, y2, res, far_lifts, restrict, inverses, _, r, rhs, w, *sends):
    parts = [stacked_dot(far_lifts[i], y[...]) for i, y in enumerate((y0, y1, y2, y3))]
    for e in range(r.shape[0]):
        left = less_remote(masks, res[e], parts, e)
        r[e] = left
        rhs[e] = 0.25 * dot(restrict[...], left)
        w[e] = damping * dot(inverses[e], rhs[e])
    fill_elements(masks, w, sends)


def prolong_kernel(ids, nbr, r, state, w, lh, ll, blocks, coef, prolong, out, corrected, traces, correction):
    slots = state.shape[0]
    columns = state.shape[2]
    raised = dot(prolong[...], jnp.concatenate([w[e] for e in range(slots)], axis=1))
    for e in range(slots):
        correction[e] = raised[:, e * columns : (e + 1) * columns]
        corrected[e] = state[e] + correction[e]
    local_residual(
        ids, nbr, r, correction, blocks, (lh[...], ll[...]), coef, out, traces
    )


def post_kernel(masks, y0, y1, y3, y2, res, state, far_prolong, inverses, v, *sends):
    parts = [stacked_dot(far_prolong[i], y[...]) for i, y in enumerate((y0, y1, y2, y3))]
    for e in range(res.shape[0]):
        v[e] = state[e] + damping * stacked_dot(inverses[e], less_remote(masks, res[e], parts, e))
    fill_traces(masks, crossing_traces(v), sends)


def coarse_lay_out_kernel(lifts_t, coefs, hot_lifts, hot_coefs, _, lifts, coef, wide):
    faces, _, nc = lifts_t.shape
    slots = coef.shape[0]
    spread = small_dot(hot_coefs[...], coefs[...].T)
    rows = small_dot(hot_lifts[...], jnp.concatenate([lifts_t[f] for f in range(faces)], axis=0))
    lifts[...] = rows.T
    for f in range(faces):
        wide[f] = rows[nc * f : nc * (f + 1)]
        for e in range(slots):
            column = spread[nc * f : nc * (f + 1), f * slots + e : f * slots + e + 1]
            coef[e, nc * f : nc * (f + 1)] = jnp.broadcast_to(column, (nc, coef.shape[2]))


def far_prolong_kernel(masks, far_lifts, face_prolong, _, far_prolong):
    slots = masks.shape[0] // 8
    for i in range(4):
        total = None
        for side in range(2):
            on = sum(masks[(2 * i + side) * slots + e] for e in range(slots))
            term = masked(on, face_prolong[2 * (i // 2) + 1 - side])
            total = term if total is None else total + term
        far_prolong[i] = jnp.concatenate(split(stacked_dot(far_lifts[i], total)), axis=1)


def coarse_remote_kernel(masks, wide, coef, inverses, remote):
    slots, nc, _ = inverses.shape
    for e in range(slots):
        scaled = []
        for i in range(4):
            total = None
            for side in range(2):
                f = 2 * (i // 2) + side
                term = masked(masks[(2 * i + side) * slots + e], coef[e, nc * f : nc * (f + 1)])
                term = wide[f] * term[:, :nc]
                total = term if total is None else total + term
            scaled.append(total)
        rows = damping * small_dot(inverses[e], jnp.concatenate(scaled, axis=0).T)
        remote[e * nc : (e + 1) * nc] = rows


def coarse_local_kernel(ids, nbr, w, rhs, blocks, inverses, lifts, coef, out):
    slots, nc, columns = w.shape
    for e in range(slots):
        out[e] = rhs[e] - dot(blocks[e], w[e])
    near = []
    for e in range(slots):
        parts = []
        for f in range(6):
            here, _, s = link(ids, nbr, slots, e, f)
            parts.append(jnp.where(here, w[s] * coef[e, nc * f : nc * (f + 1)], 0.0))
        near.append(jnp.concatenate(parts, axis=0))
    coupled = dot(lifts[...], jnp.concatenate(near, axis=1))
    for e in range(slots):
        res = out[e] - coupled[:, e * columns : (e + 1) * columns]
        out[e] = w[e] + damping * dot(inverses[e], res)


def coarse_sweep_kernel(masks, y0, y1, y3, y2, local, remote, w, *sends):
    slots, nc, _ = w.shape
    far = dot(remote[...], jnp.concatenate([y[...] for y in (y0, y1, y2, y3)], axis=0))
    for e in range(slots):
        w[e] = local[e] - far[e * nc : (e + 1) * nc]
    fill_elements(masks, w, sends)


def swap(parts):
    got = []
    for i in (0, 1, 3, 2):
        axis = AXES[i // 2]
        pairs = []
        for a in range(i % 2, lax.axis_size(axis) - 1, 2):
            pairs += [(a, a + 1), (a + 1, a)]
        got.append(lax.ppermute(parts[i], axis, pairs))
    return got


def body(
    right_side,
    fine_blocks,
    fine_inverses,
    fine_lifts,
    fine_coefs,
    coarse_blocks,
    coarse_inverses,
    coarse_lifts,
    coarse_coefs,
    neighbours,
    counts,
):
    slots, nf, columns = right_side.shape
    nface = fine_lifts.shape[2]
    nc = coarse_blocks.shape[1]
    ncf = coarse_lifts.shape[2]
    wide_here, narrow_here = lax.axis_index("wide"), lax.axis_index("narrow")
    ids = jnp.stack([wide_here, narrow_here, wide_here * lax.axis_size("narrow") + narrow_here]).astype(jnp.int32)

    prolong_np = prolong_table(NODE1, NVAR)
    coarse_table = face_rows(2, NVAR)
    fine_table = face_rows(NODE1, NVAR)
    prolong = jnp.asarray(prolong_np)
    restrict = jnp.asarray(np.ascontiguousarray(prolong_np.T))
    face_prolong = np.stack([prolong_np[fine_table[f]] for f in range(4)])
    face_prolong = jnp.asarray(np.pad(face_prolong, ((0, 0), (0, 0), (0, LANES - nc))))
    hot_lifts = np.zeros((6, nc, 6, ncf), np.float32)
    hot_coefs = np.zeros((6, nc, ncf), np.float32)
    for f in range(6):
        hot_lifts[f, coarse_table[f ^ 1], f, np.arange(ncf)] = 1.0
        hot_coefs[f, coarse_table[f ^ 1], np.arange(ncf)] = 1.0
    hot_lifts = jnp.asarray(hot_lifts.reshape(6 * nc, 6 * ncf))
    hot_coefs = jnp.asarray(hot_coefs.reshape(6 * nc, ncf))

    lifts_t = fine_lifts.transpose(0, 2, 1)
    coefs = fine_coefs.transpose(1, 0, 2).reshape(6 * slots, nface)
    coarse_lifts_t = coarse_lifts.transpose(0, 2, 1)
    coarse_coefs_t = coarse_coefs.transpose(1, 0, 2).reshape(6 * slots, ncf)

    field = ("vmem", (slots, nf, columns), f32)
    faces = [("vmem", (nface, columns), f32)] * 4
    coarse = ("vmem", (slots, nc, columns), f32)
    coarse_sends = [("vmem", (nc, columns), f32)] * 4
    trace_room = ((6 * slots, nface, columns), f32)
    field_room = (field[1], f32)
    block_flops = 3 * 2 * slots * nf * nf * columns
    lift_flops = 3 * 2 * slots * nf * 6 * nface * columns
    where = [("late", ids), ("late", neighbours)]

    def vm(*arrays):
        return [("vmem", a) for a in arrays]

    def parts(*arrays):
        return [("parts", a) for a in arrays]

    wide = 2 * (nf + -nf % LANES)
    matrix = ("vmem", (slots, nf, wide), bf16)
    mask_tiles = ("vmem", (8 * slots, 8, columns), f32)
    (on,) = call(live_kernel, [("vmem", (slots, 8, columns), f32)], [], [("smem", counts)], 64 * block_flops)
    (masks,) = call(mask_kernel, [mask_tiles], [], where + vm(on), 8 * block_flops)
    state, rhs_live, inverses, *sends = call(
        first_kernel, [field, field, matrix] + faces, [],
        vm(on, masks, right_side, fine_inverses), 8 * block_flops,
    )
    got = swap(sends)
    res, lh, ll, far_lifts, coef, blocks = call(
        first_local_kernel,
        [field]
        + [("vmem", (nf, 6 * nface), bf16)] * 2
        + [("vmem", (4, nf, 2 * nface), bf16), ("vmem", (slots, 6 * nface, columns), f32), matrix],
        [trace_room],
        where + vm(state, lifts_t, coefs, fine_blocks, rhs_live),
        block_flops + lift_flops,
    )

    def local(state):
        return call(
            local_kernel, [field], [trace_room],
            where + vm(state, lh, ll, blocks, coef, rhs_live), block_flops + lift_flops,
        )[0]

    def sweep(got, res, state, last):
        return call(
            sweep_kernel, [("hbm",) + field[1:]] if last else [field] + faces, [],
            vm(masks, *got, res, state, far_lifts, inverses), block_flops,
        )

    for i in range(PRE_SWEEPS - 1):
        state, *sends = sweep(got, res, state, False)
        got = swap(sends)
        res = local(state)
    coarse_wide, coarse_coef, coarse_faces = call(
        coarse_lay_out_kernel,
        [("vmem", (nc, 6 * nc), f32), ("vmem", (slots, 6 * nc, columns), f32), ("vmem", (6, nc, nc), f32)], [],
        vm(coarse_lifts_t, coarse_coefs_t, hot_lifts, hot_coefs, state),
    )
    residual, coarse_rhs, w, *sends = call(
        restrict_kernel, [field, coarse, coarse] + coarse_sends, [],
        vm(masks, *got, res, far_lifts, restrict, coarse_inverses, coarse_wide),
    )
    (coarse_remote,) = call(
        coarse_remote_kernel, [("vmem", (slots * nc, 4 * nc), f32)], [],
        vm(masks, coarse_faces, coarse_coef, coarse_inverses),
    )
    far_prolong = None
    for _ in range(COARSE_SWEEPS - 1):
        got = swap(sends)
        (w_local,) = call(
            coarse_local_kernel, [coarse], [],
            where + vm(w, coarse_rhs, coarse_blocks, coarse_inverses, coarse_wide, coarse_coef),
        )
        w, *sends = call(
            coarse_sweep_kernel, [coarse] + coarse_sends, [], vm(masks, *got, w_local, coarse_remote)
        )
        if far_prolong is None:
            (far_prolong,) = call(
                far_prolong_kernel, [("vmem", (4, nf, 2 * LANES), bf16)], [], vm(masks, far_lifts, face_prolong, w)
            )
    got = swap(sends)
    res, state = call(
        prolong_kernel, [field, field], [trace_room, field_room],
        where + vm(residual, state, w, lh, ll, blocks, coef, prolong),
        block_flops + lift_flops,
    )
    state, *sends = call(
        post_kernel, [field] + faces, [],
        vm(masks, *got, res, state, far_prolong, inverses), block_flops,
    )
    for i in range(POST_SWEEPS - 1):
        got = swap(sends)
        res = local(state)
        state, *sends = sweep(got, res, state, i == POST_SWEEPS - 2)
    return state


def solution(mesh):
    placed = (
        P(AXES, None, None),
        P(AXES, None, None),
        P(AXES, None, None),
        P(),
        P(AXES, None, None),
        P(AXES, None, None),
        P(AXES, None, None),
        P(),
        P(AXES, None, None),
        P(AXES, None),
        P(AXES),
    )
    return jax.shard_map(
        body,
        mesh=mesh,
        in_specs=placed,
        out_specs=P(AXES, None, None),
        check_vma=False,
    )
```
